32 devices in a mesh: src: 2 (over y), tgt: 16 (over z, x, core).
Axes of the slice: x: 2, y: 2, z: 4, core: 2. Of those that a mesh axis runs over, the one named last changes fastest.
Arguments:
- source_points: bfloat16 [4096, 128], P(('src', 'tgt')), may hold values from -1 to 1
- target_points: bfloat16 [16384, 128], P(('tgt', 'src')), may hold values from -1 to 1
- source_mass: float32 [4096], P('src'), may hold values from 0.1 to 10
- target_mass: float32 [16384], P('tgt'), may hold values from 0.1 to 10
Outputs:
- source_potential: float32 [4096], P('src')
- target_potential: float32 [16384], P('tgt')
The draws below stay inside these ranges and needn't reach their ends.
All inputs are finite; a program needn't handle non-finite values.
Results may differ from the reference program's by a relative error of at most 0.0003.
Values may be sent and summed in bfloat16 or wider, within the bound.
No kernel may reach another device: no remote copies, remote signals or barrier semaphores. Data moves between devices by JAX's collectives and lax.ppermute only.
A program may use at most 64 MiB of HBM per device.

```python
import math
import jax
import jax.numpy as jnp
from jax import lax

D = 128
ITERS = 3
NS = 4096
NT = 16384


def shared_targets(key):
    base = 0.25 * jax.random.normal(key, (NT, D), jnp.float32)
    return jnp.clip(base, -1.0, 1.0)


def draw_source_points(key, part):
    key = jax.random.fold_in(key, 11)
    values = jnp.clip(0.25 * jax.random.normal(key, (NS, D), jnp.float32), -1.0, 1.0)
    return values.astype(jnp.bfloat16)


def draw_target_points(key, part):
    targets = shared_targets(key)
    return targets.astype(jnp.bfloat16)


def level_of(key, dims, split, low, high):
    loudness, own = 1.0, jax.random.fold_in(key, 6)
    for axis_at, parts in split:
        steps = jnp.exp(jax.random.uniform(jax.random.fold_in(own, axis_at), (parts,), jnp.float32, low / len(split), high / len(split)))
        loudness = loudness * jnp.repeat(steps, dims[axis_at] // parts).reshape([-1 if axis == axis_at else 1 for axis in range(len(dims))])
    return loudness


def setup_inputs(seed: int = 0) -> dict:
    arg_keys = jax.random.split(jax.random.key(seed), 5)
    source_points = draw_source_points(jax.random.fold_in(arg_keys[4], 71), 0)
    target_points = draw_target_points(jax.random.fold_in(arg_keys[4], 71), 0)
    source_mass = jnp.clip(jnp.exp(math.log(10.0) - 4.6051702 * jax.random.uniform(arg_keys[2], (NS,), jnp.float32) ** level_of(arg_keys[2], (NS,), ((0, 2),), -0.2, 0.2)), 0.1, 10.0)
    target_mass = jnp.clip(jnp.exp(math.log(10.0) - 4.6051702 * jax.random.uniform(arg_keys[3], (NT,), jnp.float32) ** level_of(arg_keys[3], (NT,), ((0, 16),), -0.2, 0.2)), 0.1, 10.0)
    return {"source_points": source_points, "target_points": target_points, "source_mass": source_mass, "target_mass": target_mass}


EPS = 0.05


def half_norm(points):
    values = points.astype(jnp.float32)
    return 0.5 * jnp.sum(values * values, axis=1)


def update(rows, cols, col_pot, col_logm):
    count = rows.shape[0]
    block = math.gcd(512, count)
    col_half = half_norm(cols)
    shift = col_pot + EPS * col_logm
    blocks = rows.reshape(count // block, block, rows.shape[1])

    def one_block(chosen):
        cost = half_norm(chosen)[:, None] + col_half[None, :] - jnp.dot(chosen, cols.T, preferred_element_type=jnp.float32)
        scores = (shift[None, :] - cost) / EPS
        peak = jnp.max(scores, axis=1)
        total = jnp.sum(jnp.exp(scores - peak[:, None]), axis=1)
        return -EPS * (peak + jnp.log(total))

    return lax.map(one_block, blocks).reshape(count)


def reference(source_points, target_points, source_mass, target_mass):
    log_a = jnp.log(source_mass)
    log_b = jnp.log(target_mass)
    target_potential = jnp.zeros((target_points.shape[0],), jnp.float32)
    source_potential = jnp.zeros((source_points.shape[0],), jnp.float32)
    for step in range(ITERS):
        source_potential = update(source_points, target_points, target_potential, log_b)
        target_potential = update(target_points, source_points, source_potential, log_a)
    return source_potential, target_potential
```

```python
import math

import jax
import jax.numpy as jnp
from jax import lax
from jax.experimental import pallas as pl
from jax.experimental.pallas import tpu as pltpu
from jax.sharding import Mesh, PartitionSpec as P

ITERS = 3
EPS = 0.05
SCALE = 1.0 / (EPS * math.log(2.0))
UNIT = EPS * math.log(2.0)
LANES = 128
CORES = 2
F32 = jnp.float32
VMEM = pl.BlockSpec(memory_space=pltpu.VMEM)
SMEM = pl.BlockSpec(memory_space=pltpu.SMEM)


def params(limit=24):
    return pltpu.CompilerParams(vmem_limit_bytes=limit * 1024 * 1024)


def pin(value):
    return pltpu.with_memory_space_constraint(value, pltpu.VMEM)


def rows_of(count):
    return jax.ShapeDtypeStruct((count // LANES, LANES), F32)


def diagonal():
    shape = (LANES, LANES)
    return lax.broadcasted_iota(jnp.int32, shape, 0) == lax.broadcasted_iota(jnp.int32, shape, 1)


def to_column(row, mask):
    return jnp.sum(jnp.where(mask, jnp.broadcast_to(row, mask.shape), 0.0), axis=1, keepdims=True)


def to_row(column, mask):
    return jnp.sum(jnp.where(mask, jnp.broadcast_to(column, mask.shape), 0.0), axis=0, keepdims=True)


def unfold(value):
    return jnp.concatenate([value[i : i + 1, :] for i in range(value.shape[0])], axis=1)


def fold_into(ref, value):
    for row in range(ref.shape[0]):
        ref[row : row + 1, :] = value[:, row * LANES : (row + 1) * LANES]


def tree(values, join):
    while len(values) > 1:
        values = [join(values[i], values[i + 1]) for i in range(0, len(values), 2)]
    return values[0]


def log_sum(values):
    peak = tree(values, jnp.maximum)
    return peak + jnp.log2(tree([jnp.exp2(value - peak) for value in values], jnp.add))


def product(rows, cols):
    return lax.dot_general(rows, cols, (((1,), (1,)), ((), ())), preferred_element_type=F32)


def first_rows(place, masses, sources, blocks):
    count, part = sources.shape[0], blocks[0].shape[0]
    n_blocks, n_masses = len(blocks), len(masses)
    width, chunk = n_blocks * part, masses[0].shape[0]

    def kernel(place_ref, *refs):
        mass_refs, (sources_ref, *block_refs) = refs[:n_masses], refs[n_masses : n_masses + 1 + n_blocks]
        targets_ref, mass_ref, out_ref, half_ref, scores_ref = refs[n_masses + 1 + n_blocks :]
        for step in range(n_masses):
            start = pl.multiple_of(jnp.bitwise_xor(place_ref[1], step) * chunk, chunk)
            mass_ref[pl.ds(start, chunk), :] = mass_refs[step][...]
        for step in range(n_blocks):
            src = jnp.bitwise_xor(place_ref[0], step // CORES)
            core = jnp.bitwise_xor(place_ref[1], step % CORES)
            start = pl.multiple_of((core * (n_blocks // CORES) + src) * part, part)
            targets_ref[pl.ds(start, part), :] = block_refs[step][...]
        mask = diagonal()
        peak = jnp.full((8, count), -jnp.inf, F32)
        total = jnp.zeros((8, count), F32)
        for block in range(width // LANES):
            rows = targets_ref[block * LANES : (block + 1) * LANES, :]
            scores_ref[...] = product(rows, sources_ref[...])
            values = rows.astype(F32)
            half = 0.5 * jnp.sum(values * values, axis=1, keepdims=True)
            half_ref[block : block + 1, :] = to_row(half, mask)
            offset = to_column(jnp.log2(mass_ref[block : block + 1, :]), mask) - SCALE * half
            tops = peak
            for row in range(0, LANES, 8):
                scores = scores_ref[row : row + 8, :] * SCALE + offset[row : row + 8, :]
                scores_ref[row : row + 8, :] = scores
                tops = jnp.maximum(tops, scores)
            total = total * jnp.exp2(peak - tops)
            peak = tops
            for row in range(0, LANES, 8):
                total = total + jnp.exp2(scores_ref[row : row + 8, :] - peak)
        widest = jnp.max(peak, axis=0, keepdims=True)
        fold_into(out_ref, widest + jnp.log2(jnp.sum(total * jnp.exp2(peak - widest), axis=0, keepdims=True)))

    return pl.pallas_call(
        kernel,
        out_shape=(pltpu.VMEM((width, LANES), jnp.bfloat16), rows_of(width), rows_of(count), rows_of(width)),
        in_specs=[SMEM] + [VMEM] * (n_masses + 1 + n_blocks),
        out_specs=(VMEM,) * 4,
        scratch_shapes=[pltpu.VMEM((LANES, count), F32)],
        compiler_params=params(),
        name="first_rows",
    )(place, *masses, sources, *blocks)


def first_columns(sources, targets, parts, mass):
    count, width = sources.shape[0], targets.shape[0]

    def kernel(sources_ref, targets_ref, parts_ref, mass_ref, plan_ref, peak_ref, out_ref, lse_ref):
        lse = log_sum([parts_ref[i] for i in range(parts.shape[0])])
        lse_ref[...] = lse
        shift = unfold(jnp.log2(mass_ref[...]) - lse)
        mask = diagonal()
        for block in range(width // LANES):
            at = block * LANES
            plan_ref[at : at + LANES, :] = product(targets_ref[at : at + LANES, :], sources_ref[...])
            peaks, totals = [], []
            for row in range(at, at + LANES, 8):
                scores = plan_ref[row : row + 8, :] * SCALE + shift
                peak = jnp.max(scores, axis=1, keepdims=True)
                plan = jnp.exp2(scores - peak)
                plan_ref[row : row + 8, :] = plan
                peaks.append(peak)
                totals.append(jnp.sum(plan, axis=1, keepdims=True))
            peak = jnp.concatenate(peaks, axis=0)
            total = jnp.concatenate(totals, axis=0)
            peak_ref[block : block + 1, :] = to_row(peak, mask)
            out_ref[block : block + 1, :] = to_row(peak + jnp.log2(total), mask)

    return pl.pallas_call(
        kernel,
        out_shape=(pltpu.VMEM((width, count), F32), rows_of(width), rows_of(width), rows_of(count)),
        in_specs=[VMEM] * 4,
        out_specs=(VMEM,) * 4,
        compiler_params=params(),
        name="first_columns",
    )(pin(sources), pin(targets), parts, mass)


def weighted_rows(weight, plan_ref, out_ref):
    mask = diagonal()
    total = jnp.zeros((8, plan_ref.shape[1]), F32)
    for block in range(plan_ref.shape[0] // LANES):
        column = to_column(weight[block : block + 1, :], mask)
        for row in range(0, LANES, 8):
            at = block * LANES + row
            total = total + plan_ref[at : at + 8, :] * column[row : row + 8, :]
    fold_into(out_ref, jnp.sum(total, axis=0, keepdims=True))


def second_rows(plan, peak, mass, parts):
    width, count = plan.shape

    def kernel(plan_ref, peak_ref, mass_ref, *refs):
        part_refs, (lse_ref, reach_ref, out_ref) = refs[:-3], refs[-3:]
        lse = log_sum([ref[...] for ref in part_refs])
        lse_ref[...] = lse
        reach = jnp.exp2(peak_ref[...] - lse)
        reach_ref[...] = reach
        weighted_rows(reach * mass_ref[...], plan_ref, out_ref)

    return pl.pallas_call(
        kernel,
        out_shape=(rows_of(width), rows_of(width), rows_of(count)),
        in_specs=[VMEM] * (3 + len(parts)),
        out_specs=(VMEM,) * 3,
        compiler_params=params(),
        name="second_rows",
    )(pin(plan), peak, mass, *parts)


def later_rows(plan, reach, mass, parts):
    width, count = plan.shape

    def kernel(plan_ref, reach_ref, mass_ref, *refs):
        part_refs, out_ref = refs[:-1], refs[-1]
        weighted_rows(reach_ref[...] * mass_ref[...] / tree([ref[...] for ref in part_refs], jnp.add), plan_ref, out_ref)

    return pl.pallas_call(
        kernel,
        out_shape=rows_of(count),
        in_specs=[VMEM] * (3 + len(parts)),
        out_specs=VMEM,
        compiler_params=params(),
        name="later_rows",
    )(pin(plan), reach, mass, *parts)


def later_columns(plan, reach, parts, mass, lse, half):
    width, count = plan.shape

    def kernel(plan_ref, reach_ref, parts_ref, mass_ref, lse_ref, half_ref, out_ref, potential_ref):
        mask = diagonal()
        factor = mass_ref[...] / tree([parts_ref[i] for i in range(parts.shape[0])], jnp.add)
        potential_ref[...] = half_ref[...] + UNIT * (jnp.log2(factor) - lse_ref[...])
        factor = unfold(factor)
        for block in range(width // LANES):
            totals = []
            for row in range(0, LANES, 8):
                at = block * LANES + row
                totals.append(jnp.sum(plan_ref[at : at + 8, :] * factor, axis=1, keepdims=True))
            total = to_row(jnp.concatenate(totals, axis=0), mask)
            out_ref[block : block + 1, :] = total * reach_ref[block : block + 1, :]

    return pl.pallas_call(
        kernel,
        out_shape=(rows_of(width), rows_of(count)),
        in_specs=[VMEM] * 6,
        out_specs=(VMEM,) * 2,
        compiler_params=params(),
        name="later_columns",
    )(pin(plan), reach, parts, mass, lse, half)


def levels_of(size):
    bits = size.bit_length() - 1
    out = []
    while bits > 0:
        take = 2 if bits % 2 == 0 else 1
        bits -= take
        out.append([step << bits for step in range(1, 1 << take)])
    return out


def swap(value, axes, size, distance):
    return lax.ppermute(value, axes, [(i, i ^ distance) for i in range(size)])


def swap_all(value, axes, size):
    values = [value]
    for distances in levels_of(size):
        got = {d: [swap(value, axes, size, d) for value in values] for d in reversed(distances)}
        values = [part for i in range(len(values)) for part in [values[i]] + [got[d][i] for d in distances]]
    return values


def share(value, size):
    copies = jnp.broadcast_to(value[None], (size,) + value.shape)
    return lax.all_to_all(copies, "far", 0, 0, tiled=True)


def half_norm(points):
    values = points.astype(F32)
    return 0.5 * jnp.sum(values * values, axis=1)


def make_local(n_src, n_far):
    near, n_near = ("src", "core"), n_src * CORES

    def local(source_points, target_points, source_mass, target_mass):
        core = lax.axis_index("core")
        place = jnp.stack([lax.axis_index("src"), core]).astype(jnp.int32)
        part = source_points.shape[0]
        a = source_mass.reshape(n_far, CORES, part)
        a = lax.dynamic_index_in_dim(a, core, axis=1, keepdims=False).reshape(-1, LANES)
        b = target_mass.reshape(-1, LANES)
        blocks = swap_all(target_points, near, n_near)
        masses = swap_all(b, "core", CORES)
        sources = share(source_points, n_far).reshape(-1, LANES)
        targets, b, own, half_y = first_rows(place, masses, sources, blocks)
        plan, peak, own, row_lse = first_columns(sources, targets, share(own, n_far), a)
        early, own = lax.optimization_barrier((sources, own))
        half_x = half_norm(early).reshape(-1, LANES)
        parts = swap_all(own, near, n_near)
        half_x, *parts = lax.optimization_barrier((half_x, *parts))
        col_lse, reach, rows = second_rows(plan, peak, b, parts)
        for step in range(1, ITERS):
            if step > 1:
                rows = later_rows(plan, reach, b, parts)
            own, potential = later_columns(plan, reach, share(rows, n_far), a, row_lse, half_x)
            parts = swap_all(own, near, n_near)
        mine, other = swap_all(potential.reshape(n_far, part), "core", CORES)
        low, high = jnp.where(core == 0, mine, other), jnp.where(core == 0, other, mine)
        source_potential = jnp.stack([low, high], axis=1).reshape(-1)
        target_potential = half_y - UNIT * (col_lse + jnp.log2(tree(parts, jnp.add)))
        target_potential = target_potential.reshape(CORES, -1)
        target_potential = lax.dynamic_index_in_dim(target_potential, core, axis=0, keepdims=False)
        return source_potential, target_potential

    return local


def solution(mesh):
    n_src, n_tgt = mesh.shape["src"], mesh.shape["tgt"]
    n_far = n_tgt // CORES
    split = Mesh(mesh.devices.reshape(n_src, n_far, CORES), ("src", "far", "core"))
    placed = (P(("src", "far", "core"), None), P(("far", "core", "src"), None), P("src"), P(("far", "core")))
    return jax.shard_map(
        make_local(n_src, n_far),
        mesh=split,
        in_specs=placed,
        out_specs=(P("src"), P(("far", "core"))),
        check_vma=False,
    )
```

```python
import math

import jax
import jax.numpy as jnp
from jax import lax
from jax.experimental import pallas as pl
from jax.experimental.pallas import tpu as pltpu
from jax.sharding import Mesh, PartitionSpec as P

ITERS = 3
EPS = 0.05
SCALE = 1.0 / (EPS * math.log(2.0))
UNIT = EPS * math.log(2.0)
LANES = 128
CORES = 2
F32 = jnp.float32
VMEM = pl.BlockSpec(memory_space=pltpu.VMEM)
SMEM = pl.BlockSpec(memory_space=pltpu.SMEM)


def params(limit=24):
    return pltpu.CompilerParams(vmem_limit_bytes=limit * 1024 * 1024)


def pin(value):
    return pltpu.with_memory_space_constraint(value, pltpu.VMEM)


def rows_of(count):
    return jax.ShapeDtypeStruct((count // LANES, LANES), F32)


def diagonal():
    shape = (LANES, LANES)
    return lax.broadcasted_iota(jnp.int32, shape, 0) == lax.broadcasted_iota(jnp.int32, shape, 1)


def to_column(row, mask):
    return jnp.sum(jnp.where(mask, jnp.broadcast_to(row, mask.shape), 0.0), axis=1, keepdims=True)


def to_row(column, mask):
    return jnp.sum(jnp.where(mask, jnp.broadcast_to(column, mask.shape), 0.0), axis=0, keepdims=True)


def unfold(value):
    return jnp.concatenate([value[i : i + 1, :] for i in range(value.shape[0])], axis=1)


def fold_into(ref, value):
    for row in range(ref.shape[0]):
        ref[row : row + 1, :] = value[:, row * LANES : (row + 1) * LANES]


def tree(values, join):
    while len(values) > 1:
        values = [join(values[i], values[i + 1]) for i in range(0, len(values), 2)]
    return values[0]


def log_sum(values):
    peak = tree(values, jnp.maximum)
    return peak + jnp.log2(tree([jnp.exp2(value - peak) for value in values], jnp.add))


def product(rows, cols):
    return lax.dot_general(rows, cols, (((1,), (1,)), ((), ())), preferred_element_type=F32)


def first_rows(place, masses, sources, blocks):
    n_masses, n_sources, n_blocks = len(masses), len(sources), len(blocks)
    group, part, chunk = sources[0].shape[0], blocks[0].shape[0], masses[0].shape[0]
    count, width = n_sources * group, n_blocks * part
    n_in = n_masses + n_sources + n_blocks

    def kernel(place_ref, *refs):
        mass_refs, source_refs = refs[:n_masses], refs[n_masses : n_masses + n_sources]
        block_refs = refs[n_masses + n_sources : n_in]
        sources_ref, targets_ref, mass_ref, out_ref, half_ref, scores_ref = refs[n_in:]
        for step in range(n_sources):
            start = pl.multiple_of(jnp.bitwise_xor(place_ref[2], step) * group, group)
            sources_ref[pl.ds(start, group), :] = source_refs[step][...]
        for step in range(n_masses):
            start = pl.multiple_of(jnp.bitwise_xor(place_ref[1], step) * chunk, chunk)
            mass_ref[pl.ds(start, chunk), :] = mass_refs[step][...]
        for step in range(n_blocks):
            src = jnp.bitwise_xor(place_ref[0], step // CORES)
            low = jnp.bitwise_xor(place_ref[1], step % 2)
            start = pl.multiple_of((low * (n_blocks // 2) + src) * part, part)
            targets_ref[pl.ds(start, part), :] = block_refs[step][...]
        mask = diagonal()
        peak = jnp.full((8, count), -jnp.inf, F32)
        total = jnp.zeros((8, count), F32)
        for block in range(width // LANES):
            rows = targets_ref[block * LANES : (block + 1) * LANES, :]
            scores_ref[...] = product(rows, sources_ref[...])
            values = rows.astype(F32)
            half = 0.5 * jnp.sum(values * values, axis=1, keepdims=True)
            half_ref[block : block + 1, :] = to_row(half, mask)
            offset = to_column(jnp.log2(mass_ref[block : block + 1, :]), mask) - SCALE * half
            tops = peak
            for row in range(0, LANES, 8):
                scores = scores_ref[row : row + 8, :] * SCALE + offset[row : row + 8, :]
                scores_ref[row : row + 8, :] = scores
                tops = jnp.maximum(tops, scores)
            total = total * jnp.exp2(peak - tops)
            peak = tops
            for row in range(0, LANES, 8):
                total = total + jnp.exp2(scores_ref[row : row + 8, :] - peak)
        widest = jnp.max(peak, axis=0, keepdims=True)
        fold_into(out_ref, widest + jnp.log2(jnp.sum(total * jnp.exp2(peak - widest), axis=0, keepdims=True)))

    return pl.pallas_call(
        kernel,
        out_shape=(
            pltpu.VMEM((count, LANES), jnp.bfloat16),
            pltpu.VMEM((width, LANES), jnp.bfloat16),
            rows_of(width),
            rows_of(count),
            rows_of(width),
        ),
        in_specs=[SMEM] + [VMEM] * n_in,
        out_specs=(VMEM,) * 5,
        scratch_shapes=[pltpu.VMEM((LANES, count), F32)],
        compiler_params=params(),
        name="first_rows",
    )(place, *masses, *sources, *blocks)


def first_columns(sources, targets, parts, mass):
    count, width = sources.shape[0], targets.shape[0]

    def kernel(sources_ref, targets_ref, mass_ref, *refs):
        part_refs, (plan_ref, peak_ref, out_ref, lse_ref) = refs[:-4], refs[-4:]
        lse = log_sum([ref[...] for ref in part_refs])
        lse_ref[...] = lse
        shift = unfold(jnp.log2(mass_ref[...]) - lse)
        mask = diagonal()
        for block in range(width // LANES):
            at = block * LANES
            plan_ref[at : at + LANES, :] = product(targets_ref[at : at + LANES, :], sources_ref[...])
            peaks, totals = [], []
            for row in range(at, at + LANES, 8):
                scores = plan_ref[row : row + 8, :] * SCALE + shift
                peak = jnp.max(scores, axis=1, keepdims=True)
                plan = jnp.exp2(scores - peak)
                plan_ref[row : row + 8, :] = plan
                peaks.append(peak)
                totals.append(jnp.sum(plan, axis=1, keepdims=True))
            peak = jnp.concatenate(peaks, axis=0)
            total = jnp.concatenate(totals, axis=0)
            peak_ref[block : block + 1, :] = to_row(peak, mask)
            out_ref[block : block + 1, :] = to_row(peak + jnp.log2(total), mask)

    return pl.pallas_call(
        kernel,
        out_shape=(pltpu.VMEM((width, count), F32), rows_of(width), rows_of(width), rows_of(count)),
        in_specs=[VMEM] * (3 + len(parts)),
        out_specs=(VMEM,) * 4,
        compiler_params=params(),
        name="first_columns",
    )(pin(sources), pin(targets), mass, *parts)


def weighted_rows(weight, plan_ref, out_ref):
    mask = diagonal()
    total = jnp.zeros((8, plan_ref.shape[1]), F32)
    for block in range(plan_ref.shape[0] // LANES):
        column = to_column(weight[block : block + 1, :], mask)
        for row in range(0, LANES, 8):
            at = block * LANES + row
            total = total + plan_ref[at : at + 8, :] * column[row : row + 8, :]
    fold_into(out_ref, jnp.sum(total, axis=0, keepdims=True))


def second_rows(plan, peak, mass, parts):
    width, count = plan.shape

    def kernel(plan_ref, peak_ref, mass_ref, *refs):
        part_refs, (lse_ref, reach_ref, out_ref) = refs[:-3], refs[-3:]
        lse = log_sum([ref[...] for ref in part_refs])
        lse_ref[...] = lse
        reach = jnp.exp2(peak_ref[...] - lse)
        reach_ref[...] = reach
        weighted_rows(reach * mass_ref[...], plan_ref, out_ref)

    return pl.pallas_call(
        kernel,
        out_shape=(rows_of(width), rows_of(width), rows_of(count)),
        in_specs=[VMEM] * (3 + len(parts)),
        out_specs=(VMEM,) * 3,
        compiler_params=params(),
        name="second_rows",
    )(pin(plan), peak, mass, *parts)


def later_rows(plan, reach, mass, parts):
    width, count = plan.shape
    rows = width // LANES

    def kernel(plan_ref, reach_ref, mass_ref, *refs):
        part_refs, out_ref = refs[:-1], refs[-1]
        total = tree([ref[:rows, :] for ref in part_refs], jnp.add)
        weighted_rows(reach_ref[...] * mass_ref[...] / total, plan_ref, out_ref)

    return pl.pallas_call(
        kernel,
        out_shape=rows_of(count),
        in_specs=[VMEM] * (3 + len(parts)),
        out_specs=VMEM,
        compiler_params=params(),
        name="later_rows",
    )(pin(plan), reach, mass, *parts)


def later_columns(plan, reach, parts, mass, lse, half):
    width, count = plan.shape

    def kernel(plan_ref, reach_ref, mass_ref, lse_ref, half_ref, *refs):
        part_refs, out_ref = refs[:-1], refs[-1]
        mask = diagonal()
        factor = mass_ref[...] / tree([ref[...] for ref in part_refs], jnp.add)
        out_ref[width // LANES :, :] = half_ref[...] + UNIT * (jnp.log2(factor) - lse_ref[...])
        factor = unfold(factor)
        for block in range(width // LANES):
            totals = []
            for row in range(0, LANES, 8):
                at = block * LANES + row
                totals.append(jnp.sum(plan_ref[at : at + 8, :] * factor, axis=1, keepdims=True))
            total = to_row(jnp.concatenate(totals, axis=0), mask)
            out_ref[block : block + 1, :] = total * reach_ref[block : block + 1, :]

    return pl.pallas_call(
        kernel,
        out_shape=rows_of(width + count),
        in_specs=[VMEM] * (5 + len(parts)),
        out_specs=VMEM,
        compiler_params=params(),
        name="later_columns",
    )(pin(plan), reach, mass, lse, half, *parts)


def levels_of(size):
    bits = size.bit_length() - 1
    out = []
    while bits > 0:
        take = 2 if bits % 2 == 0 else 1
        bits -= take
        out.append([step << bits for step in range(1, 1 << take)])
    return out


def swap(value, axes, size, distance):
    return lax.ppermute(value, axes, [(i, i ^ distance) for i in range(size)])


def swap_all(value, axes, size):
    values = [value]
    for distances in levels_of(size):
        got = {d: [swap(value, axes, size, d) for value in values] for d in reversed(distances)}
        values = [part for i in range(len(values)) for part in [values[i]] + [got[d][i] for d in distances]]
    return values


def half_norm(points):
    values = points.astype(F32)
    return 0.5 * jnp.sum(values * values, axis=1)


def make_local(n_src, n_high, n_x):
    near, n_near = ("src", "low"), n_src * 2
    far, n_far = ("high", "x"), n_high * n_x

    def swap_rows(rows, join):
        mine, other = swap_all(rows, "core", CORES)
        return swap_all(join(mine, other), far, n_far)

    def local(source_points, target_points, source_mass, target_mass):
        low, core = lax.axis_index("low"), lax.axis_index("core")
        index = lax.axis_index(far) * CORES + core
        place = jnp.stack([lax.axis_index("src"), low, index]).astype(jnp.int32)
        part = source_points.shape[0]
        a = source_mass.reshape(n_high, 2, -1)
        a = lax.dynamic_index_in_dim(a, low, axis=1, keepdims=False).reshape(-1, LANES)
        blocks = swap_all(target_points, near, n_near)
        sources = swap_all(source_points, far, n_far)
        masses = swap_all(target_mass.reshape(-1, LANES), "low", 2)
        sources = [block for pair in [swap_all(block, "core", CORES) for block in sources] for block in pair]
        sources, targets, b, own, half_y = first_rows(place, masses, sources, blocks)
        parts = swap_rows(own, lambda *pair: log_sum(list(pair)))
        plan, peak, own, row_lse = first_columns(sources, targets, parts, a)
        early, own = lax.optimization_barrier((sources, own))
        half_x = half_norm(early).reshape(-1, LANES)
        parts = swap_all(own, near, n_near)
        half_x, *parts = lax.optimization_barrier((half_x, *parts))
        col_lse, reach, rows = second_rows(plan, peak, b, parts)
        for step in range(1, ITERS):
            if step > 1:
                rows = later_rows(plan, reach, b, parts)
            own = later_columns(plan, reach, swap_rows(rows, jnp.add), a, row_lse, half_x)
            parts = swap_all(own, near, n_near)
        rows = col_lse.shape[0]
        mine, other = [value[rows:].reshape(n_high, -1) for value in parts[:2]]
        first, second = jnp.where(low == 0, mine, other), jnp.where(low == 0, other, mine)
        source_potential = jnp.stack([first, second], axis=1).reshape(-1)
        total = tree([value[:rows] for value in parts], jnp.add)
        target_potential = (half_y - UNIT * (col_lse + jnp.log2(total))).reshape(2, -1)
        target_potential = lax.dynamic_index_in_dim(target_potential, low, axis=0, keepdims=False)
        return source_potential, target_potential

    return local


def solution(mesh):
    n_src, n_tgt = mesh.shape["src"], mesh.shape["tgt"]
    n_high, n_x = 2, n_tgt // (4 * CORES)
    split = Mesh(mesh.devices.reshape(n_src, n_high, 2, n_x, CORES), ("src", "high", "low", "x", "core"))
    tgt = ("high", "low", "x", "core")
    placed = (P(("src", *tgt), None), P((*tgt, "src"), None), P("src"), P(tgt))
    return jax.shard_map(
        make_local(n_src, n_high, n_x),
        mesh=split,
        in_specs=placed,
        out_specs=(P("src"), P(tgt)),
        check_vma=False,
    )
```

```python
import math

import jax
import jax.numpy as jnp
from jax import lax
from jax.experimental import pallas as pl
from jax.experimental.pallas import tpu as pltpu
from jax.sharding import Mesh, PartitionSpec as P

ITERS = 3
EPS = 0.05
SCALE = 1.0 / (EPS * math.log(2.0))
UNIT = EPS * math.log(2.0)
LANES = 128
CORES = 2
PIECES = 3
ROWS = 256
F32 = jnp.float32
VMEM = pl.BlockSpec(memory_space=pltpu.VMEM)
SMEM = pl.BlockSpec(memory_space=pltpu.SMEM)


def params(limit=24):
    return pltpu.CompilerParams(vmem_limit_bytes=limit * 1024 * 1024)


def pin(value):
    return pltpu.with_memory_space_constraint(value, pltpu.VMEM)


def rows_of(count):
    return jax.ShapeDtypeStruct((count // LANES, LANES), F32)


def diagonal():
    shape = (LANES, LANES)
    return lax.broadcasted_iota(jnp.int32, shape, 0) == lax.broadcasted_iota(jnp.int32, shape, 1)


def to_column(row, mask):
    return jnp.sum(jnp.where(mask, jnp.broadcast_to(row, mask.shape), 0.0), axis=1, keepdims=True)


def to_row(column, mask):
    return jnp.sum(jnp.where(mask, jnp.broadcast_to(column, mask.shape), 0.0), axis=0, keepdims=True)


def unfold(value):
    return jnp.concatenate([value[i : i + 1, :] for i in range(value.shape[0])], axis=1)


def fold_into(ref, value):
    for row in range(ref.shape[0]):
        ref[row : row + 1, :] = value[:, row * LANES : (row + 1) * LANES]


def tree(values, join):
    while len(values) > 1:
        values = [join(values[i], values[i + 1]) for i in range(0, len(values), 2)]
    return values[0]


def log_sum(values):
    peak = tree(values, jnp.maximum)
    return peak + jnp.log2(tree([jnp.exp2(value - peak) for value in values], jnp.add))


def product(rows, cols):
    return lax.dot_general(rows, cols, (((1,), (1,)), ((), ())), preferred_element_type=F32)


def ready(targets, mass, source_mass):
    def kernel(targets_ref, mass_ref, source_ref, targets_out, mass_out, source_out):
        targets_out[...] = targets_ref[...]
        mass_out[...] = mass_ref[...]
        source_out[...] = jnp.log2(source_ref[...])

    return pl.pallas_call(
        kernel,
        out_shape=(
            pltpu.VMEM(targets.shape, targets.dtype),
            pltpu.VMEM(mass.shape, F32),
            pltpu.VMEM(source_mass.shape, F32),
        ),
        in_specs=[VMEM] * 3,
        out_specs=(VMEM,) * 3,
        compiler_params=params(),
        cost_estimate=pl.CostEstimate(flops=1 << 20, bytes_accessed=1 << 20, transcendentals=0),
        name="ready",
    )(targets, mass, source_mass)


def pieces_of(value):
    lane = lax.broadcasted_iota(jnp.int32, (value.shape[0], LANES), 1)
    tile = jnp.zeros((value.shape[0], LANES), F32)
    for step in range(PIECES):
        piece = value.astype(jnp.bfloat16).astype(F32)
        tile = jnp.where(lane == step, piece, tile)
        value = value - piece
    return tile.astype(jnp.bfloat16)


def ones_for(rows):
    lane = lax.broadcasted_iota(jnp.int32, (rows, LANES), 1)
    return jnp.where(lane < PIECES, 1.0, 0.0).astype(jnp.bfloat16)


def first_rows(place, masses, sources, blocks):
    count, part = sources.shape[0], blocks[0].shape[0]
    n_blocks, n_masses = len(blocks), len(masses)
    width, chunk = n_blocks * part, masses[0].shape[0]

    def kernel(place_ref, *refs):
        mass_refs, (sources_ref, *block_refs) = refs[:n_masses], refs[n_masses : n_masses + 1 + n_blocks]
        targets_ref, mass_ref, out_ref, *score_refs = refs[n_masses + 1 + n_blocks :]
        for step in range(n_masses):
            start = pl.multiple_of(jnp.bitwise_xor(place_ref[1], step) * chunk, chunk)
            mass_ref[pl.ds(start, chunk), :] = mass_refs[step][...]
        for step in range(n_blocks):
            src = jnp.bitwise_xor(place_ref[0], step // CORES)
            core = jnp.bitwise_xor(place_ref[1], step % CORES)
            start = pl.multiple_of((core * (n_blocks // CORES) + src) * part, part)
            targets_ref[pl.ds(start, part), :] = block_refs[step][...]
        mask = diagonal()
        log_mass = jnp.log2(mass_ref[...]) * (1.0 / SCALE)
        cols = jnp.concatenate([sources_ref[...], ones_for(count)], axis=1)
        peak = jnp.full((8, count), -1e30, F32)
        total = jnp.zeros((8, count), F32)
        for at in range(0, width, ROWS):
            scores_ref = score_refs[at // ROWS % len(score_refs)]
            offsets = []
            for row in range(at, at + ROWS, LANES):
                values = targets_ref[row : row + LANES, :].astype(F32)
                half = 0.5 * jnp.sum(values * values, axis=1, keepdims=True)
                block = row // LANES
                offsets.append(pieces_of(to_column(log_mass[block : block + 1, :], mask) - half))
            rows = jnp.concatenate([targets_ref[at : at + ROWS, :], jnp.concatenate(offsets, axis=0)], axis=1)
            scores_ref[...] = product(rows, cols)
            tops = peak
            for row in range(0, ROWS, 8):
                tops = jnp.maximum(tops, scores_ref[row : row + 8, :])
            total = total * jnp.exp2((peak - tops) * SCALE)
            peak = tops
            for row in range(0, ROWS, 8):
                total = total + jnp.exp2((scores_ref[row : row + 8, :] - peak) * SCALE)
        widest = jnp.max(peak, axis=0, keepdims=True)
        total = jnp.sum(total * jnp.exp2((peak - widest) * SCALE), axis=0, keepdims=True)
        fold_into(out_ref, widest * SCALE + jnp.log2(total))

    return pl.pallas_call(
        kernel,
        out_shape=(pltpu.VMEM((width, LANES), jnp.bfloat16), rows_of(width), rows_of(count)),
        in_specs=[SMEM] + [VMEM] * (n_masses + 1 + n_blocks),
        out_specs=(VMEM,) * 3,
        scratch_shapes=[pltpu.VMEM((ROWS, count), F32)] * 2,
        compiler_params=params(),
        name="first_rows",
    )(place, *masses, sources, *blocks)


def first_columns(sources, targets, parts, log_mass):
    count, width = sources.shape[0], targets.shape[0]

    def kernel(sources_ref, targets_ref, parts_ref, log_ref, plan_ref, peak_ref, out_ref, lse_ref, *score_refs):
        lse = log_sum([parts_ref[i] for i in range(parts.shape[0])])
        lse_ref[...] = lse
        mask = diagonal()
        shift = (log_ref[...] - lse) * (1.0 / SCALE)
        shift = [pieces_of(to_column(shift[i : i + 1, :], mask)) for i in range(count // LANES)]
        cols = jnp.concatenate([sources_ref[...], jnp.concatenate(shift, axis=0)], axis=1)
        ones = ones_for(ROWS)
        for at in range(0, width, ROWS):
            scores_ref = score_refs[at // ROWS % len(score_refs)]
            scores_ref[...] = product(jnp.concatenate([targets_ref[at : at + ROWS, :], ones], axis=1), cols)
            for block in range(0, ROWS, LANES):
                peaks, totals = [], []
                for row in range(block, block + LANES, 8):
                    scores = scores_ref[row : row + 8, :]
                    pieces = [scores[:, lane : lane + LANES] for lane in range(0, count, LANES)]
                    peak = tree(pieces, jnp.maximum)
                    pieces = [jnp.exp2((piece - peak) * SCALE) for piece in pieces]
                    plan_ref[at + row : at + row + 8, :] = jnp.concatenate(pieces, axis=1)
                    peaks.append(peak * SCALE)
                    totals.append(tree(pieces, jnp.add))
                peak = jnp.concatenate(peaks, axis=0)
                peak_ref[at + block : at + block + LANES, :] = peak
                peak, total = peak.T, jnp.concatenate(totals, axis=0).T
                top = jnp.max(peak, axis=0, keepdims=True)
                total = jnp.sum(total * jnp.exp2(peak - top), axis=0, keepdims=True)
                index = (at + block) // LANES
                out_ref[index : index + 1, :] = top + jnp.log2(total)

    return pl.pallas_call(
        kernel,
        out_shape=(pltpu.VMEM((width, count), F32), pltpu.VMEM((width, LANES), F32), rows_of(width), rows_of(count)),
        in_specs=[VMEM] * 4,
        out_specs=(VMEM,) * 4,
        scratch_shapes=[pltpu.VMEM((ROWS, count), F32)] * 2,
        compiler_params=params(),
        name="first_columns",
    )(pin(sources), pin(targets), parts, log_mass)


def weighted_rows(reach_of, weight, plan_ref, out_ref):
    count = plan_ref.shape[1]
    mask = diagonal()
    total = jnp.zeros((8, count), F32)
    for block in range(plan_ref.shape[0] // LANES):
        at = block * LANES
        reach = reach_of(at, block, mask) * to_column(weight[block : block + 1, :], mask)
        for row in range(0, LANES, 8):
            factor = jnp.concatenate([reach[row : row + 8, :]] * (count // LANES), axis=1)
            total = total + plan_ref[at + row : at + row + 8, :] * factor
    fold_into(out_ref, jnp.sum(total, axis=0, keepdims=True))


def second_rows(plan, peak, mass, parts):
    width, count = plan.shape

    def kernel(plan_ref, peak_ref, mass_ref, *refs):
        part_refs, (lse_ref, reach_ref, out_ref) = refs[:-3], refs[-3:]
        lse = log_sum([ref[...] for ref in part_refs])
        lse_ref[...] = lse

        def reach_of(at, block, mask):
            reach = jnp.exp2(peak_ref[at : at + LANES, :] - to_column(lse[block : block + 1, :], mask))
            reach_ref[at : at + LANES, :] = reach
            return reach

        weighted_rows(reach_of, mass_ref[...], plan_ref, out_ref)

    return pl.pallas_call(
        kernel,
        out_shape=(rows_of(width), pltpu.VMEM((width, LANES), F32), rows_of(count)),
        in_specs=[VMEM] * (3 + len(parts)),
        out_specs=(VMEM,) * 3,
        compiler_params=params(),
        name="second_rows",
    )(pin(plan), pin(peak), mass, *parts)


def later_rows(plan, reach, mass, parts):
    width, count = plan.shape

    def kernel(plan_ref, reach_ref, mass_ref, *refs):
        part_refs, out_ref = refs[:-1], refs[-1]
        weight = mass_ref[...] / tree([ref[...] for ref in part_refs], jnp.add)
        weighted_rows(lambda at, block, mask: reach_ref[at : at + LANES, :], weight, plan_ref, out_ref)

    return pl.pallas_call(
        kernel,
        out_shape=rows_of(count),
        in_specs=[VMEM] * (3 + len(parts)),
        out_specs=VMEM,
        compiler_params=params(),
        name="later_rows",
    )(pin(plan), pin(reach), mass, *parts)


def later_columns(plan, reach, parts, log_mass, lse, half):
    width, count = plan.shape

    def kernel(plan_ref, reach_ref, parts_ref, log_ref, lse_ref, half_ref, out_ref, potential_ref):
        factor = log_ref[...] - jnp.log2(tree([parts_ref[i] for i in range(parts.shape[0])], jnp.add))
        potential_ref[...] = half_ref[...] + UNIT * (factor - lse_ref[...])
        factor = unfold(jnp.exp2(factor))
        factors = [factor[:, lane : lane + LANES] for lane in range(0, count, LANES)]
        for at in range(0, width, LANES):
            totals = []
            for row in range(at, at + LANES, 8):
                plan = plan_ref[row : row + 8, :]
                totals.append(tree([plan[:, i * LANES : (i + 1) * LANES] * factors[i] for i in range(count // LANES)], jnp.add))
            total = jnp.concatenate(totals, axis=0) * reach_ref[at : at + LANES, :]
            out_ref[at // LANES : at // LANES + 1, :] = jnp.sum(total.T, axis=0, keepdims=True)

    return pl.pallas_call(
        kernel,
        out_shape=(rows_of(width), rows_of(count)),
        in_specs=[VMEM] * 6,
        out_specs=(VMEM,) * 2,
        compiler_params=params(),
        name="later_columns",
    )(pin(plan), pin(reach), parts, log_mass, lse, half)


def levels_of(size):
    bits = size.bit_length() - 1
    out = []
    while bits > 0:
        take = 2 if bits % 2 == 0 else 1
        bits -= take
        out.append([step << bits for step in range(1, 1 << take)])
    return out


def swap(value, axes, size, distance):
    return lax.ppermute(value, axes, [(i, i ^ distance) for i in range(size)])


def swap_all(value, axes, size):
    values = [value]
    for distances in levels_of(size):
        got = {d: [swap(value, axes, size, d) for value in values] for d in reversed(distances)}
        values = [part for i in range(len(values)) for part in [values[i]] + [got[d][i] for d in distances]]
    return values


def share(value, size):
    copies = jnp.broadcast_to(value[None], (size,) + value.shape)
    return lax.all_to_all(copies, "far", 0, 0, tiled=True)


def half_norm(points):
    values = points.astype(F32)
    return 0.5 * jnp.sum(values * values, axis=1)


def make_local(n_src, n_far):
    near, n_near = ("src", "core"), n_src * CORES

    def local(source_points, target_points, source_mass, target_mass):
        core = lax.axis_index("core")
        place = jnp.stack([lax.axis_index("src"), core]).astype(jnp.int32)
        part = source_points.shape[0]
        a = source_mass.reshape(n_far, CORES, part)
        a = lax.dynamic_index_in_dim(a, core, axis=1, keepdims=False).reshape(-1, LANES)
        b = target_mass.reshape(-1, LANES)
        blocks = swap_all(target_points, near, n_near)
        masses = swap_all(b, "core", CORES)
        sources = lax.all_gather(source_points, "far", axis=0, tiled=True)
        blocks[0], masses[0], a = ready(target_points, b, a)
        place, a = lax.optimization_barrier((place, a))
        targets, b, own = first_rows(place, masses, sources, blocks)
        plan, peak, own, row_lse = first_columns(sources, targets, share(own, n_far), a)
        early_x, early_y, own = lax.optimization_barrier((sources, targets, own))
        half_x, half_y = half_norm(early_x).reshape(-1, LANES), half_norm(early_y).reshape(-1, LANES)
        parts = swap_all(own, near, n_near)
        half_x, half_y, *parts = lax.optimization_barrier((half_x, half_y, *parts))
        col_lse, reach, rows = second_rows(plan, peak, b, parts)
        for step in range(1, ITERS):
            if step > 1:
                rows = later_rows(plan, reach, b, parts)
            own, potential = later_columns(plan, reach, share(rows, n_far), a, row_lse, half_x)
            parts = swap_all(own, near, n_near)
        mine, other = swap_all(potential.reshape(n_far, part), "core", CORES)
        low, high = jnp.where(core == 0, mine, other), jnp.where(core == 0, other, mine)
        source_potential = jnp.stack([low, high], axis=1).reshape(-1)
        target_potential = half_y - UNIT * (col_lse + jnp.log2(tree(parts, jnp.add)))
        target_potential = target_potential.reshape(CORES, -1)
        target_potential = lax.dynamic_index_in_dim(target_potential, core, axis=0, keepdims=False)
        return source_potential, target_potential

    return local


def solution(mesh):
    n_src, n_tgt = mesh.shape["src"], mesh.shape["tgt"]
    n_far = n_tgt // CORES
    split = Mesh(mesh.devices.reshape(n_src, n_far, CORES), ("src", "far", "core"))
    placed = (P(("src", "far", "core"), None), P(("far", "core", "src"), None), P("src"), P(("far", "core")))
    return jax.shard_map(
        make_local(n_src, n_far),
        mesh=split,
        in_specs=placed,
        out_specs=(P("src"), P(("far", "core"))),
        check_vma=False,
    )
```

```python
import math

import jax
import jax.numpy as jnp
from jax import lax
from jax.experimental import pallas as pl
from jax.experimental.pallas import tpu as pltpu
from jax.sharding import Mesh, PartitionSpec as P

ITERS = 3
EPS = 0.05
SCALE = 1.0 / (EPS * math.log(2.0))
UNIT = EPS * math.log(2.0)
LANES = 128
CORES = 2
PIECES = 3
ROWS = 256
F32 = jnp.float32
VMEM = pl.BlockSpec(memory_space=pltpu.VMEM)
SMEM = pl.BlockSpec(memory_space=pltpu.SMEM)


def params(limit=24):
    return pltpu.CompilerParams(vmem_limit_bytes=limit * 1024 * 1024)


def pin(value):
    return pltpu.with_memory_space_constraint(value, pltpu.VMEM)


def rows_of(count):
    return jax.ShapeDtypeStruct((count // LANES, LANES), F32)


def diagonal():
    shape = (LANES, LANES)
    return lax.broadcasted_iota(jnp.int32, shape, 0) == lax.broadcasted_iota(jnp.int32, shape, 1)


def to_column(row, mask):
    return jnp.sum(jnp.where(mask, jnp.broadcast_to(row, mask.shape), 0.0), axis=1, keepdims=True)


def to_row(column, mask):
    return jnp.sum(jnp.where(mask, jnp.broadcast_to(column, mask.shape), 0.0), axis=0, keepdims=True)


def unfold(value):
    return jnp.concatenate([value[i : i + 1, :] for i in range(value.shape[0])], axis=1)


def fold_into(ref, value):
    for row in range(ref.shape[0]):
        ref[row : row + 1, :] = value[:, row * LANES : (row + 1) * LANES]


def tree(values, join):
    while len(values) > 1:
        values = [join(values[i], values[i + 1]) for i in range(0, len(values), 2)]
    return values[0]


def log_sum(values):
    peak = tree(values, jnp.maximum)
    return peak + jnp.log2(tree([jnp.exp2(value - peak) for value in values], jnp.add))


def product(rows, cols):
    return lax.dot_general(rows, cols, (((1,), (1,)), ((), ())), preferred_element_type=F32)


def ready(targets, mass, source_mass):
    part, chunk = targets.shape[0], mass.shape[0]

    def kernel(targets_ref, mass_ref, source_ref, packed_ref, mass_out, source_out):
        packed_ref[:part, :] = targets_ref[...]
        mass_out[...] = mass_ref[...]
        source_out[...] = jnp.log2(source_ref[...])
        value, pieces = mass_ref[...], []
        for step in range(PIECES):
            pieces.append(value.astype(jnp.bfloat16).astype(F32))
            value = value - pieces[-1]
        pieces.append(jnp.zeros_like(value))
        packed_ref[part:, :] = jnp.concatenate(pieces, axis=0).astype(jnp.bfloat16)

    return pl.pallas_call(
        kernel,
        out_shape=(
            pltpu.VMEM((part + (PIECES + 1) * chunk, LANES), jnp.bfloat16),
            pltpu.VMEM(mass.shape, F32),
            pltpu.VMEM(source_mass.shape, F32),
        ),
        in_specs=[VMEM] * 3,
        out_specs=(VMEM,) * 3,
        compiler_params=params(),
        cost_estimate=pl.CostEstimate(flops=1 << 20, bytes_accessed=1 << 20, transcendentals=0),
        name="ready",
    )(targets, mass, source_mass)


def pack(place, blocks):
    part = blocks[0].shape[0]

    def kernel(place_ref, *refs):
        out_ref = refs[-1]
        for step in range(len(blocks)):
            start = pl.multiple_of(jnp.bitwise_xor(place_ref[0], step) * part, part)
            out_ref[pl.ds(start, part), :] = refs[step][...]

    return pl.pallas_call(
        kernel,
        out_shape=pltpu.VMEM((len(blocks) * part, LANES), jnp.bfloat16),
        in_specs=[SMEM] + [VMEM] * len(blocks),
        out_specs=VMEM,
        compiler_params=params(),
        cost_estimate=pl.CostEstimate(flops=1 << 20, bytes_accessed=1 << 18, transcendentals=0),
        name="pack",
    )(place, *blocks)


def pieces_of(value):
    lane = lax.broadcasted_iota(jnp.int32, (value.shape[0], LANES), 1)
    tile = jnp.zeros((value.shape[0], LANES), F32)
    for step in range(PIECES):
        piece = value.astype(jnp.bfloat16).astype(F32)
        tile = jnp.where(lane == step, piece, tile)
        value = value - piece
    return tile.astype(jnp.bfloat16)


def ones_for(rows):
    lane = lax.broadcasted_iota(jnp.int32, (rows, LANES), 1)
    return jnp.where(lane < PIECES, 1.0, 0.0).astype(jnp.bfloat16)


class Rows:
    def __init__(self, count):
        self.peak = jnp.full((8, count), -1e30, F32)
        self.total = jnp.zeros((8, count), F32)

    def add(self, scores_ref):
        tops = self.peak
        for row in range(0, ROWS, 8):
            tops = jnp.maximum(tops, scores_ref[row : row + 8, :])
        self.total = self.total * jnp.exp2((self.peak - tops) * SCALE)
        self.peak = tops
        for row in range(0, ROWS, 8):
            self.total = self.total + jnp.exp2((scores_ref[row : row + 8, :] - tops) * SCALE)

    def lse(self):
        widest = jnp.max(self.peak, axis=0, keepdims=True)
        total = jnp.sum(self.total * jnp.exp2((self.peak - widest) * SCALE), axis=0, keepdims=True)
        return widest * SCALE + jnp.log2(total)


def first_rows(place, mass, packed, blocks, sources):
    count, chunk = sources.shape[0], mass.shape[0]
    n_src = len(blocks) // CORES + 1
    part = blocks[0].shape[0]
    width = CORES * n_src * part

    def kernel(place_ref, mass_ref, sources_ref, *refs):
        own_ref, other_ref, block_refs = refs[0], refs[1], refs[2 : 2 + len(blocks)]
        targets_ref, offset_ref, full_ref, out_ref, *score_refs = refs[2 + len(blocks) :]
        src, core = place_ref[0], place_ref[1]
        full_ref[pl.ds(pl.multiple_of(core * chunk, chunk), chunk), :] = mass_ref[...]
        parts = [other_ref[part + i * chunk : part + (i + 1) * chunk, :].astype(F32) for i in range(PIECES)]
        start = pl.multiple_of(jnp.bitwise_xor(core, 1) * chunk, chunk)
        full_ref[pl.ds(start, chunk), :] = parts[0] + (parts[1] + parts[2])
        for dc in range(CORES):
            for ds in range(n_src):
                index = jnp.bitwise_xor(core, dc) * n_src + jnp.bitwise_xor(src, ds)
                start = pl.multiple_of(index * part, part)
                ref = refs[dc] if ds == 0 else block_refs[dc * (n_src - 1) + ds - 1]
                targets_ref[pl.ds(start, part), :] = ref[:part, :]
        mask = diagonal()
        log_mass = jnp.log2(full_ref[...]) * (1.0 / SCALE)
        cols = jnp.concatenate([sources_ref[...], ones_for(count)], axis=1)
        rows = Rows(count)
        for at in range(0, width, ROWS):
            scores_ref = score_refs[at // ROWS % len(score_refs)]
            for row in range(at, at + ROWS, LANES):
                values = targets_ref[row : row + LANES, :].astype(F32)
                half = 0.5 * jnp.sum(values * values, axis=1, keepdims=True)
                block = row // LANES
                offset_ref[row : row + LANES, :] = pieces_of(to_column(log_mass[block : block + 1, :], mask) - half)
            scores_ref[...] = product(jnp.concatenate([targets_ref[at : at + ROWS, :], offset_ref[at : at + ROWS, :]], axis=1), cols)
            rows.add(scores_ref)
        fold_into(out_ref, rows.lse())

    return pl.pallas_call(
        kernel,
        out_shape=(
            pltpu.VMEM((width, LANES), jnp.bfloat16),
            pltpu.VMEM((width, LANES), jnp.bfloat16),
            rows_of(width),
            rows_of(count),
        ),
        in_specs=[SMEM] + [VMEM] * (4 + len(blocks)),
        out_specs=(VMEM,) * 4,
        scratch_shapes=[pltpu.VMEM((ROWS, count), F32)] * 2,
        compiler_params=params(),
        cost_estimate=pl.CostEstimate(flops=1 << 29, bytes_accessed=1 << 20, transcendentals=1 << 20),
        name="first_rows",
    )(place, mass, pin(sources), *[pin(value) for value in packed], *[pin(value) for value in blocks])


def other_rows(place, targets, offsets, first, groups):
    width, count, each = targets.shape[0], sum(group.shape[0] for group in groups), groups[0].shape[0] // LANES

    def kernel(place_ref, targets_ref, offset_ref, first_ref, *refs):
        group_refs, (out_ref, *score_refs) = refs[: len(groups)], refs[len(groups) :]
        cols = jnp.concatenate([ref[...] for ref in group_refs], axis=0)
        cols = jnp.concatenate([cols, ones_for(count)], axis=1)
        rows = Rows(count)
        for at in range(0, width, ROWS):
            scores_ref = score_refs[at // ROWS % len(score_refs)]
            scores_ref[...] = product(jnp.concatenate([targets_ref[at : at + ROWS, :], offset_ref[at : at + ROWS, :]], axis=1), cols)
            rows.add(scores_ref)
        lse = rows.lse()
        for step in range(len(groups) + 1):
            start = jnp.bitwise_xor(place_ref[2], step) * each
            for row in range(each):
                at = ((step - 1) * each + row) * LANES
                out_ref[pl.ds(start + row, 1), :] = first_ref[row : row + 1, :] if step == 0 else lse[:, at : at + LANES]

    return pl.pallas_call(
        kernel,
        out_shape=rows_of(count + each * LANES),
        in_specs=[SMEM] + [VMEM] * (3 + len(groups)),
        out_specs=VMEM,
        scratch_shapes=[pltpu.VMEM((ROWS, count), F32)] * 2,
        compiler_params=params(),
        name="other_rows",
    )(place, pin(targets), pin(offsets), first, *groups)


def first_columns(place, groups, targets, parts, log_mass):
    each, width = groups[0].shape[0], targets.shape[0]
    count = each * len(groups)

    def kernel(place_ref, targets_ref, parts_ref, log_ref, *refs):
        group_refs, (plan_ref, peak_ref, out_ref, lse_ref, sources_ref, *score_refs) = refs[: len(groups)], refs[len(groups) :]
        for step in range(len(groups)):
            start = pl.multiple_of(jnp.bitwise_xor(place_ref[2], step) * each, each)
            sources_ref[pl.ds(start, each), :] = group_refs[step][...]
        lse = log_sum([parts_ref[i] for i in range(parts.shape[0])])
        lse_ref[...] = lse
        mask = diagonal()
        shift = (log_ref[...] - lse) * (1.0 / SCALE)
        shift = [pieces_of(to_column(shift[i : i + 1, :], mask)) for i in range(count // LANES)]
        cols = jnp.concatenate([sources_ref[...], jnp.concatenate(shift, axis=0)], axis=1)
        ones = ones_for(ROWS)
        for at in range(0, width, ROWS):
            scores_ref = score_refs[at // ROWS % len(score_refs)]
            scores_ref[...] = product(jnp.concatenate([targets_ref[at : at + ROWS, :], ones], axis=1), cols)
            for block in range(0, ROWS, LANES):
                peaks, totals = [], []
                for row in range(block, block + LANES, 8):
                    scores = scores_ref[row : row + 8, :]
                    pieces = [scores[:, lane : lane + LANES] for lane in range(0, count, LANES)]
                    peak = tree(pieces, jnp.maximum)
                    pieces = [jnp.exp2((piece - peak) * SCALE) for piece in pieces]
                    plan_ref[at + row : at + row + 8, :] = jnp.concatenate(pieces, axis=1)
                    peaks.append(peak * SCALE)
                    totals.append(tree(pieces, jnp.add))
                peak = jnp.concatenate(peaks, axis=0)
                peak_ref[at + block : at + block + LANES, :] = peak
                peak, total = peak.T, jnp.concatenate(totals, axis=0).T
                top = jnp.max(peak, axis=0, keepdims=True)
                total = jnp.sum(total * jnp.exp2(peak - top), axis=0, keepdims=True)
                index = (at + block) // LANES
                out_ref[index : index + 1, :] = top + jnp.log2(total)

    return pl.pallas_call(
        kernel,
        out_shape=(
            pltpu.VMEM((width, count), F32),
            pltpu.VMEM((width, LANES), F32),
            rows_of(width),
            rows_of(count),
            pltpu.VMEM((count, LANES), jnp.bfloat16),
        ),
        in_specs=[SMEM] + [VMEM] * (3 + len(groups)),
        out_specs=(VMEM,) * 5,
        scratch_shapes=[pltpu.VMEM((ROWS, count), F32)] * 2,
        compiler_params=params(),
        name="first_columns",
    )(place, pin(targets), parts, log_mass, *[pin(group) for group in groups])


def weighted_rows(reach_of, weight, plan_ref, out_ref):
    count = plan_ref.shape[1]
    mask = diagonal()
    total = jnp.zeros((8, count), F32)
    for block in range(plan_ref.shape[0] // LANES):
        at = block * LANES
        reach = reach_of(at, block, mask) * to_column(weight[block : block + 1, :], mask)
        for row in range(0, LANES, 8):
            factor = jnp.concatenate([reach[row : row + 8, :]] * (count // LANES), axis=1)
            total = total + plan_ref[at + row : at + row + 8, :] * factor
    fold_into(out_ref, jnp.sum(total, axis=0, keepdims=True))


def second_rows(plan, peak, mass, parts):
    width, count = plan.shape

    def kernel(plan_ref, peak_ref, mass_ref, *refs):
        part_refs, (lse_ref, reach_ref, out_ref) = refs[:-3], refs[-3:]
        lse = log_sum([ref[...] for ref in part_refs])
        lse_ref[...] = lse

        def reach_of(at, block, mask):
            reach = jnp.exp2(peak_ref[at : at + LANES, :] - to_column(lse[block : block + 1, :], mask))
            reach_ref[at : at + LANES, :] = reach
            return reach

        weighted_rows(reach_of, mass_ref[...], plan_ref, out_ref)

    return pl.pallas_call(
        kernel,
        out_shape=(rows_of(width), pltpu.VMEM((width, LANES), F32), rows_of(count)),
        in_specs=[VMEM] * (3 + len(parts)),
        out_specs=(VMEM,) * 3,
        compiler_params=params(),
        name="second_rows",
    )(pin(plan), pin(peak), mass, *parts)


def later_rows(plan, reach, mass, parts):
    width, count = plan.shape

    def kernel(plan_ref, reach_ref, mass_ref, *refs):
        part_refs, out_ref = refs[:-1], refs[-1]
        weight = mass_ref[...] / tree([ref[...] for ref in part_refs], jnp.add)
        weighted_rows(lambda at, block, mask: reach_ref[at : at + LANES, :], weight, plan_ref, out_ref)

    return pl.pallas_call(
        kernel,
        out_shape=rows_of(count),
        in_specs=[VMEM] * (3 + len(parts)),
        out_specs=VMEM,
        compiler_params=params(),
        name="later_rows",
    )(pin(plan), pin(reach), mass, *parts)


def later_columns(plan, reach, parts, log_mass, lse, half):
    width, count = plan.shape

    def kernel(plan_ref, reach_ref, parts_ref, log_ref, lse_ref, half_ref, out_ref, potential_ref):
        factor = log_ref[...] - jnp.log2(tree([parts_ref[i] for i in range(parts.shape[0])], jnp.add))
        potential_ref[...] = half_ref[...] + UNIT * (factor - lse_ref[...])
        factor = unfold(jnp.exp2(factor))
        factors = [factor[:, lane : lane + LANES] for lane in range(0, count, LANES)]
        for at in range(0, width, LANES):
            totals = []
            for row in range(at, at + LANES, 8):
                plan = plan_ref[row : row + 8, :]
                totals.append(tree([plan[:, i * LANES : (i + 1) * LANES] * factors[i] for i in range(count // LANES)], jnp.add))
            total = jnp.concatenate(totals, axis=0) * reach_ref[at : at + LANES, :]
            out_ref[at // LANES : at // LANES + 1, :] = jnp.sum(total.T, axis=0, keepdims=True)

    return pl.pallas_call(
        kernel,
        out_shape=(rows_of(width), rows_of(count)),
        in_specs=[VMEM] * 6,
        out_specs=(VMEM,) * 2,
        compiler_params=params(),
        name="later_columns",
    )(pin(plan), pin(reach), parts, log_mass, lse, half)


def levels_of(size):
    bits = size.bit_length() - 1
    out = []
    while bits > 0:
        take = 2 if bits % 2 == 0 else 1
        bits -= take
        out.append([step << bits for step in range(1, 1 << take)])
    return out


def swap(value, axes, size, distance):
    return lax.ppermute(value, axes, [(i, i ^ distance) for i in range(size)])


def swap_all(value, axes, size):
    values = [value]
    for distances in levels_of(size):
        got = {d: [swap(value, axes, size, d) for value in values] for d in reversed(distances)}
        values = [part for i in range(len(values)) for part in [values[i]] + [got[d][i] for d in distances]]
    return values


def share(value, size):
    copies = jnp.broadcast_to(value[None], (size,) + value.shape)
    return lax.all_to_all(copies, ("z", "x"), 0, 0, tiled=True)


def half_norm(points):
    values = points.astype(F32)
    return 0.5 * jnp.sum(values * values, axis=1)


def make_local(n_src, n_z, n_x):
    near, n_near = ("src", "core"), n_src * CORES
    n_far = n_z * n_x

    def local(source_points, target_points, source_mass, target_mass):
        core, x = lax.axis_index("core"), lax.axis_index("x")
        place = jnp.stack([lax.axis_index("src"), core, x]).astype(jnp.int32)
        along = lax.axis_index("z").astype(jnp.int32).reshape(1)
        part = source_points.shape[0]
        a = source_mass.reshape(n_z, n_x, CORES, part)
        a = lax.dynamic_index_in_dim(a, core, axis=2, keepdims=False).swapaxes(0, 1).reshape(-1, LANES)
        blocks = swap_all(target_points, "src", n_src)[1:]
        sources = swap_all(source_points, "z", n_z)
        packed, b, a = ready(target_points, target_mass.reshape(-1, LANES), a)
        packed = swap_all(packed, "core", CORES)
        blocks = blocks + [swap(block, "core", CORES, 1) for block in blocks]
        groups = swap_all(pack(along, sources), "x", n_x)
        place, a = lax.optimization_barrier((place, a))
        targets, offsets, b, first = first_rows(place, b, packed, blocks, groups[0])
        own = other_rows(place, targets, offsets, first, groups[1:])
        plan, peak, own, row_lse, sources = first_columns(place, groups, targets, share(own, n_far), a)
        early_y, own = lax.optimization_barrier((targets, own))
        half_x, half_y = half_norm(sources).reshape(-1, LANES), half_norm(early_y).reshape(-1, LANES)
        parts = swap_all(own, near, n_near)
        half_x, half_y, *parts = lax.optimization_barrier((half_x, half_y, *parts))
        col_lse, reach, rows = second_rows(plan, peak, b, parts)
        for step in range(1, ITERS):
            if step > 1:
                rows = later_rows(plan, reach, b, parts)
            own, potential = later_columns(plan, reach, share(rows, n_far), a, row_lse, half_x)
            parts = swap_all(own, near, n_near)
        mine, other = swap_all(potential.reshape(n_x, n_z, part), "core", CORES)
        low, high = jnp.where(core == 0, mine, other), jnp.where(core == 0, other, mine)
        source_potential = jnp.stack([low, high], axis=2).swapaxes(0, 1).reshape(-1)
        target_potential = half_y - UNIT * (col_lse + jnp.log2(tree(parts, jnp.add)))
        target_potential = target_potential.reshape(CORES, -1)
        target_potential = lax.dynamic_index_in_dim(target_potential, core, axis=0, keepdims=False)
        return source_potential, target_potential

    return local


def solution(mesh):
    n_src, n_tgt = mesh.shape["src"], mesh.shape["tgt"]
    n_z = 4
    n_x = n_tgt // (n_z * CORES)
    split = Mesh(mesh.devices.reshape(n_src, n_z, n_x, CORES), ("src", "z", "x", "core"))
    tgt = ("z", "x", "core")
    placed = (P(("src", *tgt), None), P((*tgt, "src"), None), P("src"), P(tgt))
    return jax.shard_map(
        make_local(n_src, n_z, n_x),
        mesh=split,
        in_specs=placed,
        out_specs=(P("src"), P(tgt)),
        check_vma=False,
    )
```

```python
import math

import jax
import jax.numpy as jnp
from jax import lax
from jax.experimental import pallas as pl
from jax.experimental.pallas import tpu as pltpu
from jax.sharding import Mesh, PartitionSpec as P

ITERS = 3
EPS = 0.05
SCALE = 1.0 / (EPS * math.log(2.0))
UNIT = EPS * math.log(2.0)
LANES = 128
CORES = 2
PIECES = 3
ROWS = 256
F32 = jnp.float32
VMEM = pl.BlockSpec(memory_space=pltpu.VMEM)
SMEM = pl.BlockSpec(memory_space=pltpu.SMEM)


def params(limit=24):
    return pltpu.CompilerParams(vmem_limit_bytes=limit * 1024 * 1024)


def pin(value):
    return pltpu.with_memory_space_constraint(value, pltpu.VMEM)


def rows_of(count):
    return jax.ShapeDtypeStruct((count // LANES, LANES), F32)


def diagonal():
    shape = (LANES, LANES)
    return lax.broadcasted_iota(jnp.int32, shape, 0) == lax.broadcasted_iota(jnp.int32, shape, 1)


def to_column(row, mask):
    return jnp.sum(jnp.where(mask, jnp.broadcast_to(row, mask.shape), 0.0), axis=1, keepdims=True)


def to_row(column, mask):
    return jnp.sum(jnp.where(mask, jnp.broadcast_to(column, mask.shape), 0.0), axis=0, keepdims=True)


def unfold(value):
    return jnp.concatenate([value[i : i + 1, :] for i in range(value.shape[0])], axis=1)


def fold_into(ref, value):
    for row in range(ref.shape[0]):
        ref[row : row + 1, :] = value[:, row * LANES : (row + 1) * LANES]


def tree(values, join):
    while len(values) > 1:
        values = [join(values[i], values[i + 1]) for i in range(0, len(values), 2)]
    return values[0]


def log_sum(values):
    peak = tree(values, jnp.maximum)
    return peak + jnp.log2(tree([jnp.exp2(value - peak) for value in values], jnp.add))


def product(rows, cols):
    return lax.dot_general(rows, cols, (((1,), (1,)), ((), ())), preferred_element_type=F32)


def ready(sources, targets, mass, source_mass):
    part, chunk = targets.shape[0], mass.shape[0]
    anywhere = pl.BlockSpec(memory_space=pl.ANY)

    def kernel(sources_ref, targets_ref, mass_ref, source_ref, sources_out, packed_ref, mass_out, source_out, *sems):
        copies = [
            pltpu.make_async_copy(mass_ref, mass_out, sems[0]),
            pltpu.make_async_copy(targets_ref, packed_ref.at[:part], sems[1]),
            pltpu.make_async_copy(sources_ref, sources_out, sems[2]),
        ]
        for copy in copies:
            copy.start()
        source_out[...] = jnp.log2(source_ref[...])
        copies[0].wait()
        value, pieces = mass_out[...], []
        for step in range(PIECES):
            pieces.append(value.astype(jnp.bfloat16).astype(F32))
            value = value - pieces[-1]
        pieces.append(jnp.zeros_like(value))
        packed_ref[part:, :] = jnp.concatenate(pieces, axis=0).astype(jnp.bfloat16)
        copies[1].wait()
        copies[2].wait()

    return pl.pallas_call(
        kernel,
        out_shape=(
            pltpu.VMEM(sources.shape, jnp.bfloat16),
            pltpu.VMEM((part + (PIECES + 1) * chunk, LANES), jnp.bfloat16),
            pltpu.VMEM(mass.shape, F32),
            pltpu.VMEM(source_mass.shape, F32),
        ),
        in_specs=[anywhere, anywhere, anywhere, VMEM],
        out_specs=(VMEM,) * 4,
        scratch_shapes=[pltpu.SemaphoreType.DMA] * 3,
        compiler_params=params(),
        cost_estimate=pl.CostEstimate(flops=1 << 20, bytes_accessed=1 << 20, transcendentals=0),
        name="ready",
    )(*[pltpu.with_memory_space_constraint(value, pltpu.HBM) for value in (sources, targets, mass)], source_mass)


def pieces_of(value):
    lane = lax.broadcasted_iota(jnp.int32, (value.shape[0], LANES), 1)
    tile = jnp.zeros((value.shape[0], LANES), F32)
    for step in range(PIECES):
        piece = value.astype(jnp.bfloat16).astype(F32)
        tile = jnp.where(lane == step, piece, tile)
        value = value - piece
    return tile.astype(jnp.bfloat16)


def ones_for(rows):
    lane = lax.broadcasted_iota(jnp.int32, (rows, LANES), 1)
    return jnp.where(lane < PIECES, 1.0, 0.0).astype(jnp.bfloat16)


class Rows:
    def __init__(self, count):
        self.peak = jnp.full((8, count), -1e30, F32)
        self.total = jnp.zeros((8, count), F32)

    def add(self, scores_ref):
        tops = self.peak
        for row in range(0, ROWS, 8):
            tops = jnp.maximum(tops, scores_ref[row : row + 8, :])
        self.total = self.total * jnp.exp2((self.peak - tops) * SCALE)
        self.peak = tops
        for row in range(0, ROWS, 8):
            self.total = self.total + jnp.exp2((scores_ref[row : row + 8, :] - tops) * SCALE)

    def lse(self):
        widest = jnp.max(self.peak, axis=0, keepdims=True)
        total = jnp.sum(self.total * jnp.exp2((self.peak - widest) * SCALE), axis=0, keepdims=True)
        return widest * SCALE + jnp.log2(total)


class Units:
    def __init__(self, blocks, low, high):
        self.part = blocks[0][0].shape[0]
        self.each = max(1, LANES // self.part)
        self.n_z = len(blocks[0]) // self.each
        self.steps = [(dx, dz) for dz in range(low // self.each, high // self.each) for dx in range(len(blocks))]
        self.arrays = [blocks[dx][dz * self.each + inner] for dx, dz in self.steps for inner in range(self.each)]
        self.size = self.part * self.each
        self.count = self.size * len(self.steps)

    def place(self, place_ref, refs, out_ref, starts):
        for step, start in enumerate(starts):
            for inner in range(self.each):
                at = start
                if self.each > 1:
                    low = jnp.bitwise_and(place_ref[3], self.each - 1)
                    at = pl.multiple_of(start + jnp.bitwise_xor(low, inner) * self.part, self.part)
                out_ref[pl.ds(at, self.part), :] = refs[step * self.each + inner][...]

    def columns(self, place_ref, refs, scratch_ref):
        if self.each == 1:
            return jnp.concatenate([ref[...] for ref in refs], axis=0)
        self.place(place_ref, refs, scratch_ref, range(0, self.count, self.size))
        return scratch_ref[...]

    def starts(self, place_ref):
        high = place_ref[3] // self.each
        return [
            pl.multiple_of((jnp.bitwise_xor(place_ref[2], dx) * self.n_z + jnp.bitwise_xor(high, dz)) * self.size, self.size)
            for dx, dz in self.steps
        ]

    def write(self, place_ref, lse, out_ref):
        rows = self.size // LANES
        for step, start in enumerate(self.starts(place_ref)):
            for row in range(rows):
                at = (step * rows + row) * LANES
                out_ref[pl.ds(start // LANES + row, 1), :] = lse[:, at : at + LANES]


class Rows:
    def __init__(self, count):
        self.peak = jnp.full((8, count), -1e30, F32)
        self.total = jnp.zeros((8, count), F32)

    def add(self, scores_ref):
        tops = self.peak
        for row in range(0, ROWS, 8):
            tops = jnp.maximum(tops, scores_ref[row : row + 8, :])
        self.total = self.total * jnp.exp2((self.peak - tops) * SCALE)
        self.peak = tops
        for row in range(0, ROWS, 8):
            self.total = self.total + jnp.exp2((scores_ref[row : row + 8, :] - tops) * SCALE)

    def lse(self):
        widest = jnp.max(self.peak, axis=0, keepdims=True)
        total = jnp.sum(self.total * jnp.exp2((self.peak - widest) * SCALE), axis=0, keepdims=True)
        return widest * SCALE + jnp.log2(total)


def first_rows(place, mass, packed, blocks, units, total_rows):
    chunk, part = mass.shape[0], packed[0].shape[0] - (PIECES + 1) * mass.shape[0]
    n_src, n_units = len(blocks) // CORES + 1, len(units.arrays)
    width = CORES * n_src * part

    def kernel(place_ref, mass_ref, *refs):
        unit_refs, refs = refs[:n_units], refs[n_units:]
        other_ref, block_refs = refs[1], refs[2 : 2 + len(blocks)]
        targets_ref, offset_ref, full_ref, out_ref, scratch_ref, *score_refs = refs[2 + len(blocks) :]
        src, core = place_ref[0], place_ref[1]
        full_ref[pl.ds(pl.multiple_of(core * chunk, chunk), chunk), :] = mass_ref[...]
        parts = [other_ref[part + i * chunk : part + (i + 1) * chunk, :].astype(F32) for i in range(PIECES)]
        start = pl.multiple_of(jnp.bitwise_xor(core, 1) * chunk, chunk)
        full_ref[pl.ds(start, chunk), :] = parts[0] + (parts[1] + parts[2])
        for dc in range(CORES):
            for ds in range(n_src):
                index = jnp.bitwise_xor(core, dc) * n_src + jnp.bitwise_xor(src, ds)
                start = pl.multiple_of(index * part, part)
                ref = refs[dc] if ds == 0 else block_refs[dc * (n_src - 1) + ds - 1]
                targets_ref[pl.ds(start, part), :] = ref[:part, :]
        mask = diagonal()
        log_mass = jnp.log2(full_ref[...]) * (1.0 / SCALE)
        cols = jnp.concatenate([units.columns(place_ref, unit_refs, scratch_ref), ones_for(units.count)], axis=1)
        rows = Rows(units.count)
        for at in range(0, width, ROWS):
            scores_ref = score_refs[at // ROWS % len(score_refs)]
            for row in range(at, at + ROWS, LANES):
                values = targets_ref[row : row + LANES, :].astype(F32)
                half = 0.5 * jnp.sum(values * values, axis=1, keepdims=True)
                block = row // LANES
                offset_ref[row : row + LANES, :] = pieces_of(to_column(log_mass[block : block + 1, :], mask) - half)
            scores_ref[...] = product(jnp.concatenate([targets_ref[at : at + ROWS, :], offset_ref[at : at + ROWS, :]], axis=1), cols)
            rows.add(scores_ref)
        out_ref[...] = jnp.zeros_like(out_ref)
        units.write(place_ref, rows.lse(), out_ref)

    return pl.pallas_call(
        kernel,
        out_shape=(
            pltpu.VMEM((width, LANES), jnp.bfloat16),
            pltpu.VMEM((width, LANES), jnp.bfloat16),
            rows_of(width),
            pltpu.VMEM((total_rows, LANES), F32),
        ),
        in_specs=[SMEM] + [VMEM] * (3 + len(blocks) + n_units),
        out_specs=(VMEM,) * 4,
        scratch_shapes=[pltpu.VMEM((units.count, LANES), jnp.bfloat16)] + [pltpu.VMEM((ROWS, units.count), F32)] * 2,
        compiler_params=params(),
        cost_estimate=pl.CostEstimate(flops=1 << 29, bytes_accessed=1 << 20, transcendentals=1 << 20),
        name="first_rows",
    )(place, mass, *[pin(value) for value in units.arrays], *[pin(value) for value in packed], *[pin(value) for value in blocks])


def other_rows(place, targets, offsets, first, early, late):
    width, n_early = targets.shape[0], len(early.arrays)
    total = early.count + late.count

    def kernel(place_ref, targets_ref, offset_ref, first_ref, *refs):
        early_refs, late_refs = refs[:n_early], refs[n_early : n_early + len(late.arrays)]
        out_ref, sources_ref, scratch_ref, *score_refs = refs[n_early + len(late.arrays) :]
        cols = jnp.concatenate([late.columns(place_ref, late_refs, scratch_ref), ones_for(late.count)], axis=1)
        rows = Rows(late.count)
        for at in range(0, width, ROWS):
            scores_ref = score_refs[at // ROWS % len(score_refs)]
            scores_ref[...] = product(jnp.concatenate([targets_ref[at : at + ROWS, :], offset_ref[at : at + ROWS, :]], axis=1), cols)
            rows.add(scores_ref)
        early.place(place_ref, early_refs, sources_ref, early.starts(place_ref))
        late.place(place_ref, late_refs, sources_ref, late.starts(place_ref))
        out_ref[...] = first_ref[...]
        late.write(place_ref, rows.lse(), out_ref)

    return pl.pallas_call(
        kernel,
        out_shape=(rows_of(total), pltpu.VMEM((total, LANES), jnp.bfloat16)),
        in_specs=[SMEM] + [VMEM] * (3 + n_early + len(late.arrays)),
        out_specs=(VMEM,) * 2,
        scratch_shapes=[pltpu.VMEM((late.count, LANES), jnp.bfloat16)] + [pltpu.VMEM((ROWS, late.count), F32)] * 2,
        compiler_params=params(),
        name="other_rows",
    )(place, pin(targets), pin(offsets), pin(first), *[pin(value) for value in early.arrays], *[pin(value) for value in late.arrays])


def first_columns(sources, targets, parts, log_mass):
    count, width = sources.shape[0], targets.shape[0]

    def kernel(sources_ref, targets_ref, parts_ref, log_ref, plan_ref, peak_ref, out_ref, lse_ref, *score_refs):
        lse = log_sum([parts_ref[i] for i in range(parts.shape[0])])
        lse_ref[...] = lse
        mask = diagonal()
        shift = (log_ref[...] - lse) * (1.0 / SCALE)
        shift = [pieces_of(to_column(shift[i : i + 1, :], mask)) for i in range(count // LANES)]
        cols = jnp.concatenate([sources_ref[...], jnp.concatenate(shift, axis=0)], axis=1)
        ones = ones_for(ROWS)
        for at in range(0, width, ROWS):
            scores_ref = score_refs[at // ROWS % len(score_refs)]
            scores_ref[...] = product(jnp.concatenate([targets_ref[at : at + ROWS, :], ones], axis=1), cols)
            for block in range(0, ROWS, LANES):
                peaks, totals = [], []
                for row in range(block, block + LANES, 8):
                    scores = scores_ref[row : row + 8, :]
                    pieces = [scores[:, lane : lane + LANES] for lane in range(0, count, LANES)]
                    peak = tree(pieces, jnp.maximum)
                    pieces = [jnp.exp2((piece - peak) * SCALE) for piece in pieces]
                    plan_ref[at + row : at + row + 8, :] = jnp.concatenate(pieces, axis=1)
                    peaks.append(peak * SCALE)
                    totals.append(tree(pieces, jnp.add))
                peak = jnp.concatenate(peaks, axis=0)
                peak_ref[at + block : at + block + LANES, :] = peak
                peak, total = peak.T, jnp.concatenate(totals, axis=0).T
                top = jnp.max(peak, axis=0, keepdims=True)
                total = jnp.sum(total * jnp.exp2(peak - top), axis=0, keepdims=True)
                index = (at + block) // LANES
                out_ref[index : index + 1, :] = top + jnp.log2(total)

    return pl.pallas_call(
        kernel,
        out_shape=(
            pltpu.VMEM((width, count), F32),
            pltpu.VMEM((width, LANES), F32),
            rows_of(width),
            rows_of(count),
        ),
        in_specs=[VMEM] * 4,
        out_specs=(VMEM,) * 4,
        scratch_shapes=[pltpu.VMEM((ROWS, count), F32)] * 2,
        compiler_params=params(),
        name="first_columns",
    )(pin(sources), pin(targets), parts, log_mass)


def weighted_rows(reach_of, weight, plan_ref, out_ref):
    count = plan_ref.shape[1]
    mask = diagonal()
    total = jnp.zeros((8, count), F32)
    for block in range(plan_ref.shape[0] // LANES):
        at = block * LANES
        reach = reach_of(at, block, mask) * to_column(weight[block : block + 1, :], mask)
        for row in range(0, LANES, 8):
            factor = jnp.concatenate([reach[row : row + 8, :]] * (count // LANES), axis=1)
            total = total + plan_ref[at + row : at + row + 8, :] * factor
    fold_into(out_ref, jnp.sum(total, axis=0, keepdims=True))


def second_rows(plan, peak, mass, parts):
    width, count = plan.shape

    def kernel(plan_ref, peak_ref, mass_ref, *refs):
        part_refs, (lse_ref, reach_ref, out_ref) = refs[:-3], refs[-3:]
        lse = log_sum([ref[...] for ref in part_refs])
        lse_ref[...] = lse

        def reach_of(at, block, mask):
            reach = jnp.exp2(peak_ref[at : at + LANES, :] - to_column(lse[block : block + 1, :], mask))
            reach_ref[at : at + LANES, :] = reach
            return reach

        weighted_rows(reach_of, mass_ref[...], plan_ref, out_ref)

    return pl.pallas_call(
        kernel,
        out_shape=(rows_of(width), pltpu.VMEM((width, LANES), F32), rows_of(count)),
        in_specs=[VMEM] * (3 + len(parts)),
        out_specs=(VMEM,) * 3,
        compiler_params=params(),
        name="second_rows",
    )(pin(plan), pin(peak), mass, *parts)


def later_rows(plan, reach, mass, parts):
    width, count = plan.shape

    def kernel(plan_ref, reach_ref, mass_ref, *refs):
        part_refs, out_ref = refs[:-1], refs[-1]
        weight = mass_ref[...] / tree([ref[...] for ref in part_refs], jnp.add)
        weighted_rows(lambda at, block, mask: reach_ref[at : at + LANES, :], weight, plan_ref, out_ref)

    return pl.pallas_call(
        kernel,
        out_shape=rows_of(count),
        in_specs=[VMEM] * (3 + len(parts)),
        out_specs=VMEM,
        compiler_params=params(),
        name="later_rows",
    )(pin(plan), pin(reach), mass, *parts)


def later_columns(plan, reach, parts, log_mass, lse, half):
    width, count = plan.shape

    def kernel(plan_ref, reach_ref, parts_ref, log_ref, lse_ref, half_ref, out_ref, potential_ref):
        factor = log_ref[...] - jnp.log2(tree([parts_ref[i] for i in range(parts.shape[0])], jnp.add))
        potential_ref[...] = half_ref[...] + UNIT * (factor - lse_ref[...])
        factor = unfold(jnp.exp2(factor))
        factors = [factor[:, lane : lane + LANES] for lane in range(0, count, LANES)]
        for at in range(0, width, LANES):
            totals = []
            for row in range(at, at + LANES, 8):
                plan = plan_ref[row : row + 8, :]
                totals.append(tree([plan[:, i * LANES : (i + 1) * LANES] * factors[i] for i in range(count // LANES)], jnp.add))
            total = jnp.concatenate(totals, axis=0) * reach_ref[at : at + LANES, :]
            out_ref[at // LANES : at // LANES + 1, :] = jnp.sum(total.T, axis=0, keepdims=True)

    return pl.pallas_call(
        kernel,
        out_shape=(rows_of(width), rows_of(count)),
        in_specs=[VMEM] * 6,
        out_specs=(VMEM,) * 2,
        compiler_params=params(),
        name="later_columns",
    )(pin(plan), pin(reach), parts, log_mass, lse, half)


def levels_of(size):
    bits = size.bit_length() - 1
    out = []
    while bits > 0:
        take = 2 if bits % 2 == 0 else 1
        bits -= take
        out.append([step << bits for step in range(1, 1 << take)])
    return out


def swap(value, axes, size, distance):
    return lax.ppermute(value, axes, [(i, i ^ distance) for i in range(size)])


def swap_all(value, axes, size):
    values = [value]
    for distances in levels_of(size):
        got = {d: [swap(value, axes, size, d) for value in values] for d in reversed(distances)}
        values = [part for i in range(len(values)) for part in [values[i]] + [got[d][i] for d in distances]]
    return values


def share(value, size):
    copies = jnp.broadcast_to(value[None], (size,) + value.shape)
    return lax.all_to_all(copies, ("z", "x"), 0, 0, tiled=True)


def half_norm(points):
    values = points.astype(F32)
    return 0.5 * jnp.sum(values * values, axis=1)


def make_local(n_src, n_z, n_x):
    near, n_near = ("src", "core"), n_src * CORES
    n_far = n_z * n_x

    def local(source_points, target_points, source_mass, target_mass):
        core = lax.axis_index("core")
        place = jnp.stack([lax.axis_index(axis) for axis in ("src", "core", "x", "z")]).astype(jnp.int32)
        part = source_points.shape[0]
        a = source_mass.reshape(n_z, n_x, CORES, part)
        a = lax.dynamic_index_in_dim(a, core, axis=2, keepdims=False).swapaxes(0, 1).reshape(-1, LANES)
        two = swap(source_points, "z", n_z, 2)
        blocks = swap_all(target_points, "src", n_src)[1:]
        one = swap(source_points, "z", n_z, 1)
        sources = [source_points, one, two, swap(two, "z", n_z, 1)]
        across = [[swap(block, "x", n_x, dx) for block in sources] for dx in range(1, n_x)]
        mine, packed, b, a = ready(source_points, target_points, target_mass.reshape(-1, LANES), a)
        sources = [[mine, *sources[1:]], *across]
        packed = swap_all(packed, "core", CORES)
        blocks = blocks + [swap(block, "core", CORES, 1) for block in blocks]
        place, a = lax.optimization_barrier((place, a))
        last = n_z - max(1, LANES // part)
        early, late = Units(sources, 0, last), Units(sources, last, n_z)
        targets, offsets, b, first = first_rows(place, b, packed, blocks, early, a.shape[0])
        own, sources = other_rows(place, targets, offsets, first, early, late)
        plan, peak, own, row_lse = first_columns(sources, targets, share(own, n_far), a)
        early_x, early_y, own = lax.optimization_barrier((sources, targets, own))
        half_x, half_y = half_norm(early_x).reshape(-1, LANES), half_norm(early_y).reshape(-1, LANES)
        parts = swap_all(own, near, n_near)
        half_x, half_y, *parts = lax.optimization_barrier((half_x, half_y, *parts))
        col_lse, reach, rows = second_rows(plan, peak, b, parts)
        for step in range(1, ITERS):
            if step > 1:
                rows = later_rows(plan, reach, b, parts)
            own, potential = later_columns(plan, reach, share(rows, n_far), a, row_lse, half_x)
            parts = swap_all(own, near, n_near)
        mine, other = swap_all(potential.reshape(n_x, n_z, part), "core", CORES)
        low, high = jnp.where(core == 0, mine, other), jnp.where(core == 0, other, mine)
        source_potential = jnp.stack([low, high], axis=2).swapaxes(0, 1).reshape(-1)
        target_potential = half_y - UNIT * (col_lse + jnp.log2(tree(parts, jnp.add)))
        target_potential = target_potential.reshape(CORES, -1)
        target_potential = lax.dynamic_index_in_dim(target_potential, core, axis=0, keepdims=False)
        return source_potential, target_potential

    return local


def solution(mesh):
    n_src, n_tgt = mesh.shape["src"], mesh.shape["tgt"]
    n_z = 4
    n_x = n_tgt // (n_z * CORES)
    split = Mesh(mesh.devices.reshape(n_src, n_z, n_x, CORES), ("src", "z", "x", "core"))
    tgt = ("z", "x", "core")
    placed = (P(("src", *tgt), None), P((*tgt, "src"), None), P("src"), P(tgt))
    return jax.shard_map(
        make_local(n_src, n_z, n_x),
        mesh=split,
        in_specs=placed,
        out_specs=(P("src"), P(tgt)),
        check_vma=False,
    )
```

```python
import math

import jax
import jax.numpy as jnp
from jax import lax
from jax.experimental import pallas as pl
from jax.experimental.pallas import tpu as pltpu
from jax.sharding import Mesh, PartitionSpec as P

ITERS = 3
EPS = 0.05
SCALE = 1.0 / (EPS * math.log(2.0))
UNIT = EPS * math.log(2.0)
LANES = 128
CORES = 2
PIECES = 3
ROWS = 256
F32 = jnp.float32
VMEM = pl.BlockSpec(memory_space=pltpu.VMEM)
SMEM = pl.BlockSpec(memory_space=pltpu.SMEM)


def params(limit=24):
    return pltpu.CompilerParams(vmem_limit_bytes=limit * 1024 * 1024)


def pin(value):
    return pltpu.with_memory_space_constraint(value, pltpu.VMEM)


def rows_of(count):
    return jax.ShapeDtypeStruct((count // LANES, LANES), F32)


def diagonal():
    shape = (LANES, LANES)
    return lax.broadcasted_iota(jnp.int32, shape, 0) == lax.broadcasted_iota(jnp.int32, shape, 1)


def to_column(row, mask):
    return jnp.sum(jnp.where(mask, jnp.broadcast_to(row, mask.shape), 0.0), axis=1, keepdims=True)


def to_row(column, mask):
    return jnp.sum(jnp.where(mask, jnp.broadcast_to(column, mask.shape), 0.0), axis=0, keepdims=True)


def unfold(value):
    return jnp.concatenate([value[i : i + 1, :] for i in range(value.shape[0])], axis=1)


def fold_into(ref, value):
    for row in range(ref.shape[0]):
        ref[row : row + 1, :] = value[:, row * LANES : (row + 1) * LANES]


def tree(values, join):
    while len(values) > 1:
        values = [join(values[i], values[i + 1]) for i in range(0, len(values), 2)]
    return values[0]


def log_sum(values):
    peak = tree(values, jnp.maximum)
    return peak + jnp.log2(tree([jnp.exp2(value - peak) for value in values], jnp.add))


def product(rows, cols):
    return lax.dot_general(rows, cols, (((1,), (1,)), ((), ())), preferred_element_type=F32)


def ready(sources, targets, mass, source_mass):
    part, chunk = targets.shape[0], mass.shape[0]
    anywhere = pl.BlockSpec(memory_space=pl.ANY)

    def kernel(sources_ref, targets_ref, mass_ref, source_ref, sources_out, packed_ref, mass_out, source_out, *sems):
        copies = [
            pltpu.make_async_copy(mass_ref, mass_out, sems[0]),
            pltpu.make_async_copy(targets_ref, packed_ref.at[:part], sems[1]),
            pltpu.make_async_copy(sources_ref, sources_out, sems[2]),
        ]
        for copy in copies:
            copy.start()
        source_out[...] = jnp.log2(source_ref[...])
        copies[0].wait()
        value, pieces = mass_out[...], []
        for step in range(PIECES):
            pieces.append(value.astype(jnp.bfloat16).astype(F32))
            value = value - pieces[-1]
        pieces.append(jnp.zeros_like(value))
        packed_ref[part:, :] = jnp.concatenate(pieces, axis=0).astype(jnp.bfloat16)
        copies[1].wait()
        copies[2].wait()

    return pl.pallas_call(
        kernel,
        out_shape=(
            pltpu.VMEM(sources.shape, jnp.bfloat16),
            pltpu.VMEM((part + (PIECES + 1) * chunk, LANES), jnp.bfloat16),
            pltpu.VMEM(mass.shape, F32),
            pltpu.VMEM(source_mass.shape, F32),
        ),
        in_specs=[anywhere, anywhere, anywhere, VMEM],
        out_specs=(VMEM,) * 4,
        scratch_shapes=[pltpu.SemaphoreType.DMA] * 3,
        compiler_params=params(),
        cost_estimate=pl.CostEstimate(flops=1 << 20, bytes_accessed=1 << 20, transcendentals=0),
        name="ready",
    )(*[pltpu.with_memory_space_constraint(value, pltpu.HBM) for value in (sources, targets, mass)], source_mass)


def lay(place, block, step, count):
    part = block.shape[0]

    def kernel(place_ref, block_ref, out_ref):
        start = pl.multiple_of(jnp.bitwise_xor(place_ref[0], step) * part, part)
        out_ref[pl.ds(start, part), :] = block_ref[...]

    return pl.pallas_call(
        kernel,
        out_shape=pltpu.VMEM((count * part, LANES), jnp.bfloat16),
        in_specs=[SMEM, VMEM],
        out_specs=VMEM,
        compiler_params=params(),
        cost_estimate=pl.CostEstimate(flops=1 << 20, bytes_accessed=1 << 20, transcendentals=0),
        name="lay",
    )(place, block)


def pack(place, blocks, laid):
    part = blocks[0].shape[0]

    def kernel(place_ref, *refs):
        out_ref = refs[-1]
        for step in range(len(blocks)):
            start = pl.multiple_of(jnp.bitwise_xor(place_ref[0], step) * part, part)
            out_ref[pl.ds(start, part), :] = refs[step][...]

    return pl.pallas_call(
        kernel,
        out_shape=pltpu.VMEM(laid.shape, jnp.bfloat16),
        in_specs=[SMEM] + [VMEM] * (len(blocks) + 1),
        out_specs=VMEM,
        input_output_aliases={1 + len(blocks): 0},
        compiler_params=params(),
        cost_estimate=pl.CostEstimate(flops=1 << 20, bytes_accessed=1 << 18, transcendentals=0),
        name="pack",
    )(place, *blocks, laid)


def pieces_of(value):
    lane = lax.broadcasted_iota(jnp.int32, (value.shape[0], LANES), 1)
    tile = jnp.zeros((value.shape[0], LANES), F32)
    for step in range(PIECES):
        piece = value.astype(jnp.bfloat16).astype(F32)
        tile = jnp.where(lane == step, piece, tile)
        value = value - piece
    return tile.astype(jnp.bfloat16)


def ones_for(rows):
    lane = lax.broadcasted_iota(jnp.int32, (rows, LANES), 1)
    return jnp.where(lane < PIECES, 1.0, 0.0).astype(jnp.bfloat16)


class Rows:
    def __init__(self, count):
        self.peak = jnp.full((8, count), -1e30, F32)
        self.total = jnp.zeros((8, count), F32)

    def add(self, scores_ref):
        tops = self.peak
        for row in range(0, ROWS, 8):
            tops = jnp.maximum(tops, scores_ref[row : row + 8, :])
        self.total = self.total * jnp.exp2((self.peak - tops) * SCALE)
        self.peak = tops
        for row in range(0, ROWS, 8):
            self.total = self.total + jnp.exp2((scores_ref[row : row + 8, :] - tops) * SCALE)

    def lse(self):
        widest = jnp.max(self.peak, axis=0, keepdims=True)
        total = jnp.sum(self.total * jnp.exp2((self.peak - widest) * SCALE), axis=0, keepdims=True)
        return widest * SCALE + jnp.log2(total)


def first_rows(place, mass, packed, blocks, sources):
    count, chunk = sources.shape[0], mass.shape[0]
    n_src = len(blocks) // CORES + 1
    part = blocks[0].shape[0]
    width = CORES * n_src * part

    def kernel(place_ref, mass_ref, sources_ref, *refs):
        own_ref, other_ref, block_refs = refs[0], refs[1], refs[2 : 2 + len(blocks)]
        targets_ref, offset_ref, full_ref, out_ref, *score_refs = refs[2 + len(blocks) :]
        src, core = place_ref[0], place_ref[1]
        full_ref[pl.ds(pl.multiple_of(core * chunk, chunk), chunk), :] = mass_ref[...]
        parts = [other_ref[part + i * chunk : part + (i + 1) * chunk, :].astype(F32) for i in range(PIECES)]
        start = pl.multiple_of(jnp.bitwise_xor(core, 1) * chunk, chunk)
        full_ref[pl.ds(start, chunk), :] = parts[0] + (parts[1] + parts[2])
        for dc in range(CORES):
            for ds in range(n_src):
                index = jnp.bitwise_xor(core, dc) * n_src + jnp.bitwise_xor(src, ds)
                start = pl.multiple_of(index * part, part)
                ref = refs[dc] if ds == 0 else block_refs[dc * (n_src - 1) + ds - 1]
                targets_ref[pl.ds(start, part), :] = ref[:part, :]
        mask = diagonal()
        log_mass = jnp.log2(full_ref[...]) * (1.0 / SCALE)
        cols = jnp.concatenate([sources_ref[...], ones_for(count)], axis=1)
        rows = Rows(count)
        for at in range(0, width, ROWS):
            scores_ref = score_refs[at // ROWS % len(score_refs)]
            for row in range(at, at + ROWS, LANES):
                values = targets_ref[row : row + LANES, :].astype(F32)
                half = 0.5 * jnp.sum(values * values, axis=1, keepdims=True)
                block = row // LANES
                offset_ref[row : row + LANES, :] = pieces_of(to_column(log_mass[block : block + 1, :], mask) - half)
            scores_ref[...] = product(jnp.concatenate([targets_ref[at : at + ROWS, :], offset_ref[at : at + ROWS, :]], axis=1), cols)
            rows.add(scores_ref)
        fold_into(out_ref, rows.lse())

    return pl.pallas_call(
        kernel,
        out_shape=(
            pltpu.VMEM((width, LANES), jnp.bfloat16),
            pltpu.VMEM((width, LANES), jnp.bfloat16),
            rows_of(width),
            rows_of(count),
        ),
        in_specs=[SMEM] + [VMEM] * (4 + len(blocks)),
        out_specs=(VMEM,) * 4,
        scratch_shapes=[pltpu.VMEM((ROWS, count), F32)] * 2,
        compiler_params=params(),
        cost_estimate=pl.CostEstimate(flops=1 << 29, bytes_accessed=1 << 20, transcendentals=1 << 20),
        name="first_rows",
    )(place, mass, pin(sources), *[pin(value) for value in packed], *[pin(value) for value in blocks])


def other_rows(place, targets, offsets, first, groups):
    mine, groups = groups[0], groups[1:]
    width, count, each = targets.shape[0], sum(group.shape[0] for group in groups), mine.shape[0] // LANES

    def kernel(place_ref, targets_ref, offset_ref, first_ref, mine_ref, *refs):
        group_refs, (out_ref, sources_ref, *score_refs) = refs[: len(groups)], refs[len(groups) :]
        cols = jnp.concatenate([ref[...] for ref in group_refs], axis=0)
        cols = jnp.concatenate([cols, ones_for(count)], axis=1)
        rows = Rows(count)
        for at in range(0, width, ROWS):
            scores_ref = score_refs[at // ROWS % len(score_refs)]
            scores_ref[...] = product(jnp.concatenate([targets_ref[at : at + ROWS, :], offset_ref[at : at + ROWS, :]], axis=1), cols)
            rows.add(scores_ref)
        lse = rows.lse()
        for step in range(len(groups) + 1):
            start = jnp.bitwise_xor(place_ref[2], step) * each
            ref = group_refs[step - 1] if step else mine_ref
            sources_ref[pl.ds(pl.multiple_of(start * LANES, each * LANES), each * LANES), :] = ref[...]
            for row in range(each):
                at = ((step - 1) * each + row) * LANES
                out_ref[pl.ds(start + row, 1), :] = first_ref[row : row + 1, :] if step == 0 else lse[:, at : at + LANES]

    return pl.pallas_call(
        kernel,
        out_shape=(rows_of(count + each * LANES), pltpu.VMEM((count + each * LANES, LANES), jnp.bfloat16)),
        in_specs=[SMEM] + [VMEM] * (3 + len(groups) + 1),
        out_specs=(VMEM,) * 2,
        scratch_shapes=[pltpu.VMEM((ROWS, count), F32)] * 2,
        compiler_params=params(),
        name="other_rows",
    )(place, pin(targets), pin(offsets), first, pin(mine), *groups)


def first_columns(sources, targets, parts, log_mass):
    count, width = sources.shape[0], targets.shape[0]

    def kernel(sources_ref, targets_ref, parts_ref, log_ref, plan_ref, peak_ref, out_ref, lse_ref, *score_refs):
        lse = log_sum([parts_ref[i] for i in range(parts.shape[0])])
        lse_ref[...] = lse
        mask = diagonal()
        shift = (log_ref[...] - lse) * (1.0 / SCALE)
        shift = [pieces_of(to_column(shift[i : i + 1, :], mask)) for i in range(count // LANES)]
        cols = jnp.concatenate([sources_ref[...], jnp.concatenate(shift, axis=0)], axis=1)
        ones = ones_for(ROWS)
        for at in range(0, width, ROWS):
            scores_ref = score_refs[at // ROWS % len(score_refs)]
            scores_ref[...] = product(jnp.concatenate([targets_ref[at : at + ROWS, :], ones], axis=1), cols)
            for block in range(0, ROWS, LANES):
                peaks, totals = [], []
                for row in range(block, block + LANES, 8):
                    scores = scores_ref[row : row + 8, :]
                    pieces = [scores[:, lane : lane + LANES] for lane in range(0, count, LANES)]
                    peak = tree(pieces, jnp.maximum)
                    pieces = [jnp.exp2((piece - peak) * SCALE) for piece in pieces]
                    plan_ref[at + row : at + row + 8, :] = jnp.concatenate(pieces, axis=1)
                    peaks.append(peak * SCALE)
                    totals.append(tree(pieces, jnp.add))
                peak = jnp.concatenate(peaks, axis=0)
                peak_ref[at + block : at + block + LANES, :] = peak
                peak, total = peak.T, jnp.concatenate(totals, axis=0).T
                top = jnp.max(peak, axis=0, keepdims=True)
                total = jnp.sum(total * jnp.exp2(peak - top), axis=0, keepdims=True)
                index = (at + block) // LANES
                out_ref[index : index + 1, :] = top + jnp.log2(total)

    return pl.pallas_call(
        kernel,
        out_shape=(
            pltpu.VMEM((width, count), F32),
            pltpu.VMEM((width, LANES), F32),
            rows_of(width),
            rows_of(count),
        ),
        in_specs=[VMEM] * 4,
        out_specs=(VMEM,) * 4,
        scratch_shapes=[pltpu.VMEM((ROWS, count), F32)] * 2,
        compiler_params=params(),
        name="first_columns",
    )(pin(sources), pin(targets), parts, log_mass)


def weighted_rows(reach_of, weight, plan_ref, out_ref):
    count = plan_ref.shape[1]
    mask = diagonal()
    total = jnp.zeros((8, count), F32)
    for block in range(plan_ref.shape[0] // LANES):
        at = block * LANES
        reach = reach_of(at, block, mask) * to_column(weight[block : block + 1, :], mask)
        for row in range(0, LANES, 8):
            factor = jnp.concatenate([reach[row : row + 8, :]] * (count // LANES), axis=1)
            total = total + plan_ref[at + row : at + row + 8, :] * factor
    fold_into(out_ref, jnp.sum(total, axis=0, keepdims=True))


def second_rows(plan, peak, mass, parts):
    width, count = plan.shape

    def kernel(plan_ref, peak_ref, mass_ref, *refs):
        part_refs, (lse_ref, reach_ref, out_ref) = refs[:-3], refs[-3:]
        lse = log_sum([ref[...] for ref in part_refs])
        lse_ref[...] = lse

        def reach_of(at, block, mask):
            reach = jnp.exp2(peak_ref[at : at + LANES, :] - to_column(lse[block : block + 1, :], mask))
            reach_ref[at : at + LANES, :] = reach
            return reach

        weighted_rows(reach_of, mass_ref[...], plan_ref, out_ref)

    return pl.pallas_call(
        kernel,
        out_shape=(rows_of(width), pltpu.VMEM((width, LANES), F32), rows_of(count)),
        in_specs=[VMEM] * (3 + len(parts)),
        out_specs=(VMEM,) * 3,
        compiler_params=params(),
        name="second_rows",
    )(pin(plan), pin(peak), mass, *parts)


def later_rows(plan, reach, mass, parts):
    width, count = plan.shape

    def kernel(plan_ref, reach_ref, mass_ref, *refs):
        part_refs, out_ref = refs[:-1], refs[-1]
        weight = mass_ref[...] / tree([ref[...] for ref in part_refs], jnp.add)
        weighted_rows(lambda at, block, mask: reach_ref[at : at + LANES, :], weight, plan_ref, out_ref)

    return pl.pallas_call(
        kernel,
        out_shape=rows_of(count),
        in_specs=[VMEM] * (3 + len(parts)),
        out_specs=VMEM,
        compiler_params=params(),
        name="later_rows",
    )(pin(plan), pin(reach), mass, *parts)


def later_columns(plan, reach, parts, log_mass, lse, half):
    width, count = plan.shape

    def kernel(plan_ref, reach_ref, parts_ref, log_ref, lse_ref, half_ref, out_ref, potential_ref):
        factor = log_ref[...] - jnp.log2(tree([parts_ref[i] for i in range(parts.shape[0])], jnp.add))
        potential_ref[...] = half_ref[...] + UNIT * (factor - lse_ref[...])
        factor = unfold(jnp.exp2(factor))
        factors = [factor[:, lane : lane + LANES] for lane in range(0, count, LANES)]
        for at in range(0, width, LANES):
            totals = []
            for row in range(at, at + LANES, 8):
                plan = plan_ref[row : row + 8, :]
                totals.append(tree([plan[:, i * LANES : (i + 1) * LANES] * factors[i] for i in range(count // LANES)], jnp.add))
            total = jnp.concatenate(totals, axis=0) * reach_ref[at : at + LANES, :]
            out_ref[at // LANES : at // LANES + 1, :] = jnp.sum(total.T, axis=0, keepdims=True)

    return pl.pallas_call(
        kernel,
        out_shape=(rows_of(width), rows_of(count)),
        in_specs=[VMEM] * 6,
        out_specs=(VMEM,) * 2,
        compiler_params=params(),
        name="later_columns",
    )(pin(plan), pin(reach), parts, log_mass, lse, half)


def levels_of(size):
    bits = size.bit_length() - 1
    out = []
    while bits > 0:
        take = 2 if bits % 2 == 0 else 1
        bits -= take
        out.append([step << bits for step in range(1, 1 << take)])
    return out


def swap(value, axes, size, distance):
    return lax.ppermute(value, axes, [(i, i ^ distance) for i in range(size)])


def swap_all(value, axes, size):
    values = [value]
    for distances in levels_of(size):
        got = {d: [swap(value, axes, size, d) for value in values] for d in reversed(distances)}
        values = [part for i in range(len(values)) for part in [values[i]] + [got[d][i] for d in distances]]
    return values


def share(value, size):
    copies = jnp.broadcast_to(value[None], (size,) + value.shape)
    return lax.all_to_all(copies, ("z", "x"), 0, 0, tiled=True)


def half_norm(points):
    values = points.astype(F32)
    return 0.5 * jnp.sum(values * values, axis=1)


def make_local(n_src, n_z, n_x):
    near, n_near = ("src", "core"), n_src * CORES
    n_far = n_z * n_x

    def local(source_points, target_points, source_mass, target_mass):
        core, x = lax.axis_index("core"), lax.axis_index("x")
        place = jnp.stack([lax.axis_index("src"), core, x]).astype(jnp.int32)
        along = lax.axis_index("z").astype(jnp.int32).reshape(1)
        part = source_points.shape[0]
        a = source_mass.reshape(n_z, n_x, CORES, part)
        a = lax.dynamic_index_in_dim(a, core, axis=2, keepdims=False).swapaxes(0, 1).reshape(-1, LANES)
        blocks = swap_all(target_points, "src", n_src)[1:]
        three, two, one = [swap(source_points, "z", n_z, d) for d in (3, 2, 1)]
        mine, packed, b, a = ready(source_points, target_points, target_mass.reshape(-1, LANES), a)
        laid = lay(along, three, 3, n_z)
        packed = swap_all(packed, "core", CORES)
        blocks = blocks + [swap(block, "core", CORES, 1) for block in blocks]
        groups = swap_all(pack(along, [mine, one, two], laid), "x", n_x)
        place, a = lax.optimization_barrier((place, a))
        targets, offsets, b, first = first_rows(place, b, packed, blocks, groups[0])
        own, sources = other_rows(place, targets, offsets, first, groups)
        plan, peak, own, row_lse = first_columns(sources, targets, share(own, n_far), a)
        early_x, early_y, own = lax.optimization_barrier((sources, targets, own))
        half_x, half_y = half_norm(early_x).reshape(-1, LANES), half_norm(early_y).reshape(-1, LANES)
        parts = swap_all(own, near, n_near)
        half_x, half_y, *parts = lax.optimization_barrier((half_x, half_y, *parts))
        col_lse, reach, rows = second_rows(plan, peak, b, parts)
        for step in range(1, ITERS):
            if step > 1:
                rows = later_rows(plan, reach, b, parts)
            own, potential = later_columns(plan, reach, share(rows, n_far), a, row_lse, half_x)
            parts = swap_all(own, near, n_near)
        mine, other = swap_all(potential.reshape(n_x, n_z, part), "core", CORES)
        low, high = jnp.where(core == 0, mine, other), jnp.where(core == 0, other, mine)
        source_potential = jnp.stack([low, high], axis=2).swapaxes(0, 1).reshape(-1)
        target_potential = half_y - UNIT * (col_lse + jnp.log2(tree(parts, jnp.add)))
        target_potential = target_potential.reshape(CORES, -1)
        target_potential = lax.dynamic_index_in_dim(target_potential, core, axis=0, keepdims=False)
        return source_potential, target_potential

    return local


def solution(mesh):
    n_src, n_tgt = mesh.shape["src"], mesh.shape["tgt"]
    n_z = 4
    n_x = n_tgt // (n_z * CORES)
    split = Mesh(mesh.devices.reshape(n_src, n_z, n_x, CORES), ("src", "z", "x", "core"))
    tgt = ("z", "x", "core")
    placed = (P(("src", *tgt), None), P((*tgt, "src"), None), P("src"), P(tgt))
    return jax.shard_map(
        make_local(n_src, n_z, n_x),
        mesh=split,
        in_specs=placed,
        out_specs=(P("src"), P(tgt)),
        check_vma=False,
    )
```

```python
import math

import jax
import jax.numpy as jnp
from jax import lax
from jax.experimental import pallas as pl
from jax.experimental.pallas import tpu as pltpu
from jax.sharding import Mesh, PartitionSpec as P

ITERS = 3
EPS = 0.05
SCALE = 1.0 / (EPS * math.log(2.0))
UNIT = EPS * math.log(2.0)
LANES = 128
CORES = 2
PIECES = 3
ROWS = 256
TURNS = 2
F32 = jnp.float32
VMEM = pl.BlockSpec(memory_space=pltpu.VMEM)
SMEM = pl.BlockSpec(memory_space=pltpu.SMEM)


def params(limit=24):
    return pltpu.CompilerParams(vmem_limit_bytes=limit * 1024 * 1024)


def pin(value):
    return pltpu.with_memory_space_constraint(value, pltpu.VMEM)


def rows_of(count):
    return jax.ShapeDtypeStruct((count // LANES, LANES), F32)


def diagonal():
    shape = (LANES, LANES)
    return lax.broadcasted_iota(jnp.int32, shape, 0) == lax.broadcasted_iota(jnp.int32, shape, 1)


def to_column(row, mask):
    return jnp.sum(jnp.where(mask, jnp.broadcast_to(row, mask.shape), 0.0), axis=1, keepdims=True)


def to_row(column, mask):
    return jnp.sum(jnp.where(mask, jnp.broadcast_to(column, mask.shape), 0.0), axis=0, keepdims=True)


def unfold(value):
    return jnp.concatenate([value[i : i + 1, :] for i in range(value.shape[0])], axis=1)


def fold_into(ref, value):
    for row in range(ref.shape[0]):
        ref[row : row + 1, :] = value[:, row * LANES : (row + 1) * LANES]


def tree(values, join):
    while len(values) > 1:
        values = [join(values[i], values[i + 1]) for i in range(0, len(values), 2)]
    return values[0]


def log_sum(values):
    peak = tree(values, jnp.maximum)
    return peak + jnp.log2(tree([jnp.exp2(value - peak) for value in values], jnp.add))


def product(rows, cols):
    return lax.dot_general(rows, cols, (((1,), (1,)), ((), ())), preferred_element_type=F32)


def ready(sources, targets, mass, source_mass):
    part, chunk = targets.shape[0], mass.shape[0]
    anywhere = pl.BlockSpec(memory_space=pl.ANY)

    def kernel(sources_ref, targets_ref, mass_ref, source_ref, sources_out, packed_ref, mass_out, source_out, *sems):
        copies = [
            pltpu.make_async_copy(mass_ref, mass_out, sems[0]),
            pltpu.make_async_copy(targets_ref, packed_ref.at[:part], sems[1]),
            pltpu.make_async_copy(sources_ref, sources_out, sems[2]),
        ]
        for copy in copies:
            copy.start()
        source_out[...] = jnp.log2(source_ref[...])
        copies[0].wait()
        value, pieces = mass_out[...], []
        for step in range(PIECES):
            pieces.append(value.astype(jnp.bfloat16).astype(F32))
            value = value - pieces[-1]
        pieces.append(jnp.zeros_like(value))
        packed_ref[part:, :] = jnp.concatenate(pieces, axis=0).astype(jnp.bfloat16)
        copies[1].wait()
        copies[2].wait()

    return pl.pallas_call(
        kernel,
        out_shape=(
            pltpu.VMEM(sources.shape, jnp.bfloat16),
            pltpu.VMEM((part + (PIECES + 1) * chunk, LANES), jnp.bfloat16),
            pltpu.VMEM(mass.shape, F32),
            pltpu.VMEM(source_mass.shape, F32),
        ),
        in_specs=[anywhere, anywhere, anywhere, VMEM],
        out_specs=(VMEM,) * 4,
        scratch_shapes=[pltpu.SemaphoreType.DMA] * 3,
        compiler_params=params(),
        cost_estimate=pl.CostEstimate(flops=1 << 20, bytes_accessed=1 << 20, transcendentals=0),
        name="ready",
    )(*[pltpu.with_memory_space_constraint(value, pltpu.HBM) for value in (sources, targets, mass)], source_mass)


def lay(place, block, step, count):
    part = block.shape[0]

    def kernel(place_ref, block_ref, out_ref):
        start = pl.multiple_of(jnp.bitwise_xor(place_ref[0], step) * part, part)
        out_ref[pl.ds(start, part), :] = block_ref[...]

    return pl.pallas_call(
        kernel,
        out_shape=pltpu.VMEM((count * part, LANES), jnp.bfloat16),
        in_specs=[SMEM, VMEM],
        out_specs=VMEM,
        compiler_params=params(),
        cost_estimate=pl.CostEstimate(flops=1 << 20, bytes_accessed=1 << 20, transcendentals=0),
        name="lay",
    )(place, block)


def pack(place, blocks, laid):
    part = blocks[0].shape[0]

    def kernel(place_ref, *refs):
        out_ref = refs[-1]
        for step in range(len(blocks)):
            start = pl.multiple_of(jnp.bitwise_xor(place_ref[0], step) * part, part)
            out_ref[pl.ds(start, part), :] = refs[step][...]

    return pl.pallas_call(
        kernel,
        out_shape=pltpu.VMEM(laid.shape, jnp.bfloat16),
        in_specs=[SMEM] + [VMEM] * (len(blocks) + 1),
        out_specs=VMEM,
        input_output_aliases={1 + len(blocks): 0},
        compiler_params=params(),
        cost_estimate=pl.CostEstimate(flops=1 << 20, bytes_accessed=1 << 18, transcendentals=0),
        name="pack",
    )(place, *blocks, laid)


def pieces_of(value):
    lane = lax.broadcasted_iota(jnp.int32, (value.shape[0], LANES), 1)
    tile = jnp.zeros((value.shape[0], LANES), F32)
    for step in range(PIECES):
        piece = value.astype(jnp.bfloat16).astype(F32)
        tile = jnp.where(lane == step, piece, tile)
        value = value - piece
    return tile.astype(jnp.bfloat16)


def ones_for(rows):
    lane = lax.broadcasted_iota(jnp.int32, (rows, LANES), 1)
    return jnp.where(lane < PIECES, 1.0, 0.0).astype(jnp.bfloat16)


class Rows:
    def __init__(self, count, carry=None):
        empty = (jnp.full((8, count), -1e30, F32), jnp.zeros((8, count), F32))
        self.peak, self.total = empty if carry is None else carry

    def add(self, scores_ref):
        tops = self.peak
        for row in range(0, ROWS, 8):
            tops = jnp.maximum(tops, scores_ref[row : row + 8, :])
        self.total = self.total * jnp.exp2((self.peak - tops) * SCALE)
        self.peak = tops
        for row in range(0, ROWS, 8):
            self.total = self.total + jnp.exp2((scores_ref[row : row + 8, :] - tops) * SCALE)

    def lse(self):
        widest = jnp.max(self.peak, axis=0, keepdims=True)
        total = jnp.sum(self.total * jnp.exp2((self.peak - widest) * SCALE), axis=0, keepdims=True)
        return widest * SCALE + jnp.log2(total)


def first_rows(place, mass, packed, blocks, sources):
    count, chunk = sources.shape[0], mass.shape[0]
    n_src = len(blocks) // CORES + 1
    part = blocks[0].shape[0]
    width = CORES * n_src * part

    def kernel(place_ref, mass_ref, sources_ref, *refs):
        own_ref, other_ref, block_refs = refs[0], refs[1], refs[2 : 2 + len(blocks)]
        targets_ref, offset_ref, full_ref, out_ref, *score_refs = refs[2 + len(blocks) :]
        src, core = place_ref[0], place_ref[1]
        full_ref[pl.ds(pl.multiple_of(core * chunk, chunk), chunk), :] = mass_ref[...]
        parts = [other_ref[part + i * chunk : part + (i + 1) * chunk, :].astype(F32) for i in range(PIECES)]
        start = pl.multiple_of(jnp.bitwise_xor(core, 1) * chunk, chunk)
        full_ref[pl.ds(start, chunk), :] = parts[0] + (parts[1] + parts[2])
        for dc in range(CORES):
            for ds in range(n_src):
                index = jnp.bitwise_xor(core, dc) * n_src + jnp.bitwise_xor(src, ds)
                start = pl.multiple_of(index * part, part)
                ref = refs[dc] if ds == 0 else block_refs[dc * (n_src - 1) + ds - 1]
                targets_ref[pl.ds(start, part), :] = ref[:part, :]
        mask = diagonal()
        log_mass = jnp.log2(full_ref[...]) * (1.0 / SCALE)
        cols = jnp.concatenate([sources_ref[...], ones_for(count)], axis=1)
        rows = Rows(count)
        for at in range(0, width, ROWS):
            scores_ref = score_refs[at // ROWS % len(score_refs)]
            for row in range(at, at + ROWS, LANES):
                values = targets_ref[row : row + LANES, :].astype(F32)
                half = 0.5 * jnp.sum(values * values, axis=1, keepdims=True)
                block = row // LANES
                offset_ref[row : row + LANES, :] = pieces_of(to_column(log_mass[block : block + 1, :], mask) - half)
            scores_ref[...] = product(jnp.concatenate([targets_ref[at : at + ROWS, :], offset_ref[at : at + ROWS, :]], axis=1), cols)
            rows.add(scores_ref)
        fold_into(out_ref, rows.lse())

    return pl.pallas_call(
        kernel,
        out_shape=(
            pltpu.VMEM((width, LANES), jnp.bfloat16),
            pltpu.VMEM((width, LANES), jnp.bfloat16),
            rows_of(width),
            rows_of(count),
        ),
        in_specs=[SMEM] + [VMEM] * (4 + len(blocks)),
        out_specs=(VMEM,) * 4,
        scratch_shapes=[pltpu.VMEM((ROWS, count), F32)] * 2,
        compiler_params=params(),
        cost_estimate=pl.CostEstimate(flops=1 << 29, bytes_accessed=1 << 20, transcendentals=1 << 20),
        name="first_rows",
    )(place, mass, pin(sources), *[pin(value) for value in packed], *[pin(value) for value in blocks])


def other_rows(place, targets, offsets, first, groups):
    mine, groups = groups[0], groups[1:]
    width, count, each = targets.shape[0], sum(group.shape[0] for group in groups), mine.shape[0] // LANES

    def kernel(place_ref, targets_ref, offset_ref, first_ref, mine_ref, *refs):
        group_refs, (out_ref, sources_ref, *score_refs) = refs[: len(groups)], refs[len(groups) :]
        cols = jnp.concatenate([ref[...] for ref in group_refs], axis=0)
        cols = jnp.concatenate([cols, ones_for(count)], axis=1)

        def turn(index, carry):
            rows = Rows(count, carry)
            for at in range(0, width // TURNS, ROWS):
                scores_ref = score_refs[at // ROWS % len(score_refs)]
                span = pl.ds(pl.multiple_of(index * (width // TURNS) + at, ROWS), ROWS)
                scores_ref[...] = product(jnp.concatenate([targets_ref[span, :], offset_ref[span, :]], axis=1), cols)
                rows.add(scores_ref)
            return rows.peak, rows.total

        rows = Rows(count)
        lse = Rows(count, lax.fori_loop(0, TURNS, turn, (rows.peak, rows.total))).lse()
        for step in range(len(groups) + 1):
            start = jnp.bitwise_xor(place_ref[2], step) * each
            ref = group_refs[step - 1] if step else mine_ref
            sources_ref[pl.ds(pl.multiple_of(start * LANES, each * LANES), each * LANES), :] = ref[...]
            for row in range(each):
                at = ((step - 1) * each + row) * LANES
                out_ref[pl.ds(start + row, 1), :] = first_ref[row : row + 1, :] if step == 0 else lse[:, at : at + LANES]

    return pl.pallas_call(
        kernel,
        out_shape=(rows_of(count + each * LANES), pltpu.VMEM((count + each * LANES, LANES), jnp.bfloat16)),
        in_specs=[SMEM] + [VMEM] * (3 + len(groups) + 1),
        out_specs=(VMEM,) * 2,
        scratch_shapes=[pltpu.VMEM((ROWS, count), F32)] * 2,
        compiler_params=params(),
        name="other_rows",
    )(place, pin(targets), pin(offsets), first, pin(mine), *groups)


def first_columns(sources, targets, parts, log_mass):
    count, width = sources.shape[0], targets.shape[0]

    def kernel(sources_ref, targets_ref, parts_ref, log_ref, plan_ref, peak_ref, out_ref, lse_ref, *score_refs):
        lse = log_sum([parts_ref[i] for i in range(parts.shape[0])])
        lse_ref[...] = lse
        mask = diagonal()
        shift = (log_ref[...] - lse) * (1.0 / SCALE)
        shift = [pieces_of(to_column(shift[i : i + 1, :], mask)) for i in range(count // LANES)]
        cols = jnp.concatenate([sources_ref[...], jnp.concatenate(shift, axis=0)], axis=1)
        ones = ones_for(ROWS)

        def turn(index, unused):
            base = index * (width // TURNS)
            for at in range(0, width // TURNS, ROWS):
                scores_ref = score_refs[at // ROWS % len(score_refs)]
                span = pl.ds(pl.multiple_of(base + at, ROWS), ROWS)
                scores_ref[...] = product(jnp.concatenate([targets_ref[span, :], ones], axis=1), cols)
                for block in range(0, ROWS, LANES):
                    peaks, totals = [], []
                    for row in range(block, block + LANES, 8):
                        scores = scores_ref[row : row + 8, :]
                        pieces = [scores[:, lane : lane + LANES] for lane in range(0, count, LANES)]
                        peak = tree(pieces, jnp.maximum)
                        pieces = [jnp.exp2((piece - peak) * SCALE) for piece in pieces]
                        plan_ref[pl.ds(pl.multiple_of(base + at + row, 8), 8), :] = jnp.concatenate(pieces, axis=1)
                        peaks.append(peak * SCALE)
                        totals.append(tree(pieces, jnp.add))
                    peak = jnp.concatenate(peaks, axis=0)
                    peak_ref[pl.ds(pl.multiple_of(base + at + block, LANES), LANES), :] = peak
                    peak, total = peak.T, jnp.concatenate(totals, axis=0).T
                    top = jnp.max(peak, axis=0, keepdims=True)
                    total = jnp.sum(total * jnp.exp2(peak - top), axis=0, keepdims=True)
                    out_ref[pl.ds((base + at + block) // LANES, 1), :] = top + jnp.log2(total)
            return unused

        lax.fori_loop(0, TURNS, turn, 0)

    return pl.pallas_call(
        kernel,
        out_shape=(
            pltpu.VMEM((width, count), F32),
            pltpu.VMEM((width, LANES), F32),
            rows_of(width),
            rows_of(count),
        ),
        in_specs=[VMEM] * 4,
        out_specs=(VMEM,) * 4,
        scratch_shapes=[pltpu.VMEM((ROWS, count), F32)] * 2,
        compiler_params=params(),
        name="first_columns",
    )(pin(sources), pin(targets), parts, log_mass)


def weighted_rows(reach_of, weight_ref, plan_ref, out_ref):
    width, count = plan_ref.shape
    mask = diagonal()

    def turn(index, total):
        base = index * (width // TURNS)
        for step in range(0, width // TURNS, LANES):
            at, block = pl.multiple_of(base + step, LANES), pl.ds((base + step) // LANES, 1)
            reach = reach_of(at, block, mask) * to_column(weight_ref[block, :], mask)
            for row in range(0, LANES, 8):
                factor = jnp.concatenate([reach[row : row + 8, :]] * (count // LANES), axis=1)
                total = total + plan_ref[pl.ds(pl.multiple_of(at + row, 8), 8), :] * factor
        return total

    total = lax.fori_loop(0, TURNS, turn, jnp.zeros((8, count), F32))
    fold_into(out_ref, jnp.sum(total, axis=0, keepdims=True))


def second_rows(plan, peak, mass, parts):
    width, count = plan.shape

    def kernel(plan_ref, peak_ref, mass_ref, *refs):
        part_refs, (lse_ref, reach_ref, out_ref) = refs[:-3], refs[-3:]
        lse_ref[...] = log_sum([ref[...] for ref in part_refs])

        def reach_of(at, block, mask):
            reach = jnp.exp2(peak_ref[pl.ds(at, LANES), :] - to_column(lse_ref[block, :], mask))
            reach_ref[pl.ds(at, LANES), :] = reach
            return reach

        weighted_rows(reach_of, mass_ref, plan_ref, out_ref)

    return pl.pallas_call(
        kernel,
        out_shape=(rows_of(width), pltpu.VMEM((width, LANES), F32), rows_of(count)),
        in_specs=[VMEM] * (3 + len(parts)),
        out_specs=(VMEM,) * 3,
        compiler_params=params(),
        name="second_rows",
    )(pin(plan), pin(peak), mass, *parts)


def later_rows(plan, reach, mass, parts):
    width, count = plan.shape

    def kernel(plan_ref, reach_ref, mass_ref, *refs):
        part_refs, (out_ref, weight_ref) = refs[:-2], refs[-2:]
        weight_ref[...] = mass_ref[...] / tree([ref[...] for ref in part_refs], jnp.add)
        weighted_rows(lambda at, block, mask: reach_ref[pl.ds(at, LANES), :], weight_ref, plan_ref, out_ref)

    return pl.pallas_call(
        kernel,
        out_shape=rows_of(count),
        in_specs=[VMEM] * (3 + len(parts)),
        out_specs=VMEM,
        scratch_shapes=[pltpu.VMEM((width // LANES, LANES), F32)],
        compiler_params=params(),
        name="later_rows",
    )(pin(plan), pin(reach), mass, *parts)


def later_columns(plan, reach, parts, log_mass, lse, half):
    width, count = plan.shape

    def kernel(plan_ref, reach_ref, parts_ref, log_ref, lse_ref, half_ref, out_ref, potential_ref):
        factor = log_ref[...] - jnp.log2(tree([parts_ref[i] for i in range(parts.shape[0])], jnp.add))
        potential_ref[...] = half_ref[...] + UNIT * (factor - lse_ref[...])
        factor = unfold(jnp.exp2(factor))
        factors = [factor[:, lane : lane + LANES] for lane in range(0, count, LANES)]

        def turn(index, unused):
            for step in range(0, width // TURNS, LANES):
                at = pl.multiple_of(index * (width // TURNS) + step, LANES)
                totals = []
                for row in range(0, LANES, 8):
                    plan = plan_ref[pl.ds(pl.multiple_of(at + row, 8), 8), :]
                    totals.append(tree([plan[:, i * LANES : (i + 1) * LANES] * factors[i] for i in range(count // LANES)], jnp.add))
                total = jnp.concatenate(totals, axis=0) * reach_ref[pl.ds(at, LANES), :]
                out_ref[pl.ds(at // LANES, 1), :] = jnp.sum(total.T, axis=0, keepdims=True)
            return unused

        lax.fori_loop(0, TURNS, turn, 0)

    return pl.pallas_call(
        kernel,
        out_shape=(rows_of(width), rows_of(count)),
        in_specs=[VMEM] * 6,
        out_specs=(VMEM,) * 2,
        compiler_params=params(),
        name="later_columns",
    )(pin(plan), pin(reach), parts, log_mass, lse, half)


def levels_of(size):
    bits = size.bit_length() - 1
    out = []
    while bits > 0:
        take = 2 if bits % 2 == 0 else 1
        bits -= take
        out.append([step << bits for step in range(1, 1 << take)])
    return out


def swap(value, axes, size, distance):
    return lax.ppermute(value, axes, [(i, i ^ distance) for i in range(size)])


def swap_all(value, axes, size):
    values = [value]
    for distances in levels_of(size):
        got = {d: [swap(value, axes, size, d) for value in values] for d in reversed(distances)}
        values = [part for i in range(len(values)) for part in [values[i]] + [got[d][i] for d in distances]]
    return values


def share(value, size):
    copies = jnp.broadcast_to(value[None], (size,) + value.shape)
    return lax.all_to_all(copies, ("z", "x"), 0, 0, tiled=True)


def half_norm(points):
    values = points.astype(F32)
    return 0.5 * jnp.sum(values * values, axis=1)


def make_local(n_src, n_z, n_x):
    near, n_near = ("src", "core"), n_src * CORES
    n_far = n_z * n_x

    def local(source_points, target_points, source_mass, target_mass):
        core, x = lax.axis_index("core"), lax.axis_index("x")
        place = jnp.stack([lax.axis_index("src"), core, x]).astype(jnp.int32)
        along = lax.axis_index("z").astype(jnp.int32).reshape(1)
        part = source_points.shape[0]
        a = source_mass.reshape(n_z, n_x, CORES, part)
        a = lax.dynamic_index_in_dim(a, core, axis=2, keepdims=False).swapaxes(0, 1).reshape(-1, LANES)
        blocks = swap_all(target_points, "src", n_src)[1:]
        three, two, one = [swap(source_points, "z", n_z, d) for d in (3, 2, 1)]
        mine, packed, b, a = ready(source_points, target_points, target_mass.reshape(-1, LANES), a)
        laid = lay(along, three, 3, n_z)
        packed = swap_all(packed, "core", CORES)
        blocks = blocks + [swap(block, "core", CORES, 1) for block in blocks]
        groups = swap_all(pack(along, [mine, one, two], laid), "x", n_x)
        place, a = lax.optimization_barrier((place, a))
        targets, offsets, b, first = first_rows(place, b, packed, blocks, groups[0])
        own, sources = other_rows(place, targets, offsets, first, groups)
        plan, peak, own, row_lse = first_columns(sources, targets, share(own, n_far), a)
        early_x, early_y, own = lax.optimization_barrier((sources, targets, own))
        half_x, half_y = half_norm(early_x).reshape(-1, LANES), half_norm(early_y).reshape(-1, LANES)
        parts = swap_all(own, near, n_near)
        half_x, half_y, *parts = lax.optimization_barrier((half_x, half_y, *parts))
        col_lse, reach, rows = second_rows(plan, peak, b, parts)
        for step in range(1, ITERS):
            if step > 1:
                rows = later_rows(plan, reach, b, parts)
            own, potential = later_columns(plan, reach, share(rows, n_far), a, row_lse, half_x)
            parts = swap_all(own, near, n_near)
        mine, other = swap_all(potential.reshape(n_x, n_z, part), "core", CORES)
        low, high = jnp.where(core == 0, mine, other), jnp.where(core == 0, other, mine)
        source_potential = jnp.stack([low, high], axis=2).swapaxes(0, 1).reshape(-1)
        target_potential = half_y - UNIT * (col_lse + jnp.log2(tree(parts, jnp.add)))
        target_potential = target_potential.reshape(CORES, -1)
        target_potential = lax.dynamic_index_in_dim(target_potential, core, axis=0, keepdims=False)
        return source_potential, target_potential

    return local


def solution(mesh):
    n_src, n_tgt = mesh.shape["src"], mesh.shape["tgt"]
    n_z = 4
    n_x = n_tgt // (n_z * CORES)
    split = Mesh(mesh.devices.reshape(n_src, n_z, n_x, CORES), ("src", "z", "x", "core"))
    tgt = ("z", "x", "core")
    placed = (P(("src", *tgt), None), P((*tgt, "src"), None), P("src"), P(tgt))
    return jax.shard_map(
        make_local(n_src, n_z, n_x),
        mesh=split,
        in_specs=placed,
        out_specs=(P("src"), P(tgt)),
        check_vma=False,
    )
```

```python
import math

import jax
import jax.numpy as jnp
from jax import lax
from jax.experimental import pallas as pl
from jax.experimental.pallas import tpu as pltpu
from jax.sharding import Mesh, PartitionSpec as P

ITERS = 3
EPS = 0.05
SCALE = 1.0 / (EPS * math.log(2.0))
UNIT = EPS * math.log(2.0)
LANES = 128
CORES = 2
PIECES = 3
ROWS = 256
F32 = jnp.float32
VMEM = pl.BlockSpec(memory_space=pltpu.VMEM)
SMEM = pl.BlockSpec(memory_space=pltpu.SMEM)


def params(limit=24):
    return pltpu.CompilerParams(vmem_limit_bytes=limit * 1024 * 1024)


def pin(value):
    return pltpu.with_memory_space_constraint(value, pltpu.VMEM)


def rows_of(count):
    return jax.ShapeDtypeStruct((count // LANES, LANES), F32)


def diagonal():
    shape = (LANES, LANES)
    return lax.broadcasted_iota(jnp.int32, shape, 0) == lax.broadcasted_iota(jnp.int32, shape, 1)


def to_column(row, mask):
    return jnp.sum(jnp.where(mask, jnp.broadcast_to(row, mask.shape), 0.0), axis=1, keepdims=True)


def to_row(column, mask):
    return jnp.sum(jnp.where(mask, jnp.broadcast_to(column, mask.shape), 0.0), axis=0, keepdims=True)


def unfold(value):
    return jnp.concatenate([value[i : i + 1, :] for i in range(value.shape[0])], axis=1)


def fold_into(ref, value):
    for row in range(ref.shape[0]):
        ref[row : row + 1, :] = value[:, row * LANES : (row + 1) * LANES]


def tree(values, join):
    while len(values) > 1:
        values = [join(values[i], values[i + 1]) for i in range(0, len(values), 2)]
    return values[0]


def log_sum(values):
    peak = tree(values, jnp.maximum)
    return peak + jnp.log2(tree([jnp.exp2(value - peak) for value in values], jnp.add))


def product(rows, cols):
    return lax.dot_general(rows, cols, (((1,), (1,)), ((), ())), preferred_element_type=F32)


def ready(sources, targets, mass, source_mass):
    part, chunk = targets.shape[0], mass.shape[0]
    anywhere = pl.BlockSpec(memory_space=pl.ANY)

    def kernel(sources_ref, targets_ref, mass_ref, source_ref, sources_out, packed_ref, mass_out, source_out, *sems):
        copies = [
            pltpu.make_async_copy(mass_ref, mass_out, sems[0]),
            pltpu.make_async_copy(targets_ref, packed_ref.at[:part], sems[1]),
            pltpu.make_async_copy(sources_ref, sources_out, sems[2]),
        ]
        for copy in copies:
            copy.start()
        source_out[...] = jnp.log2(source_ref[...])
        copies[0].wait()
        value, pieces = mass_out[...], []
        for step in range(PIECES):
            pieces.append(value.astype(jnp.bfloat16).astype(F32))
            value = value - pieces[-1]
        pieces.append(jnp.zeros_like(value))
        packed_ref[part:, :] = jnp.concatenate(pieces, axis=0).astype(jnp.bfloat16)
        copies[1].wait()
        copies[2].wait()

    return pl.pallas_call(
        kernel,
        out_shape=(
            pltpu.VMEM(sources.shape, jnp.bfloat16),
            pltpu.VMEM((part + (PIECES + 1) * chunk, LANES), jnp.bfloat16),
            pltpu.VMEM(mass.shape, F32),
            pltpu.VMEM(source_mass.shape, F32),
        ),
        in_specs=[anywhere, anywhere, anywhere, VMEM],
        out_specs=(VMEM,) * 4,
        scratch_shapes=[pltpu.SemaphoreType.DMA] * 3,
        compiler_params=params(),
        cost_estimate=pl.CostEstimate(flops=1 << 20, bytes_accessed=1 << 20, transcendentals=0),
        name="ready",
    )(*[pltpu.with_memory_space_constraint(value, pltpu.HBM) for value in (sources, targets, mass)], source_mass)


def lay(place, block, step, count):
    part = block.shape[0]

    def kernel(place_ref, block_ref, out_ref):
        start = pl.multiple_of(jnp.bitwise_xor(place_ref[0], step) * part, part)
        out_ref[pl.ds(start, part), :] = block_ref[...]

    return pl.pallas_call(
        kernel,
        out_shape=pltpu.VMEM((count * part, LANES), jnp.bfloat16),
        in_specs=[SMEM, VMEM],
        out_specs=VMEM,
        compiler_params=params(),
        cost_estimate=pl.CostEstimate(flops=1 << 20, bytes_accessed=1 << 20, transcendentals=0),
        name="lay",
    )(place, block)


def pack(place, blocks, laid):
    part = blocks[0].shape[0]

    def kernel(place_ref, *refs):
        out_ref = refs[-1]
        for step in range(len(blocks)):
            start = pl.multiple_of(jnp.bitwise_xor(place_ref[0], step) * part, part)
            out_ref[pl.ds(start, part), :] = refs[step][...]

    return pl.pallas_call(
        kernel,
        out_shape=pltpu.VMEM(laid.shape, jnp.bfloat16),
        in_specs=[SMEM] + [VMEM] * (len(blocks) + 1),
        out_specs=VMEM,
        input_output_aliases={1 + len(blocks): 0},
        compiler_params=params(),
        cost_estimate=pl.CostEstimate(flops=1 << 20, bytes_accessed=1 << 18, transcendentals=0),
        name="pack",
    )(place, *blocks, laid)


def pieces_of(value):
    lane = lax.broadcasted_iota(jnp.int32, (value.shape[0], LANES), 1)
    tile = jnp.zeros((value.shape[0], LANES), F32)
    for step in range(PIECES):
        piece = value.astype(jnp.bfloat16).astype(F32)
        tile = jnp.where(lane == step, piece, tile)
        value = value - piece
    return tile.astype(jnp.bfloat16)


def ones_for(rows):
    lane = lax.broadcasted_iota(jnp.int32, (rows, LANES), 1)
    return jnp.where(lane < PIECES, 1.0, 0.0).astype(jnp.bfloat16)


class Rows:
    def __init__(self, count):
        self.peak = jnp.full((8, count), -1e30, F32)
        self.total = jnp.zeros((8, count), F32)

    def add(self, scores_ref):
        tops = self.peak
        for row in range(0, ROWS, 8):
            tops = jnp.maximum(tops, scores_ref[row : row + 8, :])
        self.total = self.total * jnp.exp2((self.peak - tops) * SCALE)
        self.peak = tops
        for row in range(0, ROWS, 8):
            self.total = self.total + jnp.exp2((scores_ref[row : row + 8, :] - tops) * SCALE)

    def lse(self):
        widest = jnp.max(self.peak, axis=0, keepdims=True)
        total = jnp.sum(self.total * jnp.exp2((self.peak - widest) * SCALE), axis=0, keepdims=True)
        return widest * SCALE + jnp.log2(total)


def first_rows(place, mass, packed, blocks, sources):
    count, chunk = sources.shape[0], mass.shape[0]
    n_src = len(blocks) // CORES + 1
    part = blocks[0].shape[0]
    width = CORES * n_src * part

    def kernel(place_ref, mass_ref, sources_ref, *refs):
        own_ref, other_ref, block_refs = refs[0], refs[1], refs[2 : 2 + len(blocks)]
        targets_ref, offset_ref, full_ref, out_ref, *score_refs = refs[2 + len(blocks) :]
        src, core = place_ref[0], place_ref[1]
        full_ref[pl.ds(pl.multiple_of(core * chunk, chunk), chunk), :] = jnp.log2(mass_ref[...])
        parts = [other_ref[part + i * chunk : part + (i + 1) * chunk, :].astype(F32) for i in range(PIECES)]
        start = pl.multiple_of(jnp.bitwise_xor(core, 1) * chunk, chunk)
        full_ref[pl.ds(start, chunk), :] = jnp.log2(parts[0] + (parts[1] + parts[2]))
        for dc in range(CORES):
            for ds in range(n_src):
                index = jnp.bitwise_xor(core, dc) * n_src + jnp.bitwise_xor(src, ds)
                start = pl.multiple_of(index * part, part)
                ref = refs[dc] if ds == 0 else block_refs[dc * (n_src - 1) + ds - 1]
                targets_ref[pl.ds(start, part), :] = ref[:part, :]
        mask = diagonal()
        log_mass = full_ref[...] * (1.0 / SCALE)
        cols = jnp.concatenate([sources_ref[...], ones_for(count)], axis=1)
        rows = Rows(count)
        for at in range(0, width, ROWS):
            scores_ref = score_refs[at // ROWS % len(score_refs)]
            for row in range(at, at + ROWS, LANES):
                values = targets_ref[row : row + LANES, :].astype(F32)
                half = 0.5 * jnp.sum(values * values, axis=1, keepdims=True)
                block = row // LANES
                offset_ref[row : row + LANES, :] = pieces_of(to_column(log_mass[block : block + 1, :], mask) - half)
            scores_ref[...] = product(jnp.concatenate([targets_ref[at : at + ROWS, :], offset_ref[at : at + ROWS, :]], axis=1), cols)
            rows.add(scores_ref)
        fold_into(out_ref, rows.lse())

    return pl.pallas_call(
        kernel,
        out_shape=(
            pltpu.VMEM((width, LANES), jnp.bfloat16),
            pltpu.VMEM((width, LANES), jnp.bfloat16),
            rows_of(width),
            rows_of(count),
        ),
        in_specs=[SMEM] + [VMEM] * (4 + len(blocks)),
        out_specs=(VMEM,) * 4,
        scratch_shapes=[pltpu.VMEM((ROWS, count), F32)] * 2,
        compiler_params=params(),
        cost_estimate=pl.CostEstimate(flops=1 << 29, bytes_accessed=1 << 20, transcendentals=1 << 20),
        name="first_rows",
    )(place, mass, pin(sources), *[pin(value) for value in packed], *[pin(value) for value in blocks])


def other_rows(place, targets, offsets, first, groups):
    mine, groups = groups[0], groups[1:]
    width, count, each = targets.shape[0], sum(group.shape[0] for group in groups), mine.shape[0] // LANES

    def kernel(place_ref, targets_ref, offset_ref, first_ref, mine_ref, *refs):
        group_refs, (out_ref, sources_ref, *score_refs) = refs[: len(groups)], refs[len(groups) :]
        cols = jnp.concatenate([ref[...] for ref in group_refs], axis=0)
        cols = jnp.concatenate([cols, ones_for(count)], axis=1)
        rows = Rows(count)
        for at in range(0, width, ROWS):
            scores_ref = score_refs[at // ROWS % len(score_refs)]
            scores_ref[...] = product(jnp.concatenate([targets_ref[at : at + ROWS, :], offset_ref[at : at + ROWS, :]], axis=1), cols)
            rows.add(scores_ref)
        lse = rows.lse()
        for step in range(len(groups) + 1):
            start = jnp.bitwise_xor(place_ref[2], step) * each
            ref = group_refs[step - 1] if step else mine_ref
            sources_ref[pl.ds(pl.multiple_of(start * LANES, each * LANES), each * LANES), :] = ref[...]
            for row in range(each):
                at = ((step - 1) * each + row) * LANES
                out_ref[pl.ds(start + row, 1), :] = first_ref[row : row + 1, :] if step == 0 else lse[:, at : at + LANES]

    return pl.pallas_call(
        kernel,
        out_shape=(rows_of(count + each * LANES), pltpu.VMEM((count + each * LANES, LANES), jnp.bfloat16)),
        in_specs=[SMEM] + [VMEM] * (3 + len(groups) + 1),
        out_specs=(VMEM,) * 2,
        scratch_shapes=[pltpu.VMEM((ROWS, count), F32)] * 2,
        compiler_params=params(),
        name="other_rows",
    )(place, pin(targets), pin(offsets), first, pin(mine), *groups)


def first_columns(sources, targets, parts, log_mass):
    count, width = sources.shape[0], targets.shape[0]

    def kernel(sources_ref, targets_ref, parts_ref, log_ref, plan_ref, reach_ref, top_ref, out_ref, lse_ref, *score_refs):
        lse = log_sum([parts_ref[i] for i in range(parts.shape[0])])
        lse_ref[...] = lse
        out_ref[width // LANES :, :] = jnp.zeros_like(lse)
        mask = diagonal()
        shift = (log_ref[...] - lse) * (1.0 / SCALE)
        shift = [pieces_of(to_column(shift[i : i + 1, :], mask)) for i in range(count // LANES)]
        cols = jnp.concatenate([sources_ref[...], jnp.concatenate(shift, axis=0)], axis=1)
        ones = ones_for(ROWS)
        for at in range(0, width, ROWS):
            scores_ref = score_refs[at // ROWS % len(score_refs)]
            scores_ref[...] = product(jnp.concatenate([targets_ref[at : at + ROWS, :], ones], axis=1), cols)
            for block in range(0, ROWS, LANES):
                peaks, totals = [], []
                for row in range(block, block + LANES, 8):
                    scores = scores_ref[row : row + 8, :]
                    pieces = [scores[:, lane : lane + LANES] for lane in range(0, count, LANES)]
                    peak = tree(pieces, jnp.maximum)
                    pieces = [jnp.exp2((piece - peak) * SCALE) for piece in pieces]
                    plan_ref[at + row : at + row + 8, :] = jnp.concatenate(pieces, axis=1)
                    peaks.append(peak * SCALE)
                    totals.append(tree(pieces, jnp.add))
                peak = jnp.concatenate(peaks, axis=0)
                top = jnp.max(peak, axis=1, keepdims=True)
                reach = jnp.exp2(peak - top)
                reach_ref[at + block : at + block + LANES, :] = reach
                total = jnp.sum((jnp.concatenate(totals, axis=0) * reach).T, axis=0, keepdims=True)
                index = (at + block) // LANES
                top_ref[index : index + 1, :] = to_row(top, mask)
                out_ref[index : index + 1, :] = top_ref[index : index + 1, :] + jnp.log2(total)

    return pl.pallas_call(
        kernel,
        out_shape=(
            pltpu.VMEM((width, count), F32),
            pltpu.VMEM((width, LANES), F32),
            rows_of(width),
            rows_of(width + count),
            rows_of(count),
        ),
        in_specs=[VMEM] * 4,
        out_specs=(VMEM,) * 5,
        scratch_shapes=[pltpu.VMEM((ROWS, count), F32)] * 2,
        compiler_params=params(),
        name="first_columns",
    )(pin(sources), pin(targets), parts, log_mass)


def later_rows(plan, reach, top, log_mass, parts):
    width, count = plan.shape
    rows = width // LANES

    def kernel(plan_ref, reach_ref, top_ref, log_ref, *refs):
        part_refs, out_ref = refs[:-1], refs[-1]
        weight = jnp.exp2(log_ref[...] + (top_ref[...] - log_sum([ref[:rows, :] for ref in part_refs])))
        mask = diagonal()
        total = jnp.zeros((8, count), F32)
        for block in range(rows):
            at = block * LANES
            factors = reach_ref[at : at + LANES, :] * to_column(weight[block : block + 1, :], mask)
            for row in range(0, LANES, 8):
                factor = jnp.concatenate([factors[row : row + 8, :]] * (count // LANES), axis=1)
                total = total + plan_ref[at + row : at + row + 8, :] * factor
        fold_into(out_ref, jnp.sum(total, axis=0, keepdims=True))

    return pl.pallas_call(
        kernel,
        out_shape=rows_of(count),
        in_specs=[VMEM] * (4 + len(parts)),
        out_specs=VMEM,
        compiler_params=params(),
        name="later_rows",
    )(pin(plan), pin(reach), top, log_mass, *parts)


def later_columns(plan, reach, top, parts, log_mass, lse, half):
    width, count = plan.shape

    def kernel(plan_ref, reach_ref, top_ref, parts_ref, log_ref, lse_ref, half_ref, out_ref):
        factor = log_ref[...] - jnp.log2(tree([parts_ref[i] for i in range(parts.shape[0])], jnp.add))
        out_ref[width // LANES :, :] = half_ref[...] + UNIT * (factor - lse_ref[...])
        factor = unfold(jnp.exp2(factor))
        factors = [factor[:, lane : lane + LANES] for lane in range(0, count, LANES)]
        for at in range(0, width, LANES):
            totals = []
            for row in range(at, at + LANES, 8):
                plan = plan_ref[row : row + 8, :]
                totals.append(tree([plan[:, i * LANES : (i + 1) * LANES] * factors[i] for i in range(count // LANES)], jnp.add))
            total = jnp.concatenate(totals, axis=0) * reach_ref[at : at + LANES, :]
            index = at // LANES
            total = jnp.log2(jnp.sum(total.T, axis=0, keepdims=True))
            out_ref[index : index + 1, :] = top_ref[index : index + 1, :] + total

    return pl.pallas_call(
        kernel,
        out_shape=rows_of(width + count),
        in_specs=[VMEM] * 7,
        out_specs=VMEM,
        compiler_params=params(),
        name="later_columns",
    )(pin(plan), pin(reach), top, parts, log_mass, lse, half)


def levels_of(size):
    bits = size.bit_length() - 1
    out = []
    while bits > 0:
        take = 2 if bits % 2 == 0 else 1
        bits -= take
        out.append([step << bits for step in range(1, 1 << take)])
    return out


def swap(value, axes, size, distance):
    return lax.ppermute(value, axes, [(i, i ^ distance) for i in range(size)])


def swap_all(value, axes, size):
    values = [value]
    for distances in levels_of(size):
        got = {d: [swap(value, axes, size, d) for value in values] for d in reversed(distances)}
        values = [part for i in range(len(values)) for part in [values[i]] + [got[d][i] for d in distances]]
    return values


def share(value, size):
    copies = jnp.broadcast_to(value[None], (size,) + value.shape)
    return lax.all_to_all(copies, ("z", "x"), 0, 0, tiled=True)


def half_norm(points):
    values = points.astype(F32)
    return 0.5 * jnp.sum(values * values, axis=1)


def make_local(n_src, n_z, n_x):
    near, n_near = ("src", "core"), n_src * CORES
    n_far = n_z * n_x

    def local(source_points, target_points, source_mass, target_mass):
        core, x = lax.axis_index("core"), lax.axis_index("x")
        place = jnp.stack([lax.axis_index("src"), core, x]).astype(jnp.int32)
        along = lax.axis_index("z").astype(jnp.int32).reshape(1)
        part = source_points.shape[0]
        a = source_mass.reshape(n_z, n_x, CORES, part)
        a = lax.dynamic_index_in_dim(a, core, axis=2, keepdims=False).swapaxes(0, 1).reshape(-1, LANES)
        blocks = swap_all(target_points, "src", n_src)[1:]
        three, two, one = [swap(source_points, "z", n_z, d) for d in (3, 2, 1)]
        mine, packed, b, a = ready(source_points, target_points, target_mass.reshape(-1, LANES), a)
        laid = lay(along, three, 3, n_z)
        packed = swap_all(packed, "core", CORES)
        blocks = blocks + [swap(block, "core", CORES, 1) for block in blocks]
        groups = swap_all(pack(along, [mine, one, two], laid), "x", n_x)
        place, a = lax.optimization_barrier((place, a))
        targets, offsets, b, first = first_rows(place, b, packed, blocks, groups[0])
        own, sources = other_rows(place, targets, offsets, first, groups)
        plan, reach, top, own, row_lse = first_columns(sources, targets, share(own, n_far), a)
        early_x, early_y, own = lax.optimization_barrier((sources, targets, own))
        half_x, half_y = half_norm(early_x).reshape(-1, LANES), half_norm(early_y).reshape(-1, LANES)
        parts = swap_all(own, near, n_near)
        half_x, half_y, *parts = lax.optimization_barrier((half_x, half_y, *parts))
        for step in range(1, ITERS):
            rows = later_rows(plan, reach, top, b, parts)
            own = later_columns(plan, reach, top, share(rows, n_far), a, row_lse, half_x)
            parts = swap_all(own, near, n_near)
        rows = half_y.shape[0]
        mine, other = [value[rows:].reshape(n_x, n_z, part) for value in parts[:CORES]]
        first, second = jnp.where(core == 0, mine, other), jnp.where(core == 0, other, mine)
        source_potential = jnp.stack([first, second], axis=2).swapaxes(0, 1).reshape(-1)
        target_potential = half_y - UNIT * log_sum([value[:rows] for value in parts])
        target_potential = target_potential.reshape(CORES, -1)
        target_potential = lax.dynamic_index_in_dim(target_potential, core, axis=0, keepdims=False)
        return source_potential, target_potential

    return local


def solution(mesh):
    n_src, n_tgt = mesh.shape["src"], mesh.shape["tgt"]
    n_z = 4
    n_x = n_tgt // (n_z * CORES)
    split = Mesh(mesh.devices.reshape(n_src, n_z, n_x, CORES), ("src", "z", "x", "core"))
    tgt = ("z", "x", "core")
    placed = (P(("src", *tgt), None), P((*tgt, "src"), None), P("src"), P(tgt))
    return jax.shard_map(
        make_local(n_src, n_z, n_x),
        mesh=split,
        in_specs=placed,
        out_specs=(P("src"), P(tgt)),
        check_vma=False,
    )
```

```python
import math

import jax
import jax.numpy as jnp
from jax import lax
from jax.experimental import pallas as pl
from jax.experimental.pallas import tpu as pltpu
from jax.sharding import Mesh, PartitionSpec as P

ITERS = 3
EPS = 0.05
SCALE = 1.0 / (EPS * math.log(2.0))
UNIT = EPS * math.log(2.0)
LANES = 128
CORES = 2
PIECES = 3
ROWS = 256
F32 = jnp.float32
VMEM = pl.BlockSpec(memory_space=pltpu.VMEM)
SMEM = pl.BlockSpec(memory_space=pltpu.SMEM)


def params(limit=24):
    return pltpu.CompilerParams(vmem_limit_bytes=limit * 1024 * 1024)


def pin(value):
    return pltpu.with_memory_space_constraint(value, pltpu.VMEM)


def rows_of(count):
    return jax.ShapeDtypeStruct((count // LANES, LANES), F32)


def diagonal():
    shape = (LANES, LANES)
    return lax.broadcasted_iota(jnp.int32, shape, 0) == lax.broadcasted_iota(jnp.int32, shape, 1)


def to_column(row, mask):
    return jnp.sum(jnp.where(mask, jnp.broadcast_to(row, mask.shape), 0.0), axis=1, keepdims=True)


def to_row(column, mask):
    return jnp.sum(jnp.where(mask, jnp.broadcast_to(column, mask.shape), 0.0), axis=0, keepdims=True)


def unfold(value):
    return jnp.concatenate([value[i : i + 1, :] for i in range(value.shape[0])], axis=1)


def fold_into(ref, value):
    for row in range(ref.shape[0]):
        ref[row : row + 1, :] = value[:, row * LANES : (row + 1) * LANES]


def tree(values, join):
    while len(values) > 1:
        values = [join(values[i], values[i + 1]) for i in range(0, len(values), 2)]
    return values[0]


def log_sum(values):
    peak = tree(values, jnp.maximum)
    return peak + jnp.log2(tree([jnp.exp2(value - peak) for value in values], jnp.add))


def product(rows, cols):
    return lax.dot_general(rows, cols, (((1,), (1,)), ((), ())), preferred_element_type=F32)


def ready(sources, targets, mass, source_mass):
    part, chunk = targets.shape[0], mass.shape[0]
    anywhere = pl.BlockSpec(memory_space=pl.ANY)

    def kernel(sources_ref, targets_ref, mass_ref, source_ref, sources_out, packed_ref, mass_out, source_out, *sems):
        copies = [
            pltpu.make_async_copy(mass_ref, mass_out, sems[0]),
            pltpu.make_async_copy(targets_ref, packed_ref.at[:part], sems[1]),
            pltpu.make_async_copy(sources_ref, sources_out, sems[2]),
        ]
        for copy in copies:
            copy.start()
        source_out[...] = jnp.log2(source_ref[...])
        copies[0].wait()
        value, pieces = mass_out[...], []
        for step in range(PIECES):
            pieces.append(value.astype(jnp.bfloat16).astype(F32))
            value = value - pieces[-1]
        pieces.append(jnp.zeros_like(value))
        packed_ref[part:, :] = jnp.concatenate(pieces, axis=0).astype(jnp.bfloat16)
        copies[1].wait()
        copies[2].wait()

    return pl.pallas_call(
        kernel,
        out_shape=(
            pltpu.VMEM(sources.shape, jnp.bfloat16),
            pltpu.VMEM((part + (PIECES + 1) * chunk, LANES), jnp.bfloat16),
            pltpu.VMEM(mass.shape, F32),
            pltpu.VMEM(source_mass.shape, F32),
        ),
        in_specs=[anywhere, anywhere, anywhere, VMEM],
        out_specs=(VMEM,) * 4,
        scratch_shapes=[pltpu.SemaphoreType.DMA] * 3,
        compiler_params=params(),
        cost_estimate=pl.CostEstimate(flops=1 << 20, bytes_accessed=1 << 20, transcendentals=0),
        name="ready",
    )(*[pltpu.with_memory_space_constraint(value, pltpu.HBM) for value in (sources, targets, mass)], source_mass)


def lay(place, block, step, count):
    part = block.shape[0]

    def kernel(place_ref, block_ref, out_ref):
        start = pl.multiple_of(jnp.bitwise_xor(place_ref[0], step) * part, part)
        out_ref[pl.ds(start, part), :] = block_ref[...]

    return pl.pallas_call(
        kernel,
        out_shape=pltpu.VMEM((count * part, LANES), jnp.bfloat16),
        in_specs=[SMEM, VMEM],
        out_specs=VMEM,
        compiler_params=params(),
        cost_estimate=pl.CostEstimate(flops=1 << 20, bytes_accessed=1 << 20, transcendentals=0),
        name="lay",
    )(place, block)


def pack(place, blocks, laid):
    part = blocks[0].shape[0]

    def kernel(place_ref, *refs):
        out_ref = refs[-1]
        for step in range(len(blocks)):
            start = pl.multiple_of(jnp.bitwise_xor(place_ref[0], step) * part, part)
            out_ref[pl.ds(start, part), :] = refs[step][...]

    return pl.pallas_call(
        kernel,
        out_shape=pltpu.VMEM(laid.shape, jnp.bfloat16),
        in_specs=[SMEM] + [VMEM] * (len(blocks) + 1),
        out_specs=VMEM,
        input_output_aliases={1 + len(blocks): 0},
        compiler_params=params(),
        cost_estimate=pl.CostEstimate(flops=1 << 20, bytes_accessed=1 << 18, transcendentals=0),
        name="pack",
    )(place, *blocks, laid)


def pieces_of(value):
    lane = lax.broadcasted_iota(jnp.int32, (value.shape[0], LANES), 1)
    tile = jnp.zeros((value.shape[0], LANES), F32)
    for step in range(PIECES):
        piece = value.astype(jnp.bfloat16).astype(F32)
        tile = jnp.where(lane == step, piece, tile)
        value = value - piece
    return tile.astype(jnp.bfloat16)


def ones_for(rows):
    lane = lax.broadcasted_iota(jnp.int32, (rows, LANES), 1)
    return jnp.where(lane < PIECES, 1.0, 0.0).astype(jnp.bfloat16)


class Rows:
    def __init__(self, count):
        self.peak = jnp.full((8, count), -1e30, F32)
        self.total = jnp.zeros((8, count), F32)

    def add(self, scores_ref):
        tops = self.peak
        for row in range(0, ROWS, 8):
            tops = jnp.maximum(tops, scores_ref[row : row + 8, :])
        self.total = self.total * jnp.exp2((self.peak - tops) * SCALE)
        self.peak = tops
        for row in range(0, ROWS, 8):
            self.total = self.total + jnp.exp2((scores_ref[row : row + 8, :] - tops) * SCALE)

    def lse(self):
        widest = jnp.max(self.peak, axis=0, keepdims=True)
        total = jnp.sum(self.total * jnp.exp2((self.peak - widest) * SCALE), axis=0, keepdims=True)
        return widest * SCALE + jnp.log2(total)


def first_rows(place, mass, packed, blocks, sources):
    count, chunk = sources.shape[0], mass.shape[0]
    n_src = len(blocks) // CORES + 1
    part = blocks[0].shape[0]
    width = CORES * n_src * part

    def kernel(place_ref, mass_ref, sources_ref, *refs):
        own_ref, other_ref, block_refs = refs[0], refs[1], refs[2 : 2 + len(blocks)]
        targets_ref, offset_ref, full_ref, out_ref, *score_refs = refs[2 + len(blocks) :]
        src, core = place_ref[0], place_ref[1]
        full_ref[pl.ds(pl.multiple_of(core * chunk, chunk), chunk), :] = jnp.log2(mass_ref[...])
        parts = [other_ref[part + i * chunk : part + (i + 1) * chunk, :].astype(F32) for i in range(PIECES)]
        start = pl.multiple_of(jnp.bitwise_xor(core, 1) * chunk, chunk)
        full_ref[pl.ds(start, chunk), :] = jnp.log2(parts[0] + (parts[1] + parts[2]))
        for dc in range(CORES):
            for ds in range(n_src):
                index = jnp.bitwise_xor(core, dc) * n_src + jnp.bitwise_xor(src, ds)
                start = pl.multiple_of(index * part, part)
                ref = refs[dc] if ds == 0 else block_refs[dc * (n_src - 1) + ds - 1]
                targets_ref[pl.ds(start, part), :] = ref[:part, :]
        mask = diagonal()
        log_mass = full_ref[...] * (1.0 / SCALE)
        cols = jnp.concatenate([sources_ref[...], ones_for(count)], axis=1)
        rows = Rows(count)
        for at in range(0, width, ROWS):
            scores_ref = score_refs[at // ROWS % len(score_refs)]
            for row in range(at, at + ROWS, LANES):
                values = targets_ref[row : row + LANES, :].astype(F32)
                half = 0.5 * jnp.sum(values * values, axis=1, keepdims=True)
                block = row // LANES
                offset_ref[row : row + LANES, :] = pieces_of(to_column(log_mass[block : block + 1, :], mask) - half)
            scores_ref[...] = product(jnp.concatenate([targets_ref[at : at + ROWS, :], offset_ref[at : at + ROWS, :]], axis=1), cols)
            rows.add(scores_ref)
        fold_into(out_ref, rows.lse())

    return pl.pallas_call(
        kernel,
        out_shape=(
            pltpu.VMEM((width, LANES), jnp.bfloat16),
            pltpu.VMEM((width, LANES), jnp.bfloat16),
            rows_of(width),
            rows_of(count),
        ),
        in_specs=[SMEM] + [VMEM] * (4 + len(blocks)),
        out_specs=(VMEM,) * 4,
        scratch_shapes=[pltpu.VMEM((ROWS, count), F32)] * 2,
        compiler_params=params(),
        cost_estimate=pl.CostEstimate(flops=1 << 29, bytes_accessed=1 << 20, transcendentals=1 << 20),
        name="first_rows",
    )(place, mass, pin(sources), *[pin(value) for value in packed], *[pin(value) for value in blocks])


def other_rows(place, targets, offsets, first, groups):
    mine, groups = groups[0], groups[1:]
    width, count, each = targets.shape[0], sum(group.shape[0] for group in groups), mine.shape[0] // LANES

    def kernel(place_ref, targets_ref, offset_ref, first_ref, mine_ref, *refs):
        group_refs, (out_ref, sources_ref, *score_refs) = refs[: len(groups)], refs[len(groups) :]
        cols = jnp.concatenate([ref[...] for ref in group_refs], axis=0)
        cols = jnp.concatenate([cols, ones_for(count)], axis=1)
        rows = Rows(count)
        for at in range(0, width, ROWS):
            scores_ref = score_refs[at // ROWS % len(score_refs)]
            scores_ref[...] = product(jnp.concatenate([targets_ref[at : at + ROWS, :], offset_ref[at : at + ROWS, :]], axis=1), cols)
            rows.add(scores_ref)
        lse = rows.lse()
        for step in range(len(groups) + 1):
            start = jnp.bitwise_xor(place_ref[2], step) * each
            ref = group_refs[step - 1] if step else mine_ref
            sources_ref[pl.ds(pl.multiple_of(start * LANES, each * LANES), each * LANES), :] = ref[...]
            for row in range(each):
                at = ((step - 1) * each + row) * LANES
                out_ref[pl.ds(start + row, 1), :] = first_ref[row : row + 1, :] if step == 0 else lse[:, at : at + LANES]

    return pl.pallas_call(
        kernel,
        out_shape=(rows_of(count + each * LANES), pltpu.VMEM((count + each * LANES, LANES), jnp.bfloat16)),
        in_specs=[SMEM] + [VMEM] * (3 + len(groups) + 1),
        out_specs=(VMEM,) * 2,
        scratch_shapes=[pltpu.VMEM((ROWS, count), F32)] * 2,
        compiler_params=params(),
        name="other_rows",
    )(place, pin(targets), pin(offsets), first, pin(mine), *groups)


def first_columns(sources, targets, parts, log_mass):
    count, width = sources.shape[0], targets.shape[0]

    def kernel(sources_ref, targets_ref, parts_ref, log_ref, plan_ref, reach_ref, top_ref, out_ref, lse_ref, *score_refs):
        lse = log_sum([parts_ref[i] for i in range(parts.shape[0])])
        lse_ref[...] = lse
        mask = diagonal()
        shift = (log_ref[...] - lse) * (1.0 / SCALE)
        shift = [pieces_of(to_column(shift[i : i + 1, :], mask)) for i in range(count // LANES)]
        cols = jnp.concatenate([sources_ref[...], jnp.concatenate(shift, axis=0)], axis=1)
        ones = ones_for(ROWS)
        for at in range(0, width, ROWS):
            scores_ref = score_refs[at // ROWS % len(score_refs)]
            scores_ref[...] = product(jnp.concatenate([targets_ref[at : at + ROWS, :], ones], axis=1), cols)
            for block in range(0, ROWS, LANES):
                peaks, totals = [], []
                for row in range(block, block + LANES, 8):
                    scores = scores_ref[row : row + 8, :]
                    pieces = [scores[:, lane : lane + LANES] for lane in range(0, count, LANES)]
                    peak = tree(pieces, jnp.maximum)
                    pieces = [jnp.exp2((piece - peak) * SCALE) for piece in pieces]
                    plan_ref[at + row : at + row + 8, :] = jnp.concatenate(pieces, axis=1)
                    peaks.append(peak * SCALE)
                    totals.append(tree(pieces, jnp.add))
                peak = jnp.concatenate(peaks, axis=0)
                top = jnp.max(peak, axis=1, keepdims=True)
                reach = jnp.exp2(peak - top)
                reach_ref[at + block : at + block + LANES, :] = reach
                total = jnp.sum((jnp.concatenate(totals, axis=0) * reach).T, axis=0, keepdims=True)
                index = (at + block) // LANES
                top_ref[index : index + 1, :] = to_row(top, mask)
                out_ref[index : index + 1, :] = top_ref[index : index + 1, :] + jnp.log2(total)

    return pl.pallas_call(
        kernel,
        out_shape=(
            pltpu.VMEM((width, count), F32),
            pltpu.VMEM((width, LANES), F32),
            rows_of(width),
            rows_of(width),
            rows_of(count),
        ),
        in_specs=[VMEM] * 4,
        out_specs=(VMEM,) * 5,
        scratch_shapes=[pltpu.VMEM((ROWS, count), F32)] * 2,
        compiler_params=params(),
        name="first_columns",
    )(pin(sources), pin(targets), parts, log_mass)


def later_rows(plan, reach, top, log_mass, parts):
    width, count = plan.shape
    rows = width // LANES

    def kernel(plan_ref, reach_ref, top_ref, log_ref, *refs):
        part_refs, out_ref = refs[:-1], refs[-1]
        weight = jnp.exp2(log_ref[...] + (top_ref[...] - log_sum([ref[...] for ref in part_refs])))
        mask = diagonal()
        total = jnp.zeros((8, count), F32)
        for block in range(rows):
            at = block * LANES
            factors = reach_ref[at : at + LANES, :] * to_column(weight[block : block + 1, :], mask)
            for row in range(0, LANES, 8):
                factor = jnp.concatenate([factors[row : row + 8, :]] * (count // LANES), axis=1)
                total = total + plan_ref[at + row : at + row + 8, :] * factor
        fold_into(out_ref, jnp.sum(total, axis=0, keepdims=True))

    return pl.pallas_call(
        kernel,
        out_shape=rows_of(count),
        in_specs=[VMEM] * (4 + len(parts)),
        out_specs=VMEM,
        compiler_params=params(),
        name="later_rows",
    )(pin(plan), pin(reach), top, log_mass, *parts)


def later_columns(plan, reach, top, parts, log_mass, lse, half):
    width, count = plan.shape

    def kernel(plan_ref, reach_ref, top_ref, parts_ref, log_ref, lse_ref, half_ref, out_ref, potential_ref):
        factor = log_ref[...] - jnp.log2(tree([parts_ref[i] for i in range(parts.shape[0])], jnp.add))
        potential_ref[...] = half_ref[...] + UNIT * (factor - lse_ref[...])
        factor = unfold(jnp.exp2(factor))
        factors = [factor[:, lane : lane + LANES] for lane in range(0, count, LANES)]
        for at in range(0, width, LANES):
            totals = []
            for row in range(at, at + LANES, 8):
                plan = plan_ref[row : row + 8, :]
                totals.append(tree([plan[:, i * LANES : (i + 1) * LANES] * factors[i] for i in range(count // LANES)], jnp.add))
            total = jnp.concatenate(totals, axis=0) * reach_ref[at : at + LANES, :]
            index = at // LANES
            total = jnp.log2(jnp.sum(total.T, axis=0, keepdims=True))
            out_ref[index : index + 1, :] = top_ref[index : index + 1, :] + total

    return pl.pallas_call(
        kernel,
        out_shape=(rows_of(width), pltpu.VMEM((count // LANES, LANES), F32)),
        in_specs=[VMEM] * 7,
        out_specs=(VMEM,) * 2,
        compiler_params=params(),
        name="later_columns",
    )(pin(plan), pin(reach), top, parts, log_mass, lse, half)


def levels_of(size):
    bits = size.bit_length() - 1
    out = []
    while bits > 0:
        take = 2 if bits % 2 == 0 else 1
        bits -= take
        out.append([step << bits for step in range(1, 1 << take)])
    return out


def swap(value, axes, size, distance):
    return lax.ppermute(value, axes, [(i, i ^ distance) for i in range(size)])


def swap_all(value, axes, size):
    values = [value]
    for distances in levels_of(size):
        got = {d: [swap(value, axes, size, d) for value in values] for d in reversed(distances)}
        values = [part for i in range(len(values)) for part in [values[i]] + [got[d][i] for d in distances]]
    return values


def share(value, size):
    copies = jnp.broadcast_to(value[None], (size,) + value.shape)
    return lax.all_to_all(copies, ("z", "x"), 0, 0, tiled=True)


def half_norm(points):
    values = points.astype(F32)
    return 0.5 * jnp.sum(values * values, axis=1)


def make_local(n_src, n_z, n_x):
    near, n_near = ("src", "core"), n_src * CORES
    n_far = n_z * n_x

    def local(source_points, target_points, source_mass, target_mass):
        core, x = lax.axis_index("core"), lax.axis_index("x")
        place = jnp.stack([lax.axis_index("src"), core, x]).astype(jnp.int32)
        along = lax.axis_index("z").astype(jnp.int32).reshape(1)
        part = source_points.shape[0]
        a = source_mass.reshape(n_z, n_x, CORES, part)
        a = lax.dynamic_index_in_dim(a, core, axis=2, keepdims=False).swapaxes(0, 1).reshape(-1, LANES)
        blocks = swap_all(target_points, "src", n_src)[1:]
        three, two, one = [swap(source_points, "z", n_z, d) for d in (3, 2, 1)]
        mine, packed, b, a = ready(source_points, target_points, target_mass.reshape(-1, LANES), a)
        laid = lay(along, three, 3, n_z)
        packed = swap_all(packed, "core", CORES)
        blocks = blocks + [swap(block, "core", CORES, 1) for block in blocks]
        groups = swap_all(pack(along, [mine, one, two], laid), "x", n_x)
        place, a = lax.optimization_barrier((place, a))
        targets, offsets, b, first = first_rows(place, b, packed, blocks, groups[0])
        own, sources = other_rows(place, targets, offsets, first, groups)
        plan, reach, top, own, row_lse = first_columns(sources, targets, share(own, n_far), a)
        early_x, early_y, own = lax.optimization_barrier((sources, targets, own))
        half_x, half_y = half_norm(early_x).reshape(-1, LANES), half_norm(early_y).reshape(-1, LANES)
        parts = swap_all(own, near, n_near)
        half_x, half_y, *parts = lax.optimization_barrier((half_x, half_y, *parts))
        for step in range(1, ITERS):
            rows = later_rows(plan, reach, top, b, parts)
            own, potential = later_columns(plan, reach, top, share(rows, n_far), a, row_lse, half_x)
            parts = swap_all(own, near, n_near)
        mine, other = swap_all(potential.reshape(n_x, n_z, part), "core", CORES)
        first, second = jnp.where(core == 0, mine, other), jnp.where(core == 0, other, mine)
        source_potential = jnp.stack([first, second], axis=2).swapaxes(0, 1).reshape(-1)
        target_potential = half_y - UNIT * log_sum(parts)
        target_potential = target_potential.reshape(CORES, -1)
        target_potential = lax.dynamic_index_in_dim(target_potential, core, axis=0, keepdims=False)
        return source_potential, target_potential

    return local


def solution(mesh):
    n_src, n_tgt = mesh.shape["src"], mesh.shape["tgt"]
    n_z = 4
    n_x = n_tgt // (n_z * CORES)
    split = Mesh(mesh.devices.reshape(n_src, n_z, n_x, CORES), ("src", "z", "x", "core"))
    tgt = ("z", "x", "core")
    placed = (P(("src", *tgt), None), P((*tgt, "src"), None), P("src"), P(tgt))
    return jax.shard_map(
        make_local(n_src, n_z, n_x),
        mesh=split,
        in_specs=placed,
        out_specs=(P("src"), P(tgt)),
        check_vma=False,
    )
```

```python
import math

import jax
import jax.numpy as jnp
from jax import lax
from jax.experimental import pallas as pl
from jax.experimental.pallas import tpu as pltpu
from jax.sharding import Mesh, PartitionSpec as P

ITERS = 3
EPS = 0.05
SCALE = 1.0 / (EPS * math.log(2.0))
UNIT = EPS * math.log(2.0)
LANES = 128
CORES = 2
PIECES = 3
ROWS = 256
F32 = jnp.float32
VMEM = pl.BlockSpec(memory_space=pltpu.VMEM)
SMEM = pl.BlockSpec(memory_space=pltpu.SMEM)


def params(limit=24):
    return pltpu.CompilerParams(vmem_limit_bytes=limit * 1024 * 1024)


def pin(value):
    return pltpu.with_memory_space_constraint(value, pltpu.VMEM)


def rows_of(count):
    return jax.ShapeDtypeStruct((count // LANES, LANES), F32)


def diagonal():
    shape = (LANES, LANES)
    return lax.broadcasted_iota(jnp.int32, shape, 0) == lax.broadcasted_iota(jnp.int32, shape, 1)


def to_column(row, mask):
    return jnp.sum(jnp.where(mask, jnp.broadcast_to(row, mask.shape), 0.0), axis=1, keepdims=True)


def to_row(column, mask):
    return jnp.sum(jnp.where(mask, jnp.broadcast_to(column, mask.shape), 0.0), axis=0, keepdims=True)


def unfold(value):
    return jnp.concatenate([value[i : i + 1, :] for i in range(value.shape[0])], axis=1)


def fold_into(ref, value):
    for row in range(ref.shape[0]):
        ref[row : row + 1, :] = value[:, row * LANES : (row + 1) * LANES]


def tree(values, join):
    while len(values) > 1:
        values = [join(values[i], values[i + 1]) for i in range(0, len(values), 2)]
    return values[0]


def log_sum(values):
    peak = tree(values, jnp.maximum)
    return peak + jnp.log2(tree([jnp.exp2(value - peak) for value in values], jnp.add))


def product(rows, cols):
    return lax.dot_general(rows, cols, (((1,), (1,)), ((), ())), preferred_element_type=F32)


def ready(sources, targets, mass, source_mass):
    part, chunk = targets.shape[0], mass.shape[0]
    anywhere = pl.BlockSpec(memory_space=pl.ANY)

    def kernel(sources_ref, targets_ref, mass_ref, source_ref, sources_out, packed_ref, mass_out, source_out, *sems):
        copies = [
            pltpu.make_async_copy(mass_ref, mass_out, sems[0]),
            pltpu.make_async_copy(targets_ref, packed_ref.at[:part], sems[1]),
            pltpu.make_async_copy(sources_ref, sources_out, sems[2]),
        ]
        for copy in copies:
            copy.start()
        source_out[...] = jnp.log2(source_ref[...])
        copies[0].wait()
        value, pieces = mass_out[...], []
        for step in range(PIECES):
            pieces.append(value.astype(jnp.bfloat16).astype(F32))
            value = value - pieces[-1]
        pieces.append(jnp.zeros_like(value))
        packed_ref[part:, :] = jnp.concatenate(pieces, axis=0).astype(jnp.bfloat16)
        copies[1].wait()
        copies[2].wait()

    return pl.pallas_call(
        kernel,
        out_shape=(
            pltpu.VMEM(sources.shape, jnp.bfloat16),
            pltpu.VMEM((part + (PIECES + 1) * chunk, LANES), jnp.bfloat16),
            pltpu.VMEM(mass.shape, F32),
            pltpu.VMEM(source_mass.shape, F32),
        ),
        in_specs=[anywhere, anywhere, anywhere, VMEM],
        out_specs=(VMEM,) * 4,
        scratch_shapes=[pltpu.SemaphoreType.DMA] * 3,
        compiler_params=params(),
        cost_estimate=pl.CostEstimate(flops=1 << 20, bytes_accessed=1 << 20, transcendentals=0),
        name="ready",
    )(*[pltpu.with_memory_space_constraint(value, pltpu.HBM) for value in (sources, targets, mass)], source_mass)


def lay(place, block, step, count):
    part = block.shape[0]

    def kernel(place_ref, block_ref, out_ref):
        start = pl.multiple_of(jnp.bitwise_xor(place_ref[0], step) * part, part)
        out_ref[pl.ds(start, part), :] = block_ref[...]

    return pl.pallas_call(
        kernel,
        out_shape=pltpu.VMEM((count * part, LANES), jnp.bfloat16),
        in_specs=[SMEM, VMEM],
        out_specs=VMEM,
        compiler_params=params(),
        cost_estimate=pl.CostEstimate(flops=1 << 20, bytes_accessed=1 << 20, transcendentals=0),
        name="lay",
    )(place, block)


def pack(place, blocks, laid):
    part = blocks[0].shape[0]

    def kernel(place_ref, *refs):
        out_ref = refs[-1]
        for step in range(len(blocks)):
            start = pl.multiple_of(jnp.bitwise_xor(place_ref[0], step) * part, part)
            out_ref[pl.ds(start, part), :] = refs[step][...]

    return pl.pallas_call(
        kernel,
        out_shape=pltpu.VMEM(laid.shape, jnp.bfloat16),
        in_specs=[SMEM] + [VMEM] * (len(blocks) + 1),
        out_specs=VMEM,
        input_output_aliases={1 + len(blocks): 0},
        compiler_params=params(),
        cost_estimate=pl.CostEstimate(flops=1 << 20, bytes_accessed=1 << 18, transcendentals=0),
        name="pack",
    )(place, *blocks, laid)


def pieces_of(value):
    lane = lax.broadcasted_iota(jnp.int32, (value.shape[0], LANES), 1)
    tile = jnp.zeros((value.shape[0], LANES), F32)
    for step in range(PIECES):
        piece = value.astype(jnp.bfloat16).astype(F32)
        tile = jnp.where(lane == step, piece, tile)
        value = value - piece
    return tile.astype(jnp.bfloat16)


def ones_for(rows):
    lane = lax.broadcasted_iota(jnp.int32, (rows, LANES), 1)
    return jnp.where(lane < PIECES, 1.0, 0.0).astype(jnp.bfloat16)


class Rows:
    def __init__(self, count):
        self.peak = jnp.full((8, count), -1e30, F32)
        self.total = jnp.zeros((8, count), F32)

    def add(self, scores_ref):
        tops = self.peak
        for row in range(0, ROWS, 8):
            tops = jnp.maximum(tops, scores_ref[row : row + 8, :])
        self.total = self.total * jnp.exp2((self.peak - tops) * SCALE)
        self.peak = tops
        for row in range(0, ROWS, 8):
            self.total = self.total + jnp.exp2((scores_ref[row : row + 8, :] - tops) * SCALE)

    def lse(self):
        widest = jnp.max(self.peak, axis=0, keepdims=True)
        total = jnp.sum(self.total * jnp.exp2((self.peak - widest) * SCALE), axis=0, keepdims=True)
        return widest * SCALE + jnp.log2(total)


def first_rows(place, mass, packed, blocks, sources):
    count, chunk = sources.shape[0], mass.shape[0]
    n_src = len(blocks) // CORES + 1
    part = blocks[0].shape[0]
    width = CORES * n_src * part

    def kernel(place_ref, mass_ref, sources_ref, *refs):
        own_ref, other_ref, block_refs = refs[0], refs[1], refs[2 : 2 + len(blocks)]
        targets_ref, offset_ref, full_ref, out_ref, *score_refs = refs[2 + len(blocks) :]
        src, core = place_ref[0], place_ref[1]
        full_ref[pl.ds(pl.multiple_of(core * chunk, chunk), chunk), :] = jnp.log2(mass_ref[...])
        parts = [other_ref[part + i * chunk : part + (i + 1) * chunk, :].astype(F32) for i in range(PIECES)]
        start = pl.multiple_of(jnp.bitwise_xor(core, 1) * chunk, chunk)
        full_ref[pl.ds(start, chunk), :] = jnp.log2(parts[0] + (parts[1] + parts[2]))
        for dc in range(CORES):
            for ds in range(n_src):
                index = jnp.bitwise_xor(core, dc) * n_src + jnp.bitwise_xor(src, ds)
                start = pl.multiple_of(index * part, part)
                ref = refs[dc] if ds == 0 else block_refs[dc * (n_src - 1) + ds - 1]
                targets_ref[pl.ds(start, part), :] = ref[:part, :]
        mask = diagonal()
        log_mass = full_ref[...] * (1.0 / SCALE)
        cols = jnp.concatenate([sources_ref[...], ones_for(count)], axis=1)
        rows = Rows(count)
        for at in range(0, width, ROWS):
            scores_ref = score_refs[at // ROWS % len(score_refs)]
            for row in range(at, at + ROWS, LANES):
                values = targets_ref[row : row + LANES, :].astype(F32)
                half = 0.5 * jnp.sum(values * values, axis=1, keepdims=True)
                block = row // LANES
                offset_ref[row : row + LANES, :] = pieces_of(to_column(log_mass[block : block + 1, :], mask) - half)
            scores_ref[...] = product(jnp.concatenate([targets_ref[at : at + ROWS, :], offset_ref[at : at + ROWS, :]], axis=1), cols)
            rows.add(scores_ref)
        fold_into(out_ref, rows.lse())

    return pl.pallas_call(
        kernel,
        out_shape=(
            pltpu.VMEM((width, LANES), jnp.bfloat16),
            pltpu.VMEM((width, LANES), jnp.bfloat16),
            rows_of(width),
            rows_of(count),
        ),
        in_specs=[SMEM] + [VMEM] * (4 + len(blocks)),
        out_specs=(VMEM,) * 4,
        scratch_shapes=[pltpu.VMEM((ROWS, count), F32)] * 2,
        compiler_params=params(),
        cost_estimate=pl.CostEstimate(flops=1 << 29, bytes_accessed=1 << 20, transcendentals=1 << 20),
        name="first_rows",
    )(place, mass, pin(sources), *[pin(value) for value in packed], *[pin(value) for value in blocks])


def other_rows(place, targets, offsets, first, groups):
    mine, groups = groups[0], groups[1:]
    width, count, each = targets.shape[0], sum(group.shape[0] for group in groups), mine.shape[0] // LANES

    def kernel(place_ref, targets_ref, offset_ref, first_ref, mine_ref, *refs):
        group_refs, (out_ref, sources_ref, *score_refs) = refs[: len(groups)], refs[len(groups) :]
        cols = jnp.concatenate([ref[...] for ref in group_refs], axis=0)
        cols = jnp.concatenate([cols, ones_for(count)], axis=1)
        rows = Rows(count)
        for at in range(0, width, ROWS):
            scores_ref = score_refs[at // ROWS % len(score_refs)]
            scores_ref[...] = product(jnp.concatenate([targets_ref[at : at + ROWS, :], offset_ref[at : at + ROWS, :]], axis=1), cols)
            rows.add(scores_ref)
        lse = rows.lse()
        for step in range(len(groups) + 1):
            start = jnp.bitwise_xor(place_ref[2], step) * each
            ref = group_refs[step - 1] if step else mine_ref
            sources_ref[pl.ds(pl.multiple_of(start * LANES, each * LANES), each * LANES), :] = ref[...]
            for row in range(each):
                at = ((step - 1) * each + row) * LANES
                out_ref[pl.ds(start + row, 1), :] = first_ref[row : row + 1, :] if step == 0 else lse[:, at : at + LANES]

    return pl.pallas_call(
        kernel,
        out_shape=(rows_of(count + each * LANES), pltpu.VMEM((count + each * LANES, LANES), jnp.bfloat16)),
        in_specs=[SMEM] + [VMEM] * (3 + len(groups) + 1),
        out_specs=(VMEM,) * 2,
        scratch_shapes=[pltpu.VMEM((ROWS, count), F32)] * 2,
        compiler_params=params(),
        name="other_rows",
    )(place, pin(targets), pin(offsets), first, pin(mine), *groups)


def first_columns(sources, targets, parts, log_mass):
    count, width = sources.shape[0], targets.shape[0]

    def kernel(sources_ref, targets_ref, parts_ref, log_ref, plan_ref, reach_ref, top_ref, out_ref, lse_ref, *score_refs):
        lse = log_sum([parts_ref[i] for i in range(parts.shape[0])])
        lse_ref[...] = lse
        mask = diagonal()
        shift = (log_ref[...] - lse) * (1.0 / SCALE)
        shift = [pieces_of(to_column(shift[i : i + 1, :], mask)) for i in range(count // LANES)]
        cols = jnp.concatenate([sources_ref[...], jnp.concatenate(shift, axis=0)], axis=1)
        ones = ones_for(ROWS)
        for at in range(0, width, ROWS):
            scores_ref = score_refs[at // ROWS % len(score_refs)]
            scores_ref[...] = product(jnp.concatenate([targets_ref[at : at + ROWS, :], ones], axis=1), cols)
            for block in range(0, ROWS, LANES):
                peaks, totals = [], []
                for row in range(block, block + LANES, 8):
                    scores = scores_ref[row : row + 8, :]
                    pieces = [scores[:, lane : lane + LANES] for lane in range(0, count, LANES)]
                    peak = tree(pieces, jnp.maximum)
                    pieces = [jnp.exp2((piece - peak) * SCALE) for piece in pieces]
                    plan_ref[at + row : at + row + 8, :] = jnp.concatenate(pieces, axis=1)
                    peaks.append(peak * SCALE)
                    totals.append(tree(pieces, jnp.add))
                peak = jnp.concatenate(peaks, axis=0)
                top = jnp.max(peak, axis=1, keepdims=True)
                reach = jnp.exp2(peak - top)
                reach_ref[at + block : at + block + LANES, :] = reach
                total = jnp.sum((jnp.concatenate(totals, axis=0) * reach).T, axis=0, keepdims=True)
                index = (at + block) // LANES
                top_ref[index : index + 1, :] = to_row(top, mask)
                out_ref[index : index + 1, :] = top_ref[index : index + 1, :] + jnp.log2(total)

    return pl.pallas_call(
        kernel,
        out_shape=(
            pltpu.VMEM((width, count), F32),
            pltpu.VMEM((width, LANES), F32),
            rows_of(width),
            rows_of(width),
            rows_of(count),
        ),
        in_specs=[VMEM] * 4,
        out_specs=(VMEM,) * 5,
        scratch_shapes=[pltpu.VMEM((ROWS, count), F32)] * 2,
        compiler_params=params(),
        name="first_columns",
    )(pin(sources), pin(targets), parts, log_mass)


def later_rows(plan, reach, top, log_mass, parts):
    width, count = plan.shape
    rows = width // LANES

    def kernel(plan_ref, reach_ref, top_ref, log_ref, *refs):
        part_refs, out_ref = refs[:-1], refs[-1]
        weight = jnp.exp2(log_ref[...] + (top_ref[...] - log_sum([ref[...] for ref in part_refs])))
        mask = diagonal()
        total = jnp.zeros((8, count), F32)
        for block in range(rows):
            at = block * LANES
            factors = reach_ref[at : at + LANES, :] * to_column(weight[block : block + 1, :], mask)
            for row in range(0, LANES, 8):
                factor = jnp.concatenate([factors[row : row + 8, :]] * (count // LANES), axis=1)
                total = total + plan_ref[at + row : at + row + 8, :] * factor
        fold_into(out_ref, jnp.sum(total, axis=0, keepdims=True))

    return pl.pallas_call(
        kernel,
        out_shape=rows_of(count),
        in_specs=[VMEM] * (4 + len(parts)),
        out_specs=VMEM,
        compiler_params=params(),
        name="later_rows",
    )(pin(plan), pin(reach), top, log_mass, *parts)


def later_columns(plan, reach, top, parts, log_mass, lse, half, last):
    width, count = plan.shape

    def kernel(plan_ref, reach_ref, top_ref, parts_ref, log_ref, lse_ref, half_ref, out_ref, *potential_refs):
        factor = log_ref[...] - jnp.log2(tree([parts_ref[i] for i in range(parts.shape[0])], jnp.add))
        for ref in potential_refs:
            ref[...] = half_ref[...] + UNIT * (factor - lse_ref[...])
        factor = unfold(jnp.exp2(factor))
        factors = [factor[:, lane : lane + LANES] for lane in range(0, count, LANES)]
        for at in range(0, width, LANES):
            totals = []
            for row in range(at, at + LANES, 8):
                plan = plan_ref[row : row + 8, :]
                totals.append(tree([plan[:, i * LANES : (i + 1) * LANES] * factors[i] for i in range(count // LANES)], jnp.add))
            total = jnp.concatenate(totals, axis=0) * reach_ref[at : at + LANES, :]
            index = at // LANES
            total = jnp.log2(jnp.sum(total.T, axis=0, keepdims=True))
            out_ref[index : index + 1, :] = top_ref[index : index + 1, :] + total

    return pl.pallas_call(
        kernel,
        out_shape=(rows_of(width),) + (rows_of(count),) * last,
        in_specs=[VMEM] * 7,
        out_specs=(VMEM,) * (1 + last),
        compiler_params=params(),
        name="later_columns",
    )(pin(plan), pin(reach), top, parts, log_mass, lse, half)


def levels_of(size):
    bits = size.bit_length() - 1
    out = []
    while bits > 0:
        take = 2 if bits % 2 == 0 else 1
        bits -= take
        out.append([step << bits for step in range(1, 1 << take)])
    return out


def swap(value, axes, size, distance):
    return lax.ppermute(value, axes, [(i, i ^ distance) for i in range(size)])


def swap_all(value, axes, size):
    values = [value]
    for distances in levels_of(size):
        got = {d: [swap(value, axes, size, d) for value in values] for d in reversed(distances)}
        values = [part for i in range(len(values)) for part in [values[i]] + [got[d][i] for d in distances]]
    return values


def share(value, size):
    copies = jnp.broadcast_to(value[None], (size,) + value.shape)
    return lax.all_to_all(copies, ("z", "x"), 0, 0, tiled=True)


def half_norm(points):
    values = points.astype(F32)
    return 0.5 * jnp.sum(values * values, axis=1)


def make_local(n_src, n_z, n_x):
    near, n_near = ("src", "core"), n_src * CORES
    n_far = n_z * n_x

    def local(source_points, target_points, source_mass, target_mass):
        core, x = lax.axis_index("core"), lax.axis_index("x")
        place = jnp.stack([lax.axis_index("src"), core, x]).astype(jnp.int32)
        along = lax.axis_index("z").astype(jnp.int32).reshape(1)
        part = source_points.shape[0]
        a = source_mass.reshape(n_z, n_x, CORES, part)
        a = lax.dynamic_index_in_dim(a, core, axis=2, keepdims=False).swapaxes(0, 1).reshape(-1, LANES)
        blocks = swap_all(target_points, "src", n_src)[1:]
        three, two, one = [swap(source_points, "z", n_z, d) for d in (3, 2, 1)]
        mine, packed, b, a = ready(source_points, target_points, target_mass.reshape(-1, LANES), a)
        laid = lay(along, three, 3, n_z)
        packed = swap_all(packed, "core", CORES)
        blocks = blocks + [swap(block, "core", CORES, 1) for block in blocks]
        groups = swap_all(pack(along, [mine, one, two], laid), "x", n_x)
        place, a = lax.optimization_barrier((place, a))
        targets, offsets, b, first = first_rows(place, b, packed, blocks, groups[0])
        own, sources = other_rows(place, targets, offsets, first, groups)
        plan, reach, top, own, row_lse = first_columns(sources, targets, share(own, n_far), a)
        early_x, early_y, own = lax.optimization_barrier((sources, targets, own))
        half_x, half_y = half_norm(early_x).reshape(-1, LANES), half_norm(early_y).reshape(-1, LANES)
        parts = swap_all(own, near, n_near)
        half_x, half_y, *parts = lax.optimization_barrier((half_x, half_y, *parts))
        for step in range(1, ITERS):
            rows = later_rows(plan, reach, top, b, parts)
            own, *potential = later_columns(plan, reach, top, share(rows, n_far), a, row_lse, half_x, step == ITERS - 1)
            parts = swap_all(own, near, n_near)
        mine, other = swap_all(potential[0].reshape(n_x, n_z, part), "core", CORES)
        first, second = jnp.where(core == 0, mine, other), jnp.where(core == 0, other, mine)
        source_potential = jnp.stack([first, second], axis=2).swapaxes(0, 1).reshape(-1)
        target_potential = half_y - UNIT * log_sum(parts)
        target_potential = target_potential.reshape(CORES, -1)
        target_potential = lax.dynamic_index_in_dim(target_potential, core, axis=0, keepdims=False)
        return source_potential, target_potential

    return local


def solution(mesh):
    n_src, n_tgt = mesh.shape["src"], mesh.shape["tgt"]
    n_z = 4
    n_x = n_tgt // (n_z * CORES)
    split = Mesh(mesh.devices.reshape(n_src, n_z, n_x, CORES), ("src", "z", "x", "core"))
    tgt = ("z", "x", "core")
    placed = (P(("src", *tgt), None), P((*tgt, "src"), None), P("src"), P(tgt))
    return jax.shard_map(
        make_local(n_src, n_z, n_x),
        mesh=split,
        in_specs=placed,
        out_specs=(P("src"), P(tgt)),
        check_vma=False,
    )
```

```python
import math

import jax
import jax.numpy as jnp
from jax import lax
from jax.experimental import pallas as pl
from jax.experimental.pallas import tpu as pltpu
from jax.sharding import Mesh, PartitionSpec as P

ITERS = 3
EPS = 0.05
SCALE = 1.0 / (EPS * math.log(2.0))
UNIT = EPS * math.log(2.0)
LANES = 128
CORES = 2
PIECES = 3
ROWS = 256
F32 = jnp.float32
VMEM = pl.BlockSpec(memory_space=pltpu.VMEM)
SMEM = pl.BlockSpec(memory_space=pltpu.SMEM)


def params(limit=24):
    return pltpu.CompilerParams(vmem_limit_bytes=limit * 1024 * 1024)


def pin(value):
    return pltpu.with_memory_space_constraint(value, pltpu.VMEM)


def rows_of(count):
    return jax.ShapeDtypeStruct((count // LANES, LANES), F32)


def diagonal():
    shape = (LANES, LANES)
    return lax.broadcasted_iota(jnp.int32, shape, 0) == lax.broadcasted_iota(jnp.int32, shape, 1)


def to_column(row, mask):
    return jnp.sum(jnp.where(mask, jnp.broadcast_to(row, mask.shape), 0.0), axis=1, keepdims=True)


def to_row(column, mask):
    return jnp.sum(jnp.where(mask, jnp.broadcast_to(column, mask.shape), 0.0), axis=0, keepdims=True)


def unfold(value):
    return jnp.concatenate([value[i : i + 1, :] for i in range(value.shape[0])], axis=1)


def fold_into(ref, value):
    for row in range(ref.shape[0]):
        ref[row : row + 1, :] = value[:, row * LANES : (row + 1) * LANES]


def tree(values, join):
    while len(values) > 1:
        values = [join(values[i], values[i + 1]) for i in range(0, len(values), 2)]
    return values[0]


def log_sum(values):
    peak = tree(values, jnp.maximum)
    return peak + jnp.log2(tree([jnp.exp2(value - peak) for value in values], jnp.add))


def product(rows, cols):
    return lax.dot_general(rows, cols, (((1,), (1,)), ((), ())), preferred_element_type=F32)


def ready(sources, targets, mass, source_mass):
    part, chunk = targets.shape[0], mass.shape[0]
    anywhere = pl.BlockSpec(memory_space=pl.ANY)

    def kernel(sources_ref, targets_ref, mass_ref, source_ref, sources_out, packed_ref, mass_out, source_out, *sems):
        copies = [
            pltpu.make_async_copy(mass_ref, mass_out, sems[0]),
            pltpu.make_async_copy(targets_ref, packed_ref.at[:part], sems[1]),
            pltpu.make_async_copy(sources_ref, sources_out, sems[2]),
        ]
        for copy in copies:
            copy.start()
        source_out[...] = jnp.log2(source_ref[...])
        copies[0].wait()
        value, pieces = mass_out[...], []
        for step in range(PIECES):
            pieces.append(value.astype(jnp.bfloat16).astype(F32))
            value = value - pieces[-1]
        pieces.append(jnp.zeros_like(value))
        packed_ref[part:, :] = jnp.concatenate(pieces, axis=0).astype(jnp.bfloat16)
        copies[1].wait()
        copies[2].wait()

    return pl.pallas_call(
        kernel,
        out_shape=(
            pltpu.VMEM(sources.shape, jnp.bfloat16),
            pltpu.VMEM((part + (PIECES + 1) * chunk, LANES), jnp.bfloat16),
            pltpu.VMEM(mass.shape, F32),
            pltpu.VMEM(source_mass.shape, F32),
        ),
        in_specs=[anywhere, anywhere, anywhere, VMEM],
        out_specs=(VMEM,) * 4,
        scratch_shapes=[pltpu.SemaphoreType.DMA] * 3,
        compiler_params=params(),
        cost_estimate=pl.CostEstimate(flops=1 << 20, bytes_accessed=1 << 20, transcendentals=0),
        name="ready",
    )(*[pltpu.with_memory_space_constraint(value, pltpu.HBM) for value in (sources, targets, mass)], source_mass)


def lay(place, block, step, count):
    part = block.shape[0]

    def kernel(place_ref, block_ref, out_ref):
        start = pl.multiple_of(jnp.bitwise_xor(place_ref[0], step) * part, part)
        out_ref[pl.ds(start, part), :] = block_ref[...]

    return pl.pallas_call(
        kernel,
        out_shape=pltpu.VMEM((count * part, LANES), jnp.bfloat16),
        in_specs=[SMEM, VMEM],
        out_specs=VMEM,
        compiler_params=params(),
        cost_estimate=pl.CostEstimate(flops=1<<30, bytes_accessed=1 << 18, transcendentals=0),
        name="lay",
    )(place, block)


def pack(place, blocks, laid):
    part = blocks[0].shape[0]

    def kernel(place_ref, *refs):
        out_ref = refs[-1]
        for step in range(len(blocks)):
            start = pl.multiple_of(jnp.bitwise_xor(place_ref[0], step) * part, part)
            out_ref[pl.ds(start, part), :] = refs[step][...]

    return pl.pallas_call(
        kernel,
        out_shape=pltpu.VMEM(laid.shape, jnp.bfloat16),
        in_specs=[SMEM] + [VMEM] * (len(blocks) + 1),
        out_specs=VMEM,
        input_output_aliases={1 + len(blocks): 0},
        compiler_params=params(),
        cost_estimate=pl.CostEstimate(flops=1<<20, bytes_accessed=1 << 18, transcendentals=0),
        name="pack",
    )(place, *blocks, laid)


def pieces_of(value):
    lane = lax.broadcasted_iota(jnp.int32, (value.shape[0], LANES), 1)
    tile = jnp.zeros((value.shape[0], LANES), F32)
    for step in range(PIECES):
        piece = value.astype(jnp.bfloat16).astype(F32)
        tile = jnp.where(lane == step, piece, tile)
        value = value - piece
    return tile.astype(jnp.bfloat16)


def ones_for(rows):
    lane = lax.broadcasted_iota(jnp.int32, (rows, LANES), 1)
    return jnp.where(lane < PIECES, 1.0, 0.0).astype(jnp.bfloat16)


class Rows:
    def __init__(self, count):
        self.peak = jnp.full((8, count), -1e30, F32)
        self.total = jnp.zeros((8, count), F32)

    def add(self, scores_ref):
        tops = self.peak
        for row in range(0, ROWS, 8):
            tops = jnp.maximum(tops, scores_ref[row : row + 8, :])
        self.total = self.total * jnp.exp2((self.peak - tops) * SCALE)
        self.peak = tops
        for row in range(0, ROWS, 8):
            self.total = self.total + jnp.exp2((scores_ref[row : row + 8, :] - tops) * SCALE)

    def lse(self):
        widest = jnp.max(self.peak, axis=0, keepdims=True)
        total = jnp.sum(self.total * jnp.exp2((self.peak - widest) * SCALE), axis=0, keepdims=True)
        return widest * SCALE + jnp.log2(total)


def first_rows(place, mass, packed, blocks, sources):
    count, chunk = sources.shape[0], mass.shape[0]
    n_src = len(blocks) // CORES + 1
    part = blocks[0].shape[0]
    width = CORES * n_src * part

    def kernel(place_ref, mass_ref, sources_ref, *refs):
        own_ref, other_ref, block_refs = refs[0], refs[1], refs[2 : 2 + len(blocks)]
        targets_ref, offset_ref, full_ref, out_ref, *score_refs = refs[2 + len(blocks) :]
        src, core = place_ref[0], place_ref[1]
        full_ref[pl.ds(pl.multiple_of(core * chunk, chunk), chunk), :] = jnp.log2(mass_ref[...])
        parts = [other_ref[part + i * chunk : part + (i + 1) * chunk, :].astype(F32) for i in range(PIECES)]
        start = pl.multiple_of(jnp.bitwise_xor(core, 1) * chunk, chunk)
        full_ref[pl.ds(start, chunk), :] = jnp.log2(parts[0] + (parts[1] + parts[2]))
        for dc in range(CORES):
            for ds in range(n_src):
                index = jnp.bitwise_xor(core, dc) * n_src + jnp.bitwise_xor(src, ds)
                start = pl.multiple_of(index * part, part)
                ref = refs[dc] if ds == 0 else block_refs[dc * (n_src - 1) + ds - 1]
                targets_ref[pl.ds(start, part), :] = ref[:part, :]
        mask = diagonal()
        log_mass = full_ref[...] * (1.0 / SCALE)
        cols = jnp.concatenate([sources_ref[...], ones_for(count)], axis=1)
        rows = Rows(count)
        for at in range(0, width, ROWS):
            scores_ref = score_refs[at // ROWS % len(score_refs)]
            for row in range(at, at + ROWS, LANES):
                values = targets_ref[row : row + LANES, :].astype(F32)
                half = 0.5 * jnp.sum(values * values, axis=1, keepdims=True)
                block = row // LANES
                offset_ref[row : row + LANES, :] = pieces_of(to_column(log_mass[block : block + 1, :], mask) - half)
            scores_ref[...] = product(jnp.concatenate([targets_ref[at : at + ROWS, :], offset_ref[at : at + ROWS, :]], axis=1), cols)
            rows.add(scores_ref)
        fold_into(out_ref, rows.lse())

    return pl.pallas_call(
        kernel,
        out_shape=(
            pltpu.VMEM((width, LANES), jnp.bfloat16),
            pltpu.VMEM((width, LANES), jnp.bfloat16),
            rows_of(width),
            rows_of(count),
        ),
        in_specs=[SMEM] + [VMEM] * (4 + len(blocks)),
        out_specs=(VMEM,) * 4,
        scratch_shapes=[pltpu.VMEM((ROWS, count), F32)] * 2,
        compiler_params=params(),
        cost_estimate=pl.CostEstimate(flops=1<<20, bytes_accessed=1 << 18, transcendentals=0),
        name="first_rows",
    )(place, mass, pin(sources), *[pin(value) for value in packed], *[pin(value) for value in blocks])


def other_rows(place, targets, offsets, first, groups):
    mine, groups = groups[0], groups[1:]
    width, count, each = targets.shape[0], sum(group.shape[0] for group in groups), mine.shape[0] // LANES

    def kernel(place_ref, targets_ref, offset_ref, first_ref, mine_ref, *refs):
        group_refs, (out_ref, sources_ref, *score_refs) = refs[: len(groups)], refs[len(groups) :]
        cols = jnp.concatenate([ref[...] for ref in group_refs], axis=0)
        cols = jnp.concatenate([cols, ones_for(count)], axis=1)
        rows = Rows(count)
        for at in range(0, width, ROWS):
            scores_ref = score_refs[at // ROWS % len(score_refs)]
            scores_ref[...] = product(jnp.concatenate([targets_ref[at : at + ROWS, :], offset_ref[at : at + ROWS, :]], axis=1), cols)
            rows.add(scores_ref)
        lse = rows.lse()
        for step in range(len(groups) + 1):
            start = jnp.bitwise_xor(place_ref[2], step) * each
            ref = group_refs[step - 1] if step else mine_ref
            sources_ref[pl.ds(pl.multiple_of(start * LANES, each * LANES), each * LANES), :] = ref[...]
            for row in range(each):
                at = ((step - 1) * each + row) * LANES
                out_ref[pl.ds(start + row, 1), :] = first_ref[row : row + 1, :] if step == 0 else lse[:, at : at + LANES]

    return pl.pallas_call(
        kernel,
        out_shape=(rows_of(count + each * LANES), pltpu.VMEM((count + each * LANES, LANES), jnp.bfloat16)),
        in_specs=[SMEM] + [VMEM] * (3 + len(groups) + 1),
        out_specs=(VMEM,) * 2,
        scratch_shapes=[pltpu.VMEM((ROWS, count), F32)] * 2,
        compiler_params=params(),
        name="other_rows",
    )(place, pin(targets), pin(offsets), first, pin(mine), *groups)


def first_columns(sources, targets, parts, log_mass):
    count, width = sources.shape[0], targets.shape[0]

    def kernel(sources_ref, targets_ref, parts_ref, log_ref, plan_ref, reach_ref, top_ref, out_ref, lse_ref, *score_refs):
        lse = log_sum([parts_ref[i] for i in range(parts.shape[0])])
        lse_ref[...] = lse
        mask = diagonal()
        shift = (log_ref[...] - lse) * (1.0 / SCALE)
        shift = [pieces_of(to_column(shift[i : i + 1, :], mask)) for i in range(count // LANES)]
        cols = jnp.concatenate([sources_ref[...], jnp.concatenate(shift, axis=0)], axis=1)
        ones = ones_for(ROWS)
        for at in range(0, width, ROWS):
            scores_ref = score_refs[at // ROWS % len(score_refs)]
            scores_ref[...] = product(jnp.concatenate([targets_ref[at : at + ROWS, :], ones], axis=1), cols)
            for block in range(0, ROWS, LANES):
                peaks, totals = [], []
                for row in range(block, block + LANES, 8):
                    scores = scores_ref[row : row + 8, :]
                    pieces = [scores[:, lane : lane + LANES] for lane in range(0, count, LANES)]
                    peak = tree(pieces, jnp.maximum)
                    pieces = [jnp.exp2((piece - peak) * SCALE) for piece in pieces]
                    plan_ref[at + row : at + row + 8, :] = jnp.concatenate(pieces, axis=1)
                    peaks.append(peak * SCALE)
                    totals.append(tree(pieces, jnp.add))
                peak = jnp.concatenate(peaks, axis=0)
                top = jnp.max(peak, axis=1, keepdims=True)
                reach = jnp.exp2(peak - top)
                reach_ref[at + block : at + block + LANES, :] = reach
                total = jnp.sum((jnp.concatenate(totals, axis=0) * reach).T, axis=0, keepdims=True)
                index = (at + block) // LANES
                top_ref[index : index + 1, :] = to_row(top, mask)
                out_ref[index : index + 1, :] = top_ref[index : index + 1, :] + jnp.log2(total)

    return pl.pallas_call(
        kernel,
        out_shape=(
            pltpu.VMEM((width, count), F32),
            pltpu.VMEM((width, LANES), F32),
            rows_of(width),
            rows_of(width),
            rows_of(count),
        ),
        in_specs=[VMEM] * 4,
        out_specs=(VMEM,) * 5,
        scratch_shapes=[pltpu.VMEM((ROWS, count), F32)] * 2,
        compiler_params=params(),
        name="first_columns",
    )(pin(sources), pin(targets), parts, log_mass)


def later_rows(plan, reach, top, log_mass, parts):
    width, count = plan.shape
    rows = width // LANES

    def kernel(plan_ref, reach_ref, top_ref, log_ref, *refs):
        part_refs, out_ref = refs[:-1], refs[-1]
        weight = jnp.exp2(log_ref[...] + (top_ref[...] - log_sum([ref[...] for ref in part_refs])))
        mask = diagonal()
        total = jnp.zeros((8, count), F32)
        for block in range(rows):
            at = block * LANES
            factors = reach_ref[at : at + LANES, :] * to_column(weight[block : block + 1, :], mask)
            for row in range(0, LANES, 8):
                factor = jnp.concatenate([factors[row : row + 8, :]] * (count // LANES), axis=1)
                total = total + plan_ref[at + row : at + row + 8, :] * factor
        fold_into(out_ref, jnp.sum(total, axis=0, keepdims=True))

    return pl.pallas_call(
        kernel,
        out_shape=rows_of(count),
        in_specs=[VMEM] * (4 + len(parts)),
        out_specs=VMEM,
        compiler_params=params(),
        name="later_rows",
    )(pin(plan), pin(reach), top, log_mass, *parts)


def later_columns(plan, reach, top, parts, log_mass, lse, half, last):
    width, count = plan.shape

    def kernel(plan_ref, reach_ref, top_ref, parts_ref, log_ref, lse_ref, half_ref, out_ref, *potential_refs):
        factor = log_ref[...] - jnp.log2(tree([parts_ref[i] for i in range(parts.shape[0])], jnp.add))
        for ref in potential_refs:
            ref[...] = half_ref[...] + UNIT * (factor - lse_ref[...])
        factor = unfold(jnp.exp2(factor))
        factors = [factor[:, lane : lane + LANES] for lane in range(0, count, LANES)]
        for at in range(0, width, LANES):
            totals = []
            for row in range(at, at + LANES, 8):
                plan = plan_ref[row : row + 8, :]
                totals.append(tree([plan[:, i * LANES : (i + 1) * LANES] * factors[i] for i in range(count // LANES)], jnp.add))
            total = jnp.concatenate(totals, axis=0) * reach_ref[at : at + LANES, :]
            index = at // LANES
            total = jnp.log2(jnp.sum(total.T, axis=0, keepdims=True))
            out_ref[index : index + 1, :] = top_ref[index : index + 1, :] + total

    return pl.pallas_call(
        kernel,
        out_shape=(rows_of(width),) + (rows_of(count),) * last,
        in_specs=[VMEM] * 7,
        out_specs=(VMEM,) * (1 + last),
        compiler_params=params(),
        name="later_columns",
    )(pin(plan), pin(reach), top, parts, log_mass, lse, half)


def levels_of(size):
    bits = size.bit_length() - 1
    out = []
    while bits > 0:
        take = 2 if bits % 2 == 0 else 1
        bits -= take
        out.append([step << bits for step in range(1, 1 << take)])
    return out


def swap(value, axes, size, distance):
    return lax.ppermute(value, axes, [(i, i ^ distance) for i in range(size)])


def swap_all(value, axes, size):
    values = [value]
    for distances in levels_of(size):
        got = {d: [swap(value, axes, size, d) for value in values] for d in reversed(distances)}
        values = [part for i in range(len(values)) for part in [values[i]] + [got[d][i] for d in distances]]
    return values


def share(value, size):
    copies = jnp.broadcast_to(value[None], (size,) + value.shape)
    return lax.all_to_all(copies, ("z", "x"), 0, 0, tiled=True)


def half_norm(points):
    values = points.astype(F32)
    return 0.5 * jnp.sum(values * values, axis=1)


def make_local(n_src, n_z, n_x):
    near, n_near = ("src", "core"), n_src * CORES
    n_far = n_z * n_x

    def local(source_points, target_points, source_mass, target_mass):
        core, x = lax.axis_index("core"), lax.axis_index("x")
        place = jnp.stack([lax.axis_index("src"), core, x]).astype(jnp.int32)
        along = lax.axis_index("z").astype(jnp.int32).reshape(1)
        part = source_points.shape[0]
        a = source_mass.reshape(n_z, n_x, CORES, part)
        a = lax.dynamic_index_in_dim(a, core, axis=2, keepdims=False).swapaxes(0, 1).reshape(-1, LANES)
        blocks = swap_all(target_points, "src", n_src)[1:]
        three, two = [swap(source_points, "z", n_z, d) for d in (3, 2)]
        mine, packed, b, a = ready(source_points, target_points, target_mass.reshape(-1, LANES), a)
        one = swap(mine, "z", n_z, 1)
        laid = lay(along, three, 3, n_z)
        packed = swap_all(packed, "core", CORES)
        blocks = blocks + [swap(block, "core", CORES, 1) for block in blocks]
        groups = swap_all(pack(along, [mine, one, two], laid), "x", n_x)
        place, a = lax.optimization_barrier((place, a))
        targets, offsets, b, first = first_rows(place, b, packed, blocks, groups[0])
        own, sources = other_rows(place, targets, offsets, first, groups)
        plan, reach, top, own, row_lse = first_columns(sources, targets, share(own, n_far), a)
        early_x, early_y, own = lax.optimization_barrier((sources, targets, own))
        half_x, half_y = half_norm(early_x).reshape(-1, LANES), half_norm(early_y).reshape(-1, LANES)
        parts = swap_all(own, near, n_near)
        half_x, half_y, *parts = lax.optimization_barrier((half_x, half_y, *parts))
        for step in range(1, ITERS):
            rows = later_rows(plan, reach, top, b, parts)
            own, *potential = later_columns(plan, reach, top, share(rows, n_far), a, row_lse, half_x, step == ITERS - 1)
            parts = swap_all(own, near, n_near)
        mine, other = swap_all(potential[0].reshape(n_x, n_z, part), "core", CORES)
        first, second = jnp.where(core == 0, mine, other), jnp.where(core == 0, other, mine)
        source_potential = jnp.stack([first, second], axis=2).swapaxes(0, 1).reshape(-1)
        target_potential = half_y - UNIT * log_sum(parts)
        target_potential = target_potential.reshape(CORES, -1)
        target_potential = lax.dynamic_index_in_dim(target_potential, core, axis=0, keepdims=False)
        return source_potential, target_potential

    return local


def solution(mesh):
    n_src, n_tgt = mesh.shape["src"], mesh.shape["tgt"]
    n_z = 4
    n_x = n_tgt // (n_z * CORES)
    split = Mesh(mesh.devices.reshape(n_src, n_z, n_x, CORES), ("src", "z", "x", "core"))
    tgt = ("z", "x", "core")
    placed = (P(("src", *tgt), None), P((*tgt, "src"), None), P("src"), P(tgt))
    return jax.shard_map(
        make_local(n_src, n_z, n_x),
        mesh=split,
        in_specs=placed,
        out_specs=(P("src"), P(tgt)),
        check_vma=False,
    )
```

```python
import math

import jax
import jax.numpy as jnp
from jax import lax
from jax.experimental import pallas as pl
from jax.experimental.pallas import tpu as pltpu
from jax.sharding import Mesh, PartitionSpec as P

ITERS = 3
EPS = 0.05
SCALE = 1.0 / (EPS * math.log(2.0))
UNIT = EPS * math.log(2.0)
LANES = 128
CORES = 2
PIECES = 3
ROWS = 256
CHAINS = 4
F32 = jnp.float32
VMEM = pl.BlockSpec(memory_space=pltpu.VMEM)
SMEM = pl.BlockSpec(memory_space=pltpu.SMEM)


def params(limit=24):
    return pltpu.CompilerParams(vmem_limit_bytes=limit * 1024 * 1024)


def pin(value):
    return pltpu.with_memory_space_constraint(value, pltpu.VMEM)


def rows_of(count):
    return jax.ShapeDtypeStruct((count // LANES, LANES), F32)


def diagonal():
    shape = (LANES, LANES)
    return lax.broadcasted_iota(jnp.int32, shape, 0) == lax.broadcasted_iota(jnp.int32, shape, 1)


def to_column(row, mask):
    return jnp.sum(jnp.where(mask, jnp.broadcast_to(row, mask.shape), 0.0), axis=1, keepdims=True)


def to_row(column, mask):
    return jnp.sum(jnp.where(mask, jnp.broadcast_to(column, mask.shape), 0.0), axis=0, keepdims=True)


def unfold(value):
    return jnp.concatenate([value[i : i + 1, :] for i in range(value.shape[0])], axis=1)


def fold_into(ref, value):
    for row in range(ref.shape[0]):
        ref[row : row + 1, :] = value[:, row * LANES : (row + 1) * LANES]


def tree(values, join):
    while len(values) > 1:
        values = [join(values[i], values[i + 1]) for i in range(0, len(values), 2)]
    return values[0]


def log_sum(values):
    peak = tree(values, jnp.maximum)
    return peak + jnp.log2(tree([jnp.exp2(value - peak) for value in values], jnp.add))


def product(rows, cols):
    return lax.dot_general(rows, cols, (((1,), (1,)), ((), ())), preferred_element_type=F32)


def ready(sources, targets, mass, source_mass):
    part, chunk = targets.shape[0], mass.shape[0]
    anywhere = pl.BlockSpec(memory_space=pl.ANY)

    def kernel(sources_ref, targets_ref, mass_ref, source_ref, sources_out, packed_ref, mass_out, source_out, *sems):
        copies = [
            pltpu.make_async_copy(mass_ref, mass_out, sems[0]),
            pltpu.make_async_copy(targets_ref, packed_ref.at[:part], sems[1]),
            pltpu.make_async_copy(sources_ref, sources_out, sems[2]),
        ]
        for copy in copies:
            copy.start()
        source_out[...] = jnp.log2(source_ref[...])
        copies[0].wait()
        value, pieces = mass_out[...], []
        for step in range(PIECES):
            pieces.append(value.astype(jnp.bfloat16).astype(F32))
            value = value - pieces[-1]
        pieces.append(jnp.zeros_like(value))
        packed_ref[part:, :] = jnp.concatenate(pieces, axis=0).astype(jnp.bfloat16)
        copies[1].wait()
        copies[2].wait()

    return pl.pallas_call(
        kernel,
        out_shape=(
            pltpu.VMEM(sources.shape, jnp.bfloat16),
            pltpu.VMEM((part + (PIECES + 1) * chunk, LANES), jnp.bfloat16),
            pltpu.VMEM(mass.shape, F32),
            pltpu.VMEM(source_mass.shape, F32),
        ),
        in_specs=[anywhere, anywhere, anywhere, VMEM],
        out_specs=(VMEM,) * 4,
        scratch_shapes=[pltpu.SemaphoreType.DMA] * 3,
        compiler_params=params(),
        cost_estimate=pl.CostEstimate(flops=1 << 20, bytes_accessed=1 << 20, transcendentals=0),
        name="ready",
    )(*[pltpu.with_memory_space_constraint(value, pltpu.HBM) for value in (sources, targets, mass)], source_mass)


def lay(place, block, step, count):
    part = block.shape[0]

    def kernel(place_ref, block_ref, out_ref):
        start = pl.multiple_of(jnp.bitwise_xor(place_ref[0], step) * part, part)
        out_ref[pl.ds(start, part), :] = block_ref[...]

    return pl.pallas_call(
        kernel,
        out_shape=pltpu.VMEM((count * part, LANES), jnp.bfloat16),
        in_specs=[SMEM, VMEM],
        out_specs=VMEM,
        compiler_params=params(),
        cost_estimate=pl.CostEstimate(flops=1 << 20, bytes_accessed=1 << 20, transcendentals=0),
        name="lay",
    )(place, block)


def pack(place, blocks, laid):
    part = blocks[0].shape[0]

    def kernel(place_ref, *refs):
        out_ref = refs[-1]
        for step in range(len(blocks)):
            start = pl.multiple_of(jnp.bitwise_xor(place_ref[0], step) * part, part)
            out_ref[pl.ds(start, part), :] = refs[step][...]

    return pl.pallas_call(
        kernel,
        out_shape=pltpu.VMEM(laid.shape, jnp.bfloat16),
        in_specs=[SMEM] + [VMEM] * (len(blocks) + 1),
        out_specs=VMEM,
        input_output_aliases={1 + len(blocks): 0},
        compiler_params=params(),
        cost_estimate=pl.CostEstimate(flops=1 << 20, bytes_accessed=1 << 18, transcendentals=0),
        name="pack",
    )(place, *blocks, laid)


def pieces_of(value):
    lane = lax.broadcasted_iota(jnp.int32, (value.shape[0], LANES), 1)
    tile = jnp.zeros((value.shape[0], LANES), F32)
    for step in range(PIECES):
        piece = value.astype(jnp.bfloat16).astype(F32)
        tile = jnp.where(lane == step, piece, tile)
        value = value - piece
    return tile.astype(jnp.bfloat16)


def ones_for(rows):
    lane = lax.broadcasted_iota(jnp.int32, (rows, LANES), 1)
    return jnp.where(lane < PIECES, 1.0, 0.0).astype(jnp.bfloat16)


class Rows:
    def __init__(self, count):
        self.peak = jnp.full((8, count), -1e30, F32)
        self.total = jnp.zeros((8, count), F32)

    def add(self, scores_ref):
        slices = [scores_ref[row : row + 8, :] for row in range(0, ROWS, 8)]
        tops = [tree(slices[i::CHAINS], jnp.maximum) for i in range(CHAINS)]
        tops = jnp.maximum(self.peak, tree(tops, jnp.maximum))
        totals = [self.total * jnp.exp2((self.peak - tops) * SCALE)] + [None] * (CHAINS - 1)
        for step in range(len(slices)):
            part = jnp.exp2((scores_ref[step * 8 : step * 8 + 8, :] - tops) * SCALE)
            chain = (step + 1) % CHAINS
            totals[chain] = part if totals[chain] is None else totals[chain] + part
        self.peak, self.total = tops, tree(totals, jnp.add)

    def lse(self):
        widest = jnp.max(self.peak, axis=0, keepdims=True)
        total = jnp.sum(self.total * jnp.exp2((self.peak - widest) * SCALE), axis=0, keepdims=True)
        return widest * SCALE + jnp.log2(total)


def first_rows(place, mass, packed, blocks, sources):
    count, chunk = sources.shape[0], mass.shape[0]
    n_src = len(blocks) // CORES + 1
    part = blocks[0].shape[0]
    width = CORES * n_src * part

    def kernel(place_ref, mass_ref, sources_ref, *refs):
        own_ref, other_ref, block_refs = refs[0], refs[1], refs[2 : 2 + len(blocks)]
        targets_ref, offset_ref, full_ref, out_ref, *score_refs = refs[2 + len(blocks) :]
        src, core = place_ref[0], place_ref[1]
        full_ref[pl.ds(pl.multiple_of(core * chunk, chunk), chunk), :] = jnp.log2(mass_ref[...])
        parts = [other_ref[part + i * chunk : part + (i + 1) * chunk, :].astype(F32) for i in range(PIECES)]
        start = pl.multiple_of(jnp.bitwise_xor(core, 1) * chunk, chunk)
        full_ref[pl.ds(start, chunk), :] = jnp.log2(parts[0] + (parts[1] + parts[2]))
        for dc in range(CORES):
            for ds in range(n_src):
                index = jnp.bitwise_xor(core, dc) * n_src + jnp.bitwise_xor(src, ds)
                start = pl.multiple_of(index * part, part)
                ref = refs[dc] if ds == 0 else block_refs[dc * (n_src - 1) + ds - 1]
                targets_ref[pl.ds(start, part), :] = ref[:part, :]
        mask = diagonal()
        log_mass = full_ref[...] * (1.0 / SCALE)
        cols = jnp.concatenate([sources_ref[...], ones_for(count)], axis=1)
        rows = Rows(count)
        for at in range(0, width, ROWS):
            scores_ref = score_refs[at // ROWS % len(score_refs)]
            for row in range(at, at + ROWS, LANES):
                values = targets_ref[row : row + LANES, :].astype(F32)
                half = 0.5 * jnp.sum(values * values, axis=1, keepdims=True)
                block = row // LANES
                offset_ref[row : row + LANES, :] = pieces_of(to_column(log_mass[block : block + 1, :], mask) - half)
            scores_ref[...] = product(jnp.concatenate([targets_ref[at : at + ROWS, :], offset_ref[at : at + ROWS, :]], axis=1), cols)
            rows.add(scores_ref)
        fold_into(out_ref, rows.lse())

    return pl.pallas_call(
        kernel,
        out_shape=(
            pltpu.VMEM((width, LANES), jnp.bfloat16),
            pltpu.VMEM((width, LANES), jnp.bfloat16),
            rows_of(width),
            rows_of(count),
        ),
        in_specs=[SMEM] + [VMEM] * (4 + len(blocks)),
        out_specs=(VMEM,) * 4,
        scratch_shapes=[pltpu.VMEM((ROWS, count), F32)] * 2,
        compiler_params=params(),
        cost_estimate=pl.CostEstimate(flops=1 << 29, bytes_accessed=1 << 20, transcendentals=1 << 20),
        name="first_rows",
    )(place, mass, pin(sources), *[pin(value) for value in packed], *[pin(value) for value in blocks])


def other_rows(place, targets, offsets, first, groups):
    mine, groups = groups[0], groups[1:]
    width, count, each = targets.shape[0], sum(group.shape[0] for group in groups), mine.shape[0] // LANES

    def kernel(place_ref, targets_ref, offset_ref, first_ref, mine_ref, *refs):
        group_refs, (out_ref, sources_ref, *score_refs) = refs[: len(groups)], refs[len(groups) :]
        cols = jnp.concatenate([ref[...] for ref in group_refs], axis=0)
        cols = jnp.concatenate([cols, ones_for(count)], axis=1)
        rows = Rows(count)
        for at in range(0, width, ROWS):
            scores_ref = score_refs[at // ROWS % len(score_refs)]
            scores_ref[...] = product(jnp.concatenate([targets_ref[at : at + ROWS, :], offset_ref[at : at + ROWS, :]], axis=1), cols)
            rows.add(scores_ref)
        lse = rows.lse()
        for step in range(len(groups) + 1):
            start = jnp.bitwise_xor(place_ref[2], step) * each
            ref = group_refs[step - 1] if step else mine_ref
            sources_ref[pl.ds(pl.multiple_of(start * LANES, each * LANES), each * LANES), :] = ref[...]
            for row in range(each):
                at = ((step - 1) * each + row) * LANES
                out_ref[pl.ds(start + row, 1), :] = first_ref[row : row + 1, :] if step == 0 else lse[:, at : at + LANES]

    return pl.pallas_call(
        kernel,
        out_shape=(rows_of(count + each * LANES), pltpu.VMEM((count + each * LANES, LANES), jnp.bfloat16)),
        in_specs=[SMEM] + [VMEM] * (3 + len(groups) + 1),
        out_specs=(VMEM,) * 2,
        scratch_shapes=[pltpu.VMEM((ROWS, count), F32)] * 2,
        compiler_params=params(),
        name="other_rows",
    )(place, pin(targets), pin(offsets), first, pin(mine), *groups)


def first_columns(sources, targets, parts, log_mass):
    count, width = sources.shape[0], targets.shape[0]

    def kernel(sources_ref, targets_ref, parts_ref, log_ref, plan_ref, reach_ref, top_ref, out_ref, lse_ref, *score_refs):
        lse = log_sum([parts_ref[i] for i in range(parts.shape[0])])
        lse_ref[...] = lse
        mask = diagonal()
        shift = (log_ref[...] - lse) * (1.0 / SCALE)
        shift = [pieces_of(to_column(shift[i : i + 1, :], mask)) for i in range(count // LANES)]
        cols = jnp.concatenate([sources_ref[...], jnp.concatenate(shift, axis=0)], axis=1)
        ones = ones_for(ROWS)
        for at in range(0, width, ROWS):
            scores_ref = score_refs[at // ROWS % len(score_refs)]
            scores_ref[...] = product(jnp.concatenate([targets_ref[at : at + ROWS, :], ones], axis=1), cols)
            for block in range(0, ROWS, LANES):
                peaks, totals = [], []
                for row in range(block, block + LANES, 8):
                    scores = scores_ref[row : row + 8, :]
                    pieces = [scores[:, lane : lane + LANES] for lane in range(0, count, LANES)]
                    peak = tree(pieces, jnp.maximum)
                    pieces = [jnp.exp2((piece - peak) * SCALE) for piece in pieces]
                    plan_ref[at + row : at + row + 8, :] = jnp.concatenate(pieces, axis=1)
                    peaks.append(peak * SCALE)
                    totals.append(tree(pieces, jnp.add))
                peak = jnp.concatenate(peaks, axis=0)
                top = jnp.max(peak, axis=1, keepdims=True)
                reach = jnp.exp2(peak - top)
                reach_ref[at + block : at + block + LANES, :] = reach
                total = jnp.sum((jnp.concatenate(totals, axis=0) * reach).T, axis=0, keepdims=True)
                index = (at + block) // LANES
                top_ref[index : index + 1, :] = to_row(top, mask)
                out_ref[index : index + 1, :] = top_ref[index : index + 1, :] + jnp.log2(total)

    return pl.pallas_call(
        kernel,
        out_shape=(
            pltpu.VMEM((width, count), F32),
            pltpu.VMEM((width, LANES), F32),
            rows_of(width),
            rows_of(width),
            rows_of(count),
        ),
        in_specs=[VMEM] * 4,
        out_specs=(VMEM,) * 5,
        scratch_shapes=[pltpu.VMEM((ROWS, count), F32)] * 2,
        compiler_params=params(),
        name="first_columns",
    )(pin(sources), pin(targets), parts, log_mass)


def later_rows(plan, reach, top, log_mass, parts):
    width, count = plan.shape
    rows = width // LANES

    def kernel(plan_ref, reach_ref, top_ref, log_ref, *refs):
        part_refs, out_ref = refs[:-1], refs[-1]
        weight = jnp.exp2(log_ref[...] + (top_ref[...] - log_sum([ref[...] for ref in part_refs])))
        mask = diagonal()
        totals = [jnp.zeros((8, count), F32)] * 2
        for block in range(rows):
            at = block * LANES
            factors = reach_ref[at : at + LANES, :] * to_column(weight[block : block + 1, :], mask)
            for step, row in enumerate(range(0, LANES, 8)):
                factor = jnp.concatenate([factors[row : row + 8, :]] * (count // LANES), axis=1)
                totals[step % 2] = totals[step % 2] + plan_ref[at + row : at + row + 8, :] * factor
        total = totals[0] + totals[1]
        fold_into(out_ref, jnp.sum(total, axis=0, keepdims=True))

    return pl.pallas_call(
        kernel,
        out_shape=rows_of(count),
        in_specs=[VMEM] * (4 + len(parts)),
        out_specs=VMEM,
        compiler_params=params(),
        name="later_rows",
    )(pin(plan), pin(reach), top, log_mass, *parts)


def later_columns(plan, reach, top, parts, log_mass, lse, half, last):
    width, count = plan.shape

    def kernel(plan_ref, reach_ref, top_ref, parts_ref, log_ref, lse_ref, half_ref, out_ref, *potential_refs):
        factor = log_ref[...] - jnp.log2(tree([parts_ref[i] for i in range(parts.shape[0])], jnp.add))
        for ref in potential_refs:
            ref[...] = half_ref[...] + UNIT * (factor - lse_ref[...])
        factor = unfold(jnp.exp2(factor))
        factors = [factor[:, lane : lane + LANES] for lane in range(0, count, LANES)]
        for at in range(0, width, LANES):
            totals = []
            for row in range(at, at + LANES, 8):
                plan = plan_ref[row : row + 8, :]
                totals.append(tree([plan[:, i * LANES : (i + 1) * LANES] * factors[i] for i in range(count // LANES)], jnp.add))
            total = jnp.concatenate(totals, axis=0) * reach_ref[at : at + LANES, :]
            index = at // LANES
            total = jnp.log2(jnp.sum(total.T, axis=0, keepdims=True))
            out_ref[index : index + 1, :] = top_ref[index : index + 1, :] + total

    return pl.pallas_call(
        kernel,
        out_shape=(rows_of(width),) + (rows_of(count),) * last,
        in_specs=[VMEM] * 7,
        out_specs=(VMEM,) * (1 + last),
        compiler_params=params(),
        name="later_columns",
    )(pin(plan), pin(reach), top, parts, log_mass, lse, half)


def levels_of(size):
    bits = size.bit_length() - 1
    out = []
    while bits > 0:
        take = 2 if bits % 2 == 0 else 1
        bits -= take
        out.append([step << bits for step in range(1, 1 << take)])
    return out


def swap(value, axes, size, distance):
    return lax.ppermute(value, axes, [(i, i ^ distance) for i in range(size)])


def swap_all(value, axes, size):
    values = [value]
    for distances in levels_of(size):
        got = {d: [swap(value, axes, size, d) for value in values] for d in reversed(distances)}
        values = [part for i in range(len(values)) for part in [values[i]] + [got[d][i] for d in distances]]
    return values


def share(value, size):
    copies = jnp.broadcast_to(value[None], (size,) + value.shape)
    return lax.all_to_all(copies, ("z", "x"), 0, 0, tiled=True)


def half_norm(points):
    values = points.astype(F32)
    return 0.5 * jnp.sum(values * values, axis=1)


def make_local(n_src, n_z, n_x):
    near, n_near = ("src", "core"), n_src * CORES
    n_far = n_z * n_x

    def local(source_points, target_points, source_mass, target_mass):
        core, x = lax.axis_index("core"), lax.axis_index("x")
        place = jnp.stack([lax.axis_index("src"), core, x]).astype(jnp.int32)
        along = lax.axis_index("z").astype(jnp.int32).reshape(1)
        part = source_points.shape[0]
        a = source_mass.reshape(n_z, n_x, CORES, part)
        a = lax.dynamic_index_in_dim(a, core, axis=2, keepdims=False).swapaxes(0, 1).reshape(-1, LANES)
        blocks = swap_all(target_points, "src", n_src)[1:]
        three, two, one = [swap(source_points, "z", n_z, d) for d in (3, 2, 1)]
        mine, packed, b, a = ready(source_points, target_points, target_mass.reshape(-1, LANES), a)
        laid = lay(along, three, 3, n_z)
        packed = swap_all(packed, "core", CORES)
        blocks = blocks + [swap(block, "core", CORES, 1) for block in blocks]
        groups = swap_all(pack(along, [mine, one, two], laid), "x", n_x)
        place, a = lax.optimization_barrier((place, a))
        targets, offsets, b, first = first_rows(place, b, packed, blocks, groups[0])
        own, sources = other_rows(place, targets, offsets, first, groups)
        plan, reach, top, own, row_lse = first_columns(sources, targets, share(own, n_far), a)
        early_x, early_y, own = lax.optimization_barrier((sources, targets, own))
        half_x, half_y = half_norm(early_x).reshape(-1, LANES), half_norm(early_y).reshape(-1, LANES)
        parts = swap_all(own, near, n_near)
        half_x, half_y, *parts = lax.optimization_barrier((half_x, half_y, *parts))
        for step in range(1, ITERS):
            rows = later_rows(plan, reach, top, b, parts)
            own, *potential = later_columns(plan, reach, top, share(rows, n_far), a, row_lse, half_x, step == ITERS - 1)
            parts = swap_all(own, near, n_near)
        mine, other = swap_all(potential[0].reshape(n_x, n_z, part), "core", CORES)
        first, second = jnp.where(core == 0, mine, other), jnp.where(core == 0, other, mine)
        source_potential = jnp.stack([first, second], axis=2).swapaxes(0, 1).reshape(-1)
        target_potential = half_y - UNIT * log_sum(parts)
        target_potential = target_potential.reshape(CORES, -1)
        target_potential = lax.dynamic_index_in_dim(target_potential, core, axis=0, keepdims=False)
        return source_potential, target_potential

    return local


def solution(mesh):
    n_src, n_tgt = mesh.shape["src"], mesh.shape["tgt"]
    n_z = 4
    n_x = n_tgt // (n_z * CORES)
    split = Mesh(mesh.devices.reshape(n_src, n_z, n_x, CORES), ("src", "z", "x", "core"))
    tgt = ("z", "x", "core")
    placed = (P(("src", *tgt), None), P((*tgt, "src"), None), P("src"), P(tgt))
    return jax.shard_map(
        make_local(n_src, n_z, n_x),
        mesh=split,
        in_specs=placed,
        out_specs=(P("src"), P(tgt)),
        check_vma=False,
    )
```

```python
import math

import jax
import jax.numpy as jnp
from jax import lax
from jax.experimental import pallas as pl
from jax.experimental.pallas import tpu as pltpu
from jax.sharding import Mesh, PartitionSpec as P

ITERS = 3
EPS = 0.05
SCALE = 1.0 / (EPS * math.log(2.0))
UNIT = EPS * math.log(2.0)
LANES = 128
CORES = 2
PIECES = 3
ROWS = 512
F32 = jnp.float32
VMEM = pl.BlockSpec(memory_space=pltpu.VMEM)
SMEM = pl.BlockSpec(memory_space=pltpu.SMEM)


def params(limit=24):
    return pltpu.CompilerParams(vmem_limit_bytes=limit * 1024 * 1024)


def pin(value):
    return pltpu.with_memory_space_constraint(value, pltpu.VMEM)


def rows_of(count):
    return jax.ShapeDtypeStruct((count // LANES, LANES), F32)


def diagonal():
    shape = (LANES, LANES)
    return lax.broadcasted_iota(jnp.int32, shape, 0) == lax.broadcasted_iota(jnp.int32, shape, 1)


def to_column(row, mask):
    return jnp.sum(jnp.where(mask, jnp.broadcast_to(row, mask.shape), 0.0), axis=1, keepdims=True)


def to_row(column, mask):
    return jnp.sum(jnp.where(mask, jnp.broadcast_to(column, mask.shape), 0.0), axis=0, keepdims=True)


def unfold(value):
    return jnp.concatenate([value[i : i + 1, :] for i in range(value.shape[0])], axis=1)


def fold_into(ref, value):
    for row in range(ref.shape[0]):
        ref[row : row + 1, :] = value[:, row * LANES : (row + 1) * LANES]


def tree(values, join):
    while len(values) > 1:
        values = [join(values[i], values[i + 1]) for i in range(0, len(values), 2)]
    return values[0]


def log_sum(values):
    peak = tree(values, jnp.maximum)
    return peak + jnp.log2(tree([jnp.exp2(value - peak) for value in values], jnp.add))


def product(rows, cols):
    return lax.dot_general(rows, cols, (((1,), (1,)), ((), ())), preferred_element_type=F32)


def ready(sources, targets, mass, source_mass):
    part, chunk = targets.shape[0], mass.shape[0]
    anywhere = pl.BlockSpec(memory_space=pl.ANY)

    def kernel(sources_ref, targets_ref, mass_ref, source_ref, sources_out, packed_ref, mass_out, source_out, *sems):
        copies = [
            pltpu.make_async_copy(mass_ref, mass_out, sems[0]),
            pltpu.make_async_copy(targets_ref, packed_ref.at[:part], sems[1]),
            pltpu.make_async_copy(sources_ref, sources_out, sems[2]),
        ]
        for copy in copies:
            copy.start()
        source_out[...] = jnp.log2(source_ref[...])
        copies[0].wait()
        value, pieces = mass_out[...], []
        for step in range(PIECES):
            pieces.append(value.astype(jnp.bfloat16).astype(F32))
            value = value - pieces[-1]
        pieces.append(jnp.zeros_like(value))
        packed_ref[part:, :] = jnp.concatenate(pieces, axis=0).astype(jnp.bfloat16)
        copies[1].wait()
        copies[2].wait()

    return pl.pallas_call(
        kernel,
        out_shape=(
            pltpu.VMEM(sources.shape, jnp.bfloat16),
            pltpu.VMEM((part + (PIECES + 1) * chunk, LANES), jnp.bfloat16),
            pltpu.VMEM(mass.shape, F32),
            pltpu.VMEM(source_mass.shape, F32),
        ),
        in_specs=[anywhere, anywhere, anywhere, VMEM],
        out_specs=(VMEM,) * 4,
        scratch_shapes=[pltpu.SemaphoreType.DMA] * 3,
        compiler_params=params(),
        cost_estimate=pl.CostEstimate(flops=1 << 20, bytes_accessed=1 << 20, transcendentals=0),
        name="ready",
    )(*[pltpu.with_memory_space_constraint(value, pltpu.HBM) for value in (sources, targets, mass)], source_mass)


def lay(place, block, step, count):
    part = block.shape[0]

    def kernel(place_ref, block_ref, out_ref):
        start = pl.multiple_of(jnp.bitwise_xor(place_ref[0], step) * part, part)
        out_ref[pl.ds(start, part), :] = block_ref[...]

    return pl.pallas_call(
        kernel,
        out_shape=pltpu.VMEM((count * part, LANES), jnp.bfloat16),
        in_specs=[SMEM, VMEM],
        out_specs=VMEM,
        compiler_params=params(),
        cost_estimate=pl.CostEstimate(flops=1 << 20, bytes_accessed=1 << 20, transcendentals=0),
        name="lay",
    )(place, block)


def pack(place, blocks, laid):
    part = blocks[0].shape[0]

    def kernel(place_ref, *refs):
        out_ref = refs[-1]
        for step in range(len(blocks)):
            start = pl.multiple_of(jnp.bitwise_xor(place_ref[0], step) * part, part)
            out_ref[pl.ds(start, part), :] = refs[step][...]

    return pl.pallas_call(
        kernel,
        out_shape=pltpu.VMEM(laid.shape, jnp.bfloat16),
        in_specs=[SMEM] + [VMEM] * (len(blocks) + 1),
        out_specs=VMEM,
        input_output_aliases={1 + len(blocks): 0},
        compiler_params=params(),
        cost_estimate=pl.CostEstimate(flops=1 << 20, bytes_accessed=1 << 18, transcendentals=0),
        name="pack",
    )(place, *blocks, laid)


def pieces_of(value):
    lane = lax.broadcasted_iota(jnp.int32, (value.shape[0], LANES), 1)
    tile = jnp.zeros((value.shape[0], LANES), F32)
    for step in range(PIECES):
        piece = value.astype(jnp.bfloat16).astype(F32)
        tile = jnp.where(lane == step, piece, tile)
        value = value - piece
    return tile.astype(jnp.bfloat16)


def ones_for(rows):
    lane = lax.broadcasted_iota(jnp.int32, (rows, LANES), 1)
    return jnp.where(lane < PIECES, 1.0, 0.0).astype(jnp.bfloat16)


class Rows:
    def __init__(self, count):
        self.peak = jnp.full((8, count), -1e30, F32)
        self.total = jnp.zeros((8, count), F32)

    def add(self, scores_ref):
        tops = self.peak
        for row in range(0, ROWS, 8):
            tops = jnp.maximum(tops, scores_ref[row : row + 8, :])
        self.total = self.total * jnp.exp2((self.peak - tops) * SCALE)
        self.peak = tops
        for row in range(0, ROWS, 8):
            self.total = self.total + jnp.exp2((scores_ref[row : row + 8, :] - tops) * SCALE)

    def lse(self):
        widest = jnp.max(self.peak, axis=0, keepdims=True)
        total = jnp.sum(self.total * jnp.exp2((self.peak - widest) * SCALE), axis=0, keepdims=True)
        return widest * SCALE + jnp.log2(total)


def first_rows(place, mass, packed, blocks, sources):
    count, chunk = sources.shape[0], mass.shape[0]
    n_src = len(blocks) // CORES + 1
    part = blocks[0].shape[0]
    width = CORES * n_src * part

    def kernel(place_ref, mass_ref, sources_ref, *refs):
        own_ref, other_ref, block_refs = refs[0], refs[1], refs[2 : 2 + len(blocks)]
        targets_ref, offset_ref, full_ref, out_ref, *score_refs = refs[2 + len(blocks) :]
        src, core = place_ref[0], place_ref[1]
        full_ref[pl.ds(pl.multiple_of(core * chunk, chunk), chunk), :] = jnp.log2(mass_ref[...])
        parts = [other_ref[part + i * chunk : part + (i + 1) * chunk, :].astype(F32) for i in range(PIECES)]
        start = pl.multiple_of(jnp.bitwise_xor(core, 1) * chunk, chunk)
        full_ref[pl.ds(start, chunk), :] = jnp.log2(parts[0] + (parts[1] + parts[2]))
        for dc in range(CORES):
            for ds in range(n_src):
                index = jnp.bitwise_xor(core, dc) * n_src + jnp.bitwise_xor(src, ds)
                start = pl.multiple_of(index * part, part)
                ref = refs[dc] if ds == 0 else block_refs[dc * (n_src - 1) + ds - 1]
                targets_ref[pl.ds(start, part), :] = ref[:part, :]
        mask = diagonal()
        log_mass = full_ref[...] * (1.0 / SCALE)
        cols = jnp.concatenate([sources_ref[...], ones_for(count)], axis=1)
        rows = Rows(count)
        for at in range(0, width, ROWS):
            scores_ref = score_refs[at // ROWS % len(score_refs)]
            for row in range(at, at + ROWS, LANES):
                values = targets_ref[row : row + LANES, :].astype(F32)
                half = 0.5 * jnp.sum(values * values, axis=1, keepdims=True)
                block = row // LANES
                offset_ref[row : row + LANES, :] = pieces_of(to_column(log_mass[block : block + 1, :], mask) - half)
            scores_ref[...] = product(jnp.concatenate([targets_ref[at : at + ROWS, :], offset_ref[at : at + ROWS, :]], axis=1), cols)
            rows.add(scores_ref)
        fold_into(out_ref, rows.lse())

    return pl.pallas_call(
        kernel,
        out_shape=(
            pltpu.VMEM((width, LANES), jnp.bfloat16),
            pltpu.VMEM((width, LANES), jnp.bfloat16),
            rows_of(width),
            rows_of(count),
        ),
        in_specs=[SMEM] + [VMEM] * (4 + len(blocks)),
        out_specs=(VMEM,) * 4,
        scratch_shapes=[pltpu.VMEM((ROWS, count), F32)] * 2,
        compiler_params=params(),
        cost_estimate=pl.CostEstimate(flops=1 << 29, bytes_accessed=1 << 20, transcendentals=1 << 20),
        name="first_rows",
    )(place, mass, pin(sources), *[pin(value) for value in packed], *[pin(value) for value in blocks])


def other_rows(place, targets, offsets, first, groups):
    mine, groups = groups[0], groups[1:]
    width, count, each = targets.shape[0], sum(group.shape[0] for group in groups), mine.shape[0] // LANES

    def kernel(place_ref, targets_ref, offset_ref, first_ref, mine_ref, *refs):
        group_refs, (out_ref, sources_ref, *score_refs) = refs[: len(groups)], refs[len(groups) :]
        cols = jnp.concatenate([ref[...] for ref in group_refs], axis=0)
        cols = jnp.concatenate([cols, ones_for(count)], axis=1)
        rows = Rows(count)
        for at in range(0, width, ROWS):
            scores_ref = score_refs[at // ROWS % len(score_refs)]
            scores_ref[...] = product(jnp.concatenate([targets_ref[at : at + ROWS, :], offset_ref[at : at + ROWS, :]], axis=1), cols)
            rows.add(scores_ref)
        lse = rows.lse()
        for step in range(len(groups) + 1):
            start = jnp.bitwise_xor(place_ref[2], step) * each
            ref = group_refs[step - 1] if step else mine_ref
            sources_ref[pl.ds(pl.multiple_of(start * LANES, each * LANES), each * LANES), :] = ref[...]
            for row in range(each):
                at = ((step - 1) * each + row) * LANES
                out_ref[pl.ds(start + row, 1), :] = first_ref[row : row + 1, :] if step == 0 else lse[:, at : at + LANES]

    return pl.pallas_call(
        kernel,
        out_shape=(rows_of(count + each * LANES), pltpu.VMEM((count + each * LANES, LANES), jnp.bfloat16)),
        in_specs=[SMEM] + [VMEM] * (3 + len(groups) + 1),
        out_specs=(VMEM,) * 2,
        scratch_shapes=[pltpu.VMEM((ROWS, count), F32)] * 2,
        compiler_params=params(),
        name="other_rows",
    )(place, pin(targets), pin(offsets), first, pin(mine), *groups)


def first_columns(sources, targets, parts, log_mass):
    count, width = sources.shape[0], targets.shape[0]

    def kernel(sources_ref, targets_ref, parts_ref, log_ref, plan_ref, reach_ref, top_ref, out_ref, lse_ref, *score_refs):
        lse = log_sum([parts_ref[i] for i in range(parts.shape[0])])
        lse_ref[...] = lse
        mask = diagonal()
        shift = (log_ref[...] - lse) * (1.0 / SCALE)
        shift = [pieces_of(to_column(shift[i : i + 1, :], mask)) for i in range(count // LANES)]
        cols = jnp.concatenate([sources_ref[...], jnp.concatenate(shift, axis=0)], axis=1)
        ones = ones_for(ROWS)
        for at in range(0, width, ROWS):
            scores_ref = score_refs[at // ROWS % len(score_refs)]
            scores_ref[...] = product(jnp.concatenate([targets_ref[at : at + ROWS, :], ones], axis=1), cols)
            for block in range(0, ROWS, LANES):
                peaks, totals = [], []
                for row in range(block, block + LANES, 8):
                    scores = scores_ref[row : row + 8, :]
                    pieces = [scores[:, lane : lane + LANES] for lane in range(0, count, LANES)]
                    peak = tree(pieces, jnp.maximum)
                    pieces = [jnp.exp2((piece - peak) * SCALE) for piece in pieces]
                    plan_ref[at + row : at + row + 8, :] = jnp.concatenate(pieces, axis=1)
                    peaks.append(peak * SCALE)
                    totals.append(tree(pieces, jnp.add))
                peak = jnp.concatenate(peaks, axis=0)
                top = jnp.max(peak, axis=1, keepdims=True)
                reach = jnp.exp2(peak - top)
                reach_ref[at + block : at + block + LANES, :] = reach
                total = jnp.sum((jnp.concatenate(totals, axis=0) * reach).T, axis=0, keepdims=True)
                index = (at + block) // LANES
                top_ref[index : index + 1, :] = to_row(top, mask)
                out_ref[index : index + 1, :] = top_ref[index : index + 1, :] + jnp.log2(total)

    return pl.pallas_call(
        kernel,
        out_shape=(
            pltpu.VMEM((width, count), F32),
            pltpu.VMEM((width, LANES), F32),
            rows_of(width),
            rows_of(width),
            rows_of(count),
        ),
        in_specs=[VMEM] * 4,
        out_specs=(VMEM,) * 5,
        scratch_shapes=[pltpu.VMEM((ROWS, count), F32)] * 2,
        compiler_params=params(),
        name="first_columns",
    )(pin(sources), pin(targets), parts, log_mass)


def later_rows(plan, reach, top, log_mass, parts):
    width, count = plan.shape
    rows = width // LANES

    def kernel(plan_ref, reach_ref, top_ref, log_ref, *refs):
        part_refs, out_ref = refs[:-1], refs[-1]
        weight = jnp.exp2(log_ref[...] + (top_ref[...] - log_sum([ref[...] for ref in part_refs])))
        mask = diagonal()
        total = jnp.zeros((8, count), F32)
        for block in range(rows):
            at = block * LANES
            factors = reach_ref[at : at + LANES, :] * to_column(weight[block : block + 1, :], mask)
            for row in range(0, LANES, 8):
                factor = jnp.concatenate([factors[row : row + 8, :]] * (count // LANES), axis=1)
                total = total + plan_ref[at + row : at + row + 8, :] * factor
        fold_into(out_ref, jnp.sum(total, axis=0, keepdims=True))

    return pl.pallas_call(
        kernel,
        out_shape=rows_of(count),
        in_specs=[VMEM] * (4 + len(parts)),
        out_specs=VMEM,
        compiler_params=params(),
        name="later_rows",
    )(pin(plan), pin(reach), top, log_mass, *parts)


def later_columns(plan, reach, top, parts, log_mass, lse, half, last):
    width, count = plan.shape

    def kernel(plan_ref, reach_ref, top_ref, parts_ref, log_ref, lse_ref, half_ref, out_ref, *potential_refs):
        factor = log_ref[...] - jnp.log2(tree([parts_ref[i] for i in range(parts.shape[0])], jnp.add))
        for ref in potential_refs:
            ref[...] = half_ref[...] + UNIT * (factor - lse_ref[...])
        factor = unfold(jnp.exp2(factor))
        factors = [factor[:, lane : lane + LANES] for lane in range(0, count, LANES)]
        for at in range(0, width, LANES):
            totals = []
            for row in range(at, at + LANES, 8):
                plan = plan_ref[row : row + 8, :]
                totals.append(tree([plan[:, i * LANES : (i + 1) * LANES] * factors[i] for i in range(count // LANES)], jnp.add))
            total = jnp.concatenate(totals, axis=0) * reach_ref[at : at + LANES, :]
            index = at // LANES
            total = jnp.log2(jnp.sum(total.T, axis=0, keepdims=True))
            out_ref[index : index + 1, :] = top_ref[index : index + 1, :] + total

    return pl.pallas_call(
        kernel,
        out_shape=(rows_of(width),) + (rows_of(count),) * last,
        in_specs=[VMEM] * 7,
        out_specs=(VMEM,) * (1 + last),
        compiler_params=params(),
        name="later_columns",
    )(pin(plan), pin(reach), top, parts, log_mass, lse, half)


def levels_of(size):
    bits = size.bit_length() - 1
    out = []
    while bits > 0:
        take = 2 if bits % 2 == 0 else 1
        bits -= take
        out.append([step << bits for step in range(1, 1 << take)])
    return out


def swap(value, axes, size, distance):
    return lax.ppermute(value, axes, [(i, i ^ distance) for i in range(size)])


def swap_all(value, axes, size):
    values = [value]
    for distances in levels_of(size):
        got = {d: [swap(value, axes, size, d) for value in values] for d in reversed(distances)}
        values = [part for i in range(len(values)) for part in [values[i]] + [got[d][i] for d in distances]]
    return values


def share(value, size):
    copies = jnp.broadcast_to(value[None], (size,) + value.shape)
    return lax.all_to_all(copies, ("z", "x"), 0, 0, tiled=True)


def half_norm(points):
    values = points.astype(F32)
    return 0.5 * jnp.sum(values * values, axis=1)


def make_local(n_src, n_z, n_x):
    near, n_near = ("src", "core"), n_src * CORES
    n_far = n_z * n_x

    def local(source_points, target_points, source_mass, target_mass):
        core, x = lax.axis_index("core"), lax.axis_index("x")
        place = jnp.stack([lax.axis_index("src"), core, x]).astype(jnp.int32)
        along = lax.axis_index("z").astype(jnp.int32).reshape(1)
        part = source_points.shape[0]
        a = source_mass.reshape(n_z, n_x, CORES, part)
        a = lax.dynamic_index_in_dim(a, core, axis=2, keepdims=False).swapaxes(0, 1).reshape(-1, LANES)
        blocks = swap_all(target_points, "src", n_src)[1:]
        three, two, one = [swap(source_points, "z", n_z, d) for d in (3, 2, 1)]
        mine, packed, b, a = ready(source_points, target_points, target_mass.reshape(-1, LANES), a)
        laid = lay(along, three, 3, n_z)
        packed = swap_all(packed, "core", CORES)
        blocks = blocks + [swap(block, "core", CORES, 1) for block in blocks]
        groups = swap_all(pack(along, [mine, one, two], laid), "x", n_x)
        place, a = lax.optimization_barrier((place, a))
        targets, offsets, b, first = first_rows(place, b, packed, blocks, groups[0])
        own, sources = other_rows(place, targets, offsets, first, groups)
        plan, reach, top, own, row_lse = first_columns(sources, targets, share(own, n_far), a)
        early_x, early_y, own = lax.optimization_barrier((sources, targets, own))
        half_x, half_y = half_norm(early_x).reshape(-1, LANES), half_norm(early_y).reshape(-1, LANES)
        parts = swap_all(own, near, n_near)
        half_x, half_y, *parts = lax.optimization_barrier((half_x, half_y, *parts))
        for step in range(1, ITERS):
            rows = later_rows(plan, reach, top, b, parts)
            own, *potential = later_columns(plan, reach, top, share(rows, n_far), a, row_lse, half_x, step == ITERS - 1)
            parts = swap_all(own, near, n_near)
        mine, other = swap_all(potential[0].reshape(n_x, n_z, part), "core", CORES)
        first, second = jnp.where(core == 0, mine, other), jnp.where(core == 0, other, mine)
        source_potential = jnp.stack([first, second], axis=2).swapaxes(0, 1).reshape(-1)
        target_potential = half_y - UNIT * log_sum(parts)
        target_potential = target_potential.reshape(CORES, -1)
        target_potential = lax.dynamic_index_in_dim(target_potential, core, axis=0, keepdims=False)
        return source_potential, target_potential

    return local


def solution(mesh):
    n_src, n_tgt = mesh.shape["src"], mesh.shape["tgt"]
    n_z = 4
    n_x = n_tgt // (n_z * CORES)
    split = Mesh(mesh.devices.reshape(n_src, n_z, n_x, CORES), ("src", "z", "x", "core"))
    tgt = ("z", "x", "core")
    placed = (P(("src", *tgt), None), P((*tgt, "src"), None), P("src"), P(tgt))
    return jax.shard_map(
        make_local(n_src, n_z, n_x),
        mesh=split,
        in_specs=placed,
        out_specs=(P("src"), P(tgt)),
        check_vma=False,
    )
```

```python
import math

import jax
import jax.numpy as jnp
from jax import lax
from jax.experimental import pallas as pl
from jax.experimental.pallas import tpu as pltpu
from jax.sharding import Mesh, PartitionSpec as P

ITERS = 3
EPS = 0.05
SCALE = 1.0 / (EPS * math.log(2.0))
UNIT = EPS * math.log(2.0)
LANES = 128
CORES = 2
PIECES = 3
ROWS = 256
F32 = jnp.float32
VMEM = pl.BlockSpec(memory_space=pltpu.VMEM)
SMEM = pl.BlockSpec(memory_space=pltpu.SMEM)


def params(limit=24):
    return pltpu.CompilerParams(vmem_limit_bytes=limit * 1024 * 1024)


def pin(value):
    return pltpu.with_memory_space_constraint(value, pltpu.VMEM)


def rows_of(count):
    return jax.ShapeDtypeStruct((count // LANES, LANES), F32)


def diagonal():
    shape = (LANES, LANES)
    return lax.broadcasted_iota(jnp.int32, shape, 0) == lax.broadcasted_iota(jnp.int32, shape, 1)


def to_column(row, mask):
    return jnp.sum(jnp.where(mask, jnp.broadcast_to(row, mask.shape), 0.0), axis=1, keepdims=True)


def to_row(column, mask):
    return jnp.sum(jnp.where(mask, jnp.broadcast_to(column, mask.shape), 0.0), axis=0, keepdims=True)


def unfold(value):
    return jnp.concatenate([value[i : i + 1, :] for i in range(value.shape[0])], axis=1)


def fold_into(ref, value):
    for row in range(ref.shape[0]):
        ref[row : row + 1, :] = value[:, row * LANES : (row + 1) * LANES]


def tree(values, join):
    while len(values) > 1:
        values = [join(values[i], values[i + 1]) for i in range(0, len(values), 2)]
    return values[0]


def log_sum(values):
    peak = tree(values, jnp.maximum)
    return peak + jnp.log2(tree([jnp.exp2(value - peak) for value in values], jnp.add))


def product(rows, cols):
    return lax.dot_general(rows, cols, (((1,), (1,)), ((), ())), preferred_element_type=F32)


def ready(sources, targets, mass, source_mass):
    part, chunk = targets.shape[0], mass.shape[0]
    anywhere = pl.BlockSpec(memory_space=pl.ANY)

    def kernel(sources_ref, targets_ref, mass_ref, source_ref, sources_out, packed_ref, mass_out, source_out, *sems):
        copies = [
            pltpu.make_async_copy(mass_ref, mass_out, sems[0]),
            pltpu.make_async_copy(targets_ref, packed_ref.at[:part], sems[1]),
            pltpu.make_async_copy(sources_ref, sources_out, sems[2]),
        ]
        for copy in copies:
            copy.start()
        source_out[...] = jnp.log2(source_ref[...])
        copies[0].wait()
        value, pieces = mass_out[...], []
        for step in range(PIECES):
            pieces.append(value.astype(jnp.bfloat16).astype(F32))
            value = value - pieces[-1]
        pieces.append(jnp.zeros_like(value))
        packed_ref[part:, :] = jnp.concatenate(pieces, axis=0).astype(jnp.bfloat16)
        copies[1].wait()
        copies[2].wait()

    return pl.pallas_call(
        kernel,
        out_shape=(
            pltpu.VMEM(sources.shape, jnp.bfloat16),
            pltpu.VMEM((part + (PIECES + 1) * chunk, LANES), jnp.bfloat16),
            pltpu.VMEM(mass.shape, F32),
            pltpu.VMEM(source_mass.shape, F32),
        ),
        in_specs=[anywhere, anywhere, anywhere, VMEM],
        out_specs=(VMEM,) * 4,
        scratch_shapes=[pltpu.SemaphoreType.DMA] * 3,
        compiler_params=params(),
        cost_estimate=pl.CostEstimate(flops=1 << 20, bytes_accessed=1 << 20, transcendentals=0),
        name="ready",
    )(*[pltpu.with_memory_space_constraint(value, pltpu.HBM) for value in (sources, targets, mass)], source_mass)


def lay(place, block, step, count):
    part = block.shape[0]

    def kernel(place_ref, block_ref, out_ref):
        start = pl.multiple_of(jnp.bitwise_xor(place_ref[0], step) * part, part)
        out_ref[pl.ds(start, part), :] = block_ref[...]

    return pl.pallas_call(
        kernel,
        out_shape=pltpu.VMEM((count * part, LANES), jnp.bfloat16),
        in_specs=[SMEM, VMEM],
        out_specs=VMEM,
        compiler_params=params(),
        cost_estimate=pl.CostEstimate(flops=1 << 20, bytes_accessed=1 << 20, transcendentals=0),
        name="lay",
    )(place, block)


def pack(place, blocks, laid):
    part = blocks[0].shape[0]

    def kernel(place_ref, *refs):
        out_ref = refs[-1]
        for step in range(len(blocks)):
            start = pl.multiple_of(jnp.bitwise_xor(place_ref[0], step) * part, part)
            out_ref[pl.ds(start, part), :] = refs[step][...]

    return pl.pallas_call(
        kernel,
        out_shape=pltpu.VMEM(laid.shape, jnp.bfloat16),
        in_specs=[SMEM] + [VMEM] * (len(blocks) + 1),
        out_specs=VMEM,
        input_output_aliases={1 + len(blocks): 0},
        compiler_params=params(),
        cost_estimate=pl.CostEstimate(flops=1 << 20, bytes_accessed=1 << 18, transcendentals=0),
        name="pack",
    )(place, *blocks, laid)


def pieces_of(value):
    lane = lax.broadcasted_iota(jnp.int32, (value.shape[0], LANES), 1)
    tile = jnp.zeros((value.shape[0], LANES), F32)
    for step in range(PIECES):
        piece = value.astype(jnp.bfloat16).astype(F32)
        tile = jnp.where(lane == step, piece, tile)
        value = value - piece
    return tile.astype(jnp.bfloat16)


def ones_for(rows):
    lane = lax.broadcasted_iota(jnp.int32, (rows, LANES), 1)
    return jnp.where(lane < PIECES, 1.0, 0.0).astype(jnp.bfloat16)


class Rows:
    def __init__(self, count):
        self.peak = jnp.full((8, count), -1e30, F32)
        self.total = jnp.zeros((8, count), F32)

    def add(self, scores_ref):
        tops = self.peak
        for row in range(0, ROWS, 8):
            tops = jnp.maximum(tops, scores_ref[row : row + 8, :])
        self.total = self.total * jnp.exp2((self.peak - tops) * SCALE)
        self.peak = tops
        for row in range(0, ROWS, 8):
            self.total = self.total + jnp.exp2((scores_ref[row : row + 8, :] - tops) * SCALE)

    def lse(self):
        widest = jnp.max(self.peak, axis=0, keepdims=True)
        total = jnp.sum(self.total * jnp.exp2((self.peak - widest) * SCALE), axis=0, keepdims=True)
        return widest * SCALE + jnp.log2(total)


def first_rows(place, mass, packed, blocks, sources):
    count, chunk = sources.shape[0], mass.shape[0]
    n_src = len(blocks) // CORES + 1
    part = blocks[0].shape[0]
    width = CORES * n_src * part

    def kernel(place_ref, mass_ref, sources_ref, *refs):
        own_ref, other_ref, block_refs = refs[0], refs[1], refs[2 : 2 + len(blocks)]
        targets_ref, offset_ref, full_ref, out_ref, *score_refs = refs[2 + len(blocks) :]
        src, core = place_ref[0], place_ref[1]
        full_ref[pl.ds(pl.multiple_of(core * chunk, chunk), chunk), :] = jnp.log2(mass_ref[...])
        parts = [other_ref[part + i * chunk : part + (i + 1) * chunk, :].astype(F32) for i in range(PIECES)]
        start = pl.multiple_of(jnp.bitwise_xor(core, 1) * chunk, chunk)
        full_ref[pl.ds(start, chunk), :] = jnp.log2(parts[0] + (parts[1] + parts[2]))
        for dc in range(CORES):
            for ds in range(n_src):
                index = jnp.bitwise_xor(core, dc) * n_src + jnp.bitwise_xor(src, ds)
                start = pl.multiple_of(index * part, part)
                ref = refs[dc] if ds == 0 else block_refs[dc * (n_src - 1) + ds - 1]
                targets_ref[pl.ds(start, part), :] = ref[:part, :]
        mask = diagonal()
        log_mass = full_ref[...] * (1.0 / SCALE)
        cols = jnp.concatenate([sources_ref[...], ones_for(count)], axis=1)
        rows = Rows(count)
        for at in range(0, width, ROWS):
            scores_ref = score_refs[at // ROWS % len(score_refs)]
            for row in range(at, at + ROWS, LANES):
                values = targets_ref[row : row + LANES, :].astype(F32)
                half = 0.5 * jnp.sum(values * values, axis=1, keepdims=True)
                block = row // LANES
                offset_ref[row : row + LANES, :] = pieces_of(to_column(log_mass[block : block + 1, :], mask) - half)
            scores_ref[...] = product(jnp.concatenate([targets_ref[at : at + ROWS, :], offset_ref[at : at + ROWS, :]], axis=1), cols)
            rows.add(scores_ref)
        fold_into(out_ref, rows.lse())

    return pl.pallas_call(
        kernel,
        out_shape=(
            pltpu.VMEM((width, LANES), jnp.bfloat16),
            pltpu.VMEM((width, LANES), jnp.bfloat16),
            rows_of(width),
            rows_of(count),
        ),
        in_specs=[SMEM] + [VMEM] * (4 + len(blocks)),
        out_specs=(VMEM,) * 4,
        scratch_shapes=[pltpu.VMEM((ROWS, count), F32)] * 2,
        compiler_params=params(),
        cost_estimate=pl.CostEstimate(flops=1 << 29, bytes_accessed=1 << 20, transcendentals=1 << 20),
        name="first_rows",
    )(place, mass, pin(sources), *[pin(value) for value in packed], *[pin(value) for value in blocks])


def other_rows(place, targets, offsets, first, groups):
    mine, groups = groups[0], groups[1:]
    width, count, each = targets.shape[0], sum(group.shape[0] for group in groups), mine.shape[0] // LANES

    def kernel(place_ref, targets_ref, offset_ref, first_ref, mine_ref, *refs):
        group_refs, (out_ref, sources_ref, *score_refs) = refs[: len(groups)], refs[len(groups) :]
        cols = jnp.concatenate([ref[...] for ref in group_refs], axis=0)
        cols = jnp.concatenate([cols, ones_for(count)], axis=1)
        rows = Rows(count)
        for at in range(0, width, ROWS):
            scores_ref = score_refs[at // ROWS % len(score_refs)]
            scores_ref[...] = product(jnp.concatenate([targets_ref[at : at + ROWS, :], offset_ref[at : at + ROWS, :]], axis=1), cols)
            rows.add(scores_ref)
        lse = rows.lse()
        for step in range(len(groups) + 1):
            start = jnp.bitwise_xor(place_ref[2], step) * each
            ref = group_refs[step - 1] if step else mine_ref
            sources_ref[pl.ds(pl.multiple_of(start * LANES, each * LANES), each * LANES), :] = ref[...]
            for row in range(each):
                at = ((step - 1) * each + row) * LANES
                out_ref[pl.ds(start + row, 1), :] = first_ref[row : row + 1, :] if step == 0 else lse[:, at : at + LANES]

    return pl.pallas_call(
        kernel,
        out_shape=(rows_of(count + each * LANES), pltpu.VMEM((count + each * LANES, LANES), jnp.bfloat16)),
        in_specs=[SMEM] + [VMEM] * (3 + len(groups) + 1),
        out_specs=(VMEM,) * 2,
        scratch_shapes=[pltpu.VMEM((ROWS, count), F32)] * 2,
        compiler_params=params(),
        name="other_rows",
    )(place, pin(targets), pin(offsets), first, pin(mine), *groups)


def first_columns(sources, targets, parts, log_mass):
    count, width = sources.shape[0], targets.shape[0]

    def kernel(sources_ref, targets_ref, parts_ref, log_ref, plan_ref, reach_ref, top_ref, out_ref, lse_ref, *score_refs):
        lse = log_sum([parts_ref[i] for i in range(parts.shape[0])])
        lse_ref[...] = lse
        mask = diagonal()
        shift = (log_ref[...] - lse) * (1.0 / SCALE)
        shift = [pieces_of(to_column(shift[i : i + 1, :], mask)) for i in range(count // LANES)]
        cols = jnp.concatenate([sources_ref[...], jnp.concatenate(shift, axis=0)], axis=1)
        ones = ones_for(ROWS)
        for at in range(0, width, ROWS):
            scores_ref = score_refs[at // ROWS % len(score_refs)]
            scores_ref[...] = product(jnp.concatenate([targets_ref[at : at + ROWS, :], ones], axis=1), cols)
            for block in range(0, ROWS, LANES):
                peaks, totals = [], []
                for row in range(block, block + LANES, 8):
                    scores = scores_ref[row : row + 8, :]
                    pieces = [scores[:, lane : lane + LANES] for lane in range(0, count, LANES)]
                    peak = tree(pieces, jnp.maximum)
                    pieces = [jnp.exp2((piece - peak) * SCALE) for piece in pieces]
                    plan_ref[at + row : at + row + 8, :] = jnp.concatenate(pieces, axis=1)
                    peaks.append(peak * SCALE)
                    totals.append(tree(pieces, jnp.add))
                peak = jnp.concatenate(peaks, axis=0)
                top = jnp.max(peak, axis=1, keepdims=True)
                reach = jnp.exp2(peak - top)
                reach_ref[at + block : at + block + LANES, :] = reach
                total = jnp.sum((jnp.concatenate(totals, axis=0) * reach).T, axis=0, keepdims=True)
                index = (at + block) // LANES
                top_ref[index : index + 1, :] = to_row(top, mask)
                out_ref[index : index + 1, :] = top_ref[index : index + 1, :] + jnp.log2(total)

    return pl.pallas_call(
        kernel,
        out_shape=(
            pltpu.VMEM((width, count), F32),
            pltpu.VMEM((width, LANES), F32),
            rows_of(width),
            rows_of(width),
            rows_of(count),
        ),
        in_specs=[VMEM] * 4,
        out_specs=(VMEM,) * 5,
        scratch_shapes=[pltpu.VMEM((ROWS, count), F32)] * 2,
        compiler_params=params(),
        name="first_columns",
    )(pin(sources), pin(targets), parts, log_mass)


def later_rows(plan, reach, top, log_mass, parts):
    width, count = plan.shape
    rows = width // LANES

    def kernel(plan_ref, reach_ref, top_ref, log_ref, *refs):
        part_refs, out_ref = refs[:-1], refs[-1]
        weight = jnp.exp2(log_ref[...] + (top_ref[...] - log_sum([ref[...] for ref in part_refs])))
        mask = diagonal()
        total = jnp.zeros((8, count), F32)
        for block in range(rows):
            at = block * LANES
            factors = reach_ref[at : at + LANES, :] * to_column(weight[block : block + 1, :], mask)
            for row in range(0, LANES, 8):
                factor = jnp.concatenate([factors[row : row + 8, :]] * (count // LANES), axis=1)
                total = total + plan_ref[at + row : at + row + 8, :] * factor
        fold_into(out_ref, jnp.sum(total, axis=0, keepdims=True))

    return pl.pallas_call(
        kernel,
        out_shape=rows_of(count),
        in_specs=[VMEM] * (4 + len(parts)),
        out_specs=VMEM,
        compiler_params=params(),
        name="later_rows",
    )(pin(plan), pin(reach), top, log_mass, *parts)


def later_columns(plan, reach, top, parts, log_mass, lse, half, last):
    width, count = plan.shape

    def kernel(plan_ref, reach_ref, top_ref, parts_ref, log_ref, lse_ref, half_ref, out_ref, *potential_refs):
        factor = log_ref[...] - jnp.log2(tree([parts_ref[i] for i in range(parts.shape[0])], jnp.add))
        for ref in potential_refs:
            ref[...] = half_ref[...] + UNIT * (factor - lse_ref[...])
        factor = unfold(jnp.exp2(factor))
        factors = [factor[:, lane : lane + LANES] for lane in range(0, count, LANES)]
        for at in range(0, width, LANES):
            totals = []
            for row in range(at, at + LANES, 8):
                plan = plan_ref[row : row + 8, :]
                totals.append(tree([plan[:, i * LANES : (i + 1) * LANES] * factors[i] for i in range(count // LANES)], jnp.add))
            total = jnp.concatenate(totals, axis=0) * reach_ref[at : at + LANES, :]
            index = at // LANES
            total = jnp.log2(jnp.sum(total.T, axis=0, keepdims=True))
            out_ref[index : index + 1, :] = top_ref[index : index + 1, :] + total

    return pl.pallas_call(
        kernel,
        out_shape=(rows_of(width),) + (rows_of(count),) * last,
        in_specs=[VMEM] * 7,
        out_specs=(VMEM,) * (1 + last),
        compiler_params=params(),
        name="later_columns",
    )(pin(plan), pin(reach), top, parts, log_mass, lse, half)


def levels_of(size):
    bits = size.bit_length() - 1
    out = []
    while bits > 0:
        take = 2 if bits % 2 == 0 else 1
        bits -= take
        out.append([step << bits for step in range(1, 1 << take)])
    return out


def swap(value, axes, size, distance):
    return lax.ppermute(value, axes, [(i, i ^ distance) for i in range(size)])


def swap_all(value, axes, size):
    values = [value]
    for distances in levels_of(size):
        got = {d: [swap(value, axes, size, d) for value in values] for d in reversed(distances)}
        values = [part for i in range(len(values)) for part in [values[i]] + [got[d][i] for d in distances]]
    return values


def share(value, n_z, n_x):
    walk = [z * n_x + (x if z % 2 == 0 else n_x - 1 - x) for z in range(n_z) for x in range(n_x)]
    if n_x == 2:
        walk = [z * n_x for z in range(n_z)] + [z * n_x + 1 for z in reversed(range(n_z))]
    copies = jnp.broadcast_to(value[None], (n_z * n_x,) + value.shape)
    return lax.all_to_all(copies, "far", 0, 0, axis_index_groups=[walk], tiled=True)


def half_norm(points):
    values = points.astype(F32)
    return 0.5 * jnp.sum(values * values, axis=1)


def make_local(n_src, n_z, n_x):
    near, n_near = ("src", "core"), n_src * CORES
    n_far = n_z * n_x

    def swap_x(value):
        return [value] + [swap(value, "far", n_far, dx) for dx in range(1, n_x)]

    def local(source_points, target_points, source_mass, target_mass):
        core, x = lax.axis_index("core"), (lax.axis_index("far") % n_x)
        place = jnp.stack([lax.axis_index("src"), core, x]).astype(jnp.int32)
        along = (lax.axis_index("far") // n_x).astype(jnp.int32).reshape(1)
        part = source_points.shape[0]
        a = source_mass.reshape(n_z, n_x, CORES, part)
        a = lax.dynamic_index_in_dim(a, core, axis=2, keepdims=False).swapaxes(0, 1).reshape(-1, LANES)
        blocks = swap_all(target_points, "src", n_src)[1:]
        three, two, one = [swap(source_points, "far", n_far, d * n_x) for d in (3, 2, 1)]
        mine, packed, b, a = ready(source_points, target_points, target_mass.reshape(-1, LANES), a)
        laid = lay(along, three, 3, n_z)
        packed = swap_all(packed, "core", CORES)
        blocks = blocks + [swap(block, "core", CORES, 1) for block in blocks]
        groups = swap_x(pack(along, [mine, one, two], laid))
        place, a = lax.optimization_barrier((place, a))
        targets, offsets, b, first = first_rows(place, b, packed, blocks, groups[0])
        own, sources = other_rows(place, targets, offsets, first, groups)
        plan, reach, top, own, row_lse = first_columns(sources, targets, share(own, n_z, n_x), a)
        early_x, early_y, own = lax.optimization_barrier((sources, targets, own))
        half_x, half_y = half_norm(early_x).reshape(-1, LANES), half_norm(early_y).reshape(-1, LANES)
        parts = swap_all(own, near, n_near)
        half_x, half_y, *parts = lax.optimization_barrier((half_x, half_y, *parts))
        for step in range(1, ITERS):
            rows = later_rows(plan, reach, top, b, parts)
            own, *potential = later_columns(plan, reach, top, share(rows, n_z, n_x), a, row_lse, half_x, step == ITERS - 1)
            parts = swap_all(own, near, n_near)
        mine, other = swap_all(potential[0].reshape(n_x, n_z, part), "core", CORES)
        first, second = jnp.where(core == 0, mine, other), jnp.where(core == 0, other, mine)
        source_potential = jnp.stack([first, second], axis=2).swapaxes(0, 1).reshape(-1)
        target_potential = half_y - UNIT * log_sum(parts)
        target_potential = target_potential.reshape(CORES, -1)
        target_potential = lax.dynamic_index_in_dim(target_potential, core, axis=0, keepdims=False)
        return source_potential, target_potential

    return local


def solution(mesh):
    n_src, n_tgt = mesh.shape["src"], mesh.shape["tgt"]
    n_z = 4
    n_x = n_tgt // (n_z * CORES)
    split = Mesh(mesh.devices.reshape(n_src, n_z * n_x, CORES), ("src", "far", "core"))
    tgt = ("far", "core")
    placed = (P(("src", *tgt), None), P((*tgt, "src"), None), P("src"), P(tgt))
    return jax.shard_map(
        make_local(n_src, n_z, n_x),
        mesh=split,
        in_specs=placed,
        out_specs=(P("src"), P(tgt)),
        check_vma=False,
    )
```

```python
import math

import jax
import jax.numpy as jnp
from jax import lax
from jax.experimental import pallas as pl
from jax.experimental.pallas import tpu as pltpu
from jax.sharding import Mesh, PartitionSpec as P

ITERS = 3
EPS = 0.05
SCALE = 1.0 / (EPS * math.log(2.0))
UNIT = EPS * math.log(2.0)
LANES = 128
CORES = 2
PIECES = 3
ROWS = 256
F32 = jnp.float32
VMEM = pl.BlockSpec(memory_space=pltpu.VMEM)
SMEM = pl.BlockSpec(memory_space=pltpu.SMEM)


def params(limit=24):
    return pltpu.CompilerParams(vmem_limit_bytes=limit * 1024 * 1024)


def pin(value):
    return pltpu.with_memory_space_constraint(value, pltpu.VMEM)


def rows_of(count):
    return jax.ShapeDtypeStruct((count // LANES, LANES), F32)


def diagonal():
    shape = (LANES, LANES)
    return lax.broadcasted_iota(jnp.int32, shape, 0) == lax.broadcasted_iota(jnp.int32, shape, 1)


def to_column(row, mask):
    return jnp.sum(jnp.where(mask, jnp.broadcast_to(row, mask.shape), 0.0), axis=1, keepdims=True)


def to_row(column, mask):
    return jnp.sum(jnp.where(mask, jnp.broadcast_to(column, mask.shape), 0.0), axis=0, keepdims=True)


def unfold(value):
    return jnp.concatenate([value[i : i + 1, :] for i in range(value.shape[0])], axis=1)


def fold_into(ref, value):
    for row in range(ref.shape[0]):
        ref[row : row + 1, :] = value[:, row * LANES : (row + 1) * LANES]


def tree(values, join):
    while len(values) > 1:
        values = [join(values[i], values[i + 1]) for i in range(0, len(values), 2)]
    return values[0]


def log_sum(values):
    peak = tree(values, jnp.maximum)
    return peak + jnp.log2(tree([jnp.exp2(value - peak) for value in values], jnp.add))


def product(rows, cols):
    return lax.dot_general(rows, cols, (((1,), (1,)), ((), ())), preferred_element_type=F32)


def ready(sources, targets, mass, source_mass):
    part, chunk = targets.shape[0], mass.shape[0]
    anywhere = pl.BlockSpec(memory_space=pl.ANY)

    def kernel(sources_ref, targets_ref, mass_ref, source_ref, sources_out, packed_ref, mass_out, source_out, *sems):
        copies = [
            pltpu.make_async_copy(mass_ref, mass_out, sems[0]),
            pltpu.make_async_copy(targets_ref, packed_ref.at[:part], sems[1]),
            pltpu.make_async_copy(sources_ref, sources_out, sems[2]),
        ]
        for copy in copies:
            copy.start()
        source_out[...] = jnp.log2(source_ref[...])
        copies[0].wait()
        value, pieces = mass_out[...], []
        for step in range(PIECES):
            pieces.append(value.astype(jnp.bfloat16).astype(F32))
            value = value - pieces[-1]
        pieces.append(jnp.zeros_like(value))
        packed_ref[part:, :] = jnp.concatenate(pieces, axis=0).astype(jnp.bfloat16)
        copies[1].wait()
        copies[2].wait()

    return pl.pallas_call(
        kernel,
        out_shape=(
            pltpu.VMEM(sources.shape, jnp.bfloat16),
            pltpu.VMEM((part + (PIECES + 1) * chunk, LANES), jnp.bfloat16),
            pltpu.VMEM(mass.shape, F32),
            pltpu.VMEM(source_mass.shape, F32),
        ),
        in_specs=[anywhere, anywhere, anywhere, VMEM],
        out_specs=(VMEM,) * 4,
        scratch_shapes=[pltpu.SemaphoreType.DMA] * 3,
        compiler_params=params(),
        cost_estimate=pl.CostEstimate(flops=1 << 20, bytes_accessed=1 << 20, transcendentals=0),
        name="ready",
    )(*[pltpu.with_memory_space_constraint(value, pltpu.HBM) for value in (sources, targets, mass)], source_mass)


def lay(place, block, step, count):
    part = block.shape[0]

    def kernel(place_ref, block_ref, out_ref):
        start = pl.multiple_of(jnp.bitwise_xor(place_ref[0], step) * part, part)
        out_ref[pl.ds(start, part), :] = block_ref[...]

    return pl.pallas_call(
        kernel,
        out_shape=pltpu.VMEM((count * part, LANES), jnp.bfloat16),
        in_specs=[SMEM, VMEM],
        out_specs=VMEM,
        compiler_params=params(),
        cost_estimate=pl.CostEstimate(flops=1 << 20, bytes_accessed=1 << 20, transcendentals=0),
        name="lay",
    )(place, block)


def pack(place, blocks, laid):
    part = blocks[0].shape[0]

    def kernel(place_ref, *refs):
        out_ref = refs[-1]
        for step in range(len(blocks)):
            start = pl.multiple_of(jnp.bitwise_xor(place_ref[0], step) * part, part)
            out_ref[pl.ds(start, part), :] = refs[step][...]

    return pl.pallas_call(
        kernel,
        out_shape=pltpu.VMEM(laid.shape, jnp.bfloat16),
        in_specs=[SMEM] + [VMEM] * (len(blocks) + 1),
        out_specs=VMEM,
        input_output_aliases={1 + len(blocks): 0},
        compiler_params=params(),
        cost_estimate=pl.CostEstimate(flops=1 << 20, bytes_accessed=1 << 18, transcendentals=0),
        name="pack",
    )(place, *blocks, laid)


def pieces_of(value):
    lane = lax.broadcasted_iota(jnp.int32, (value.shape[0], LANES), 1)
    tile = jnp.zeros((value.shape[0], LANES), F32)
    for step in range(PIECES):
        piece = value.astype(jnp.bfloat16).astype(F32)
        tile = jnp.where(lane == step, piece, tile)
        value = value - piece
    return tile.astype(jnp.bfloat16)


def ones_for(rows):
    lane = lax.broadcasted_iota(jnp.int32, (rows, LANES), 1)
    return jnp.where(lane < PIECES, 1.0, 0.0).astype(jnp.bfloat16)


class Rows:
    def __init__(self, count):
        self.peak = jnp.full((8, count), -1e30, F32)
        self.total = jnp.zeros((8, count), F32)

    def add(self, scores_ref):
        tops = self.peak
        for row in range(0, ROWS, 8):
            tops = jnp.maximum(tops, scores_ref[row : row + 8, :])
        self.total = self.total * jnp.exp2((self.peak - tops) * SCALE)
        self.peak = tops
        for row in range(0, ROWS, 8):
            self.total = self.total + jnp.exp2((scores_ref[row : row + 8, :] - tops) * SCALE)

    def lse(self):
        widest = jnp.max(self.peak, axis=0, keepdims=True)
        total = jnp.sum(self.total * jnp.exp2((self.peak - widest) * SCALE), axis=0, keepdims=True)
        return widest * SCALE + jnp.log2(total)


def first_rows(place, mass, packed, blocks, sources):
    count, chunk = sources.shape[0], mass.shape[0]
    n_src = len(blocks) // CORES + 1
    part = blocks[0].shape[0]
    width = CORES * n_src * part

    def kernel(place_ref, mass_ref, sources_ref, *refs):
        own_ref, other_ref, block_refs = refs[0], refs[1], refs[2 : 2 + len(blocks)]
        targets_ref, offset_ref, full_ref, out_ref, *score_refs = refs[2 + len(blocks) :]
        src, core = place_ref[0], place_ref[1]
        full_ref[pl.ds(pl.multiple_of(core * chunk, chunk), chunk), :] = jnp.log2(mass_ref[...])
        parts = [other_ref[part + i * chunk : part + (i + 1) * chunk, :].astype(F32) for i in range(PIECES)]
        start = pl.multiple_of(jnp.bitwise_xor(core, 1) * chunk, chunk)
        full_ref[pl.ds(start, chunk), :] = jnp.log2(parts[0] + (parts[1] + parts[2]))
        for dc in range(CORES):
            for ds in range(n_src):
                index = jnp.bitwise_xor(core, dc) * n_src + jnp.bitwise_xor(src, ds)
                start = pl.multiple_of(index * part, part)
                ref = refs[dc] if ds == 0 else block_refs[dc * (n_src - 1) + ds - 1]
                targets_ref[pl.ds(start, part), :] = ref[:part, :]
        mask = diagonal()
        log_mass = full_ref[...] * (1.0 / SCALE)
        cols = jnp.concatenate([sources_ref[...], ones_for(count)], axis=1)
        rows = Rows(count)
        for at in range(0, width, ROWS):
            scores_ref = score_refs[at // ROWS % len(score_refs)]
            for row in range(at, at + ROWS, LANES):
                values = targets_ref[row : row + LANES, :].astype(F32)
                half = 0.5 * jnp.sum(values * values, axis=1, keepdims=True)
                block = row // LANES
                offset_ref[row : row + LANES, :] = pieces_of(to_column(log_mass[block : block + 1, :], mask) - half)
            scores_ref[...] = product(jnp.concatenate([targets_ref[at : at + ROWS, :], offset_ref[at : at + ROWS, :]], axis=1), cols)
            rows.add(scores_ref)
        fold_into(out_ref, rows.lse())

    return pl.pallas_call(
        kernel,
        out_shape=(
            pltpu.VMEM((width, LANES), jnp.bfloat16),
            pltpu.VMEM((width, LANES), jnp.bfloat16),
            rows_of(width),
            rows_of(count),
        ),
        in_specs=[SMEM] + [VMEM] * (4 + len(blocks)),
        out_specs=(VMEM,) * 4,
        scratch_shapes=[pltpu.VMEM((ROWS, count), F32)] * 2,
        compiler_params=params(),
        cost_estimate=pl.CostEstimate(flops=1 << 29, bytes_accessed=1 << 20, transcendentals=1 << 20),
        name="first_rows",
    )(place, mass, pin(sources), *[pin(value) for value in packed], *[pin(value) for value in blocks])


def other_rows(place, targets, offsets, first, groups):
    mine, groups = groups[0], groups[1:]
    width, count, each = targets.shape[0], sum(group.shape[0] for group in groups), mine.shape[0] // LANES

    def kernel(place_ref, targets_ref, offset_ref, first_ref, mine_ref, *refs):
        group_refs, (out_ref, sources_ref, *score_refs) = refs[: len(groups)], refs[len(groups) :]
        cols = jnp.concatenate([ref[...] for ref in group_refs], axis=0)
        cols = jnp.concatenate([cols, ones_for(count)], axis=1)
        rows = Rows(count)
        for at in range(0, width, ROWS):
            scores_ref = score_refs[at // ROWS % len(score_refs)]
            scores_ref[...] = product(jnp.concatenate([targets_ref[at : at + ROWS, :], offset_ref[at : at + ROWS, :]], axis=1), cols)
            rows.add(scores_ref)
        lse = rows.lse()
        for step in range(len(groups) + 1):
            start = jnp.bitwise_xor(place_ref[2], step) * each
            ref = group_refs[step - 1] if step else mine_ref
            sources_ref[pl.ds(pl.multiple_of(start * LANES, each * LANES), each * LANES), :] = ref[...]
            for row in range(each):
                at = ((step - 1) * each + row) * LANES
                out_ref[pl.ds(start + row, 1), :] = first_ref[row : row + 1, :] if step == 0 else lse[:, at : at + LANES]

    return pl.pallas_call(
        kernel,
        out_shape=(rows_of(count + each * LANES), pltpu.VMEM((count + each * LANES, LANES), jnp.bfloat16)),
        in_specs=[SMEM] + [VMEM] * (3 + len(groups) + 1),
        out_specs=(VMEM,) * 2,
        scratch_shapes=[pltpu.VMEM((ROWS, count), F32)] * 2,
        compiler_params=params(),
        name="other_rows",
    )(place, pin(targets), pin(offsets), first, pin(mine), *groups)


def first_columns(sources, targets, parts, log_mass):
    count, width = sources.shape[0], targets.shape[0]

    def kernel(sources_ref, targets_ref, parts_ref, log_ref, plan_ref, reach_ref, top_ref, out_ref, lse_ref, *score_refs):
        lse = log_sum([parts_ref[i] for i in range(parts.shape[0])])
        lse_ref[...] = lse
        mask = diagonal()
        shift = (log_ref[...] - lse) * (1.0 / SCALE)
        shift = [pieces_of(to_column(shift[i : i + 1, :], mask)) for i in range(count // LANES)]
        cols = jnp.concatenate([sources_ref[...], jnp.concatenate(shift, axis=0)], axis=1)
        ones = ones_for(ROWS)
        for at in range(0, width, ROWS):
            scores_ref = score_refs[at // ROWS % len(score_refs)]
            scores_ref[...] = product(jnp.concatenate([targets_ref[at : at + ROWS, :], ones], axis=1), cols)
            for block in range(0, ROWS, LANES):
                peaks, totals = [], []
                for row in range(block, block + LANES, 8):
                    scores = scores_ref[row : row + 8, :]
                    pieces = [scores[:, lane : lane + LANES] for lane in range(0, count, LANES)]
                    peak = tree(pieces, jnp.maximum)
                    pieces = [jnp.exp2((piece - peak) * SCALE) for piece in pieces]
                    plan_ref[at + row : at + row + 8, :] = jnp.concatenate(pieces, axis=1)
                    peaks.append(peak * SCALE)
                    totals.append(tree(pieces, jnp.add))
                peak = jnp.concatenate(peaks, axis=0)
                top = jnp.max(peak, axis=1, keepdims=True)
                reach = jnp.exp2(peak - top)
                reach_ref[at + block : at + block + LANES, :] = reach
                total = jnp.sum((jnp.concatenate(totals, axis=0) * reach).T, axis=0, keepdims=True)
                index = (at + block) // LANES
                top_ref[index : index + 1, :] = to_row(top, mask)
                out_ref[index : index + 1, :] = top_ref[index : index + 1, :] + jnp.log2(total)

    return pl.pallas_call(
        kernel,
        out_shape=(
            pltpu.VMEM((width, count), F32),
            pltpu.VMEM((width, LANES), F32),
            rows_of(width),
            rows_of(width),
            rows_of(count),
        ),
        in_specs=[VMEM] * 4,
        out_specs=(VMEM,) * 5,
        scratch_shapes=[pltpu.VMEM((ROWS, count), F32)] * 2,
        compiler_params=params(),
        name="first_columns",
    )(pin(sources), pin(targets), parts, log_mass)


def later_rows(plan, reach, top, log_mass, parts):
    width, count = plan.shape
    rows = width // LANES

    def kernel(plan_ref, reach_ref, top_ref, log_ref, *refs):
        part_refs, out_ref = refs[:-1], refs[-1]
        weight = jnp.exp2(log_ref[...] + (top_ref[...] - log_sum([ref[...] for ref in part_refs])))
        mask = diagonal()
        total = jnp.zeros((8, count), F32)
        for block in range(rows):
            at = block * LANES
            factors = reach_ref[at : at + LANES, :] * to_column(weight[block : block + 1, :], mask)
            for row in range(0, LANES, 8):
                factor = jnp.concatenate([factors[row : row + 8, :]] * (count // LANES), axis=1)
                total = total + plan_ref[at + row : at + row + 8, :] * factor
        fold_into(out_ref, jnp.sum(total, axis=0, keepdims=True))

    return pl.pallas_call(
        kernel,
        out_shape=rows_of(count),
        in_specs=[VMEM] * (4 + len(parts)),
        out_specs=VMEM,
        compiler_params=params(),
        name="later_rows",
    )(pin(plan), pin(reach), top, log_mass, *parts)


def later_columns(plan, reach, top, parts, log_mass, lse, half, last):
    width, count = plan.shape

    def kernel(plan_ref, reach_ref, top_ref, parts_ref, log_ref, lse_ref, half_ref, out_ref, *potential_refs):
        factor = log_ref[...] - jnp.log2(tree([parts_ref[i] for i in range(parts.shape[0])], jnp.add))
        for ref in potential_refs:
            ref[width // LANES :, :] = half_ref[...] + UNIT * (factor - lse_ref[...])
        factor = unfold(jnp.exp2(factor))
        factors = [factor[:, lane : lane + LANES] for lane in range(0, count, LANES)]
        for at in range(0, width, LANES):
            totals = []
            for row in range(at, at + LANES, 8):
                plan = plan_ref[row : row + 8, :]
                totals.append(tree([plan[:, i * LANES : (i + 1) * LANES] * factors[i] for i in range(count // LANES)], jnp.add))
            total = jnp.concatenate(totals, axis=0) * reach_ref[at : at + LANES, :]
            index = at // LANES
            total = jnp.log2(jnp.sum(total.T, axis=0, keepdims=True))
            for ref in (out_ref, *potential_refs):
                ref[index : index + 1, :] = top_ref[index : index + 1, :] + total

    return pl.pallas_call(
        kernel,
        out_shape=(rows_of(width),) + (rows_of(width + count),) * last,
        in_specs=[VMEM] * 7,
        out_specs=(VMEM,) * (1 + last),
        compiler_params=params(),
        name="later_columns",
    )(pin(plan), pin(reach), top, parts, log_mass, lse, half)


def levels_of(size):
    bits = size.bit_length() - 1
    out = []
    while bits > 0:
        take = 2 if bits % 2 == 0 else 1
        bits -= take
        out.append([step << bits for step in range(1, 1 << take)])
    return out


def swap(value, axes, size, distance):
    return lax.ppermute(value, axes, [(i, i ^ distance) for i in range(size)])


def swap_all(value, axes, size):
    values = [value]
    for distances in levels_of(size):
        got = {d: [swap(value, axes, size, d) for value in values] for d in reversed(distances)}
        values = [part for i in range(len(values)) for part in [values[i]] + [got[d][i] for d in distances]]
    return values


def share(value, size):
    copies = jnp.broadcast_to(value[None], (size,) + value.shape)
    return lax.all_to_all(copies, ("z", "x"), 0, 0, tiled=True)


def swap_far(value, pair, axes, size):
    levels = levels_of(size)
    if len(levels) == 1:
        return pair + [swap(value, axes, size, d) for d in levels[0][1:]]
    values = swap_all(value, axes, size)
    return pair + values[2:]


def half_norm(points):
    values = points.astype(F32)
    return 0.5 * jnp.sum(values * values, axis=1)


def make_local(n_src, n_z, n_x):
    near, n_near = ("src", "core"), n_src * CORES
    n_far = n_z * n_x

    def local(source_points, target_points, source_mass, target_mass):
        core, x = lax.axis_index("core"), lax.axis_index("x")
        place = jnp.stack([lax.axis_index("src"), core, x]).astype(jnp.int32)
        along = lax.axis_index("z").astype(jnp.int32).reshape(1)
        part = source_points.shape[0]
        a = source_mass.reshape(n_z, n_x, CORES, part)
        a = lax.dynamic_index_in_dim(a, core, axis=2, keepdims=False).swapaxes(0, 1).reshape(-1, LANES)
        blocks = swap_all(target_points, "src", n_src)[1:]
        three, two, one = [swap(source_points, "z", n_z, d) for d in (3, 2, 1)]
        mine, packed, b, a = ready(source_points, target_points, target_mass.reshape(-1, LANES), a)
        laid = lay(along, three, 3, n_z)
        packed = swap_all(packed, "core", CORES)
        blocks = blocks + [swap(block, "core", CORES, 1) for block in blocks]
        groups = swap_all(pack(along, [mine, one, two], laid), "x", n_x)
        place, a = lax.optimization_barrier((place, a))
        targets, offsets, b, first = first_rows(place, b, packed, blocks, groups[0])
        own, sources = other_rows(place, targets, offsets, first, groups)
        plan, reach, top, own, row_lse = first_columns(sources, targets, share(own, n_far), a)
        early_x, early_y, own = lax.optimization_barrier((sources, targets, own))
        half_x, half_y = half_norm(early_x).reshape(-1, LANES), half_norm(early_y).reshape(-1, LANES)
        parts = swap_all(own, near, n_near)
        half_x, half_y, *parts = lax.optimization_barrier((half_x, half_y, *parts))
        for step in range(1, ITERS):
            rows = later_rows(plan, reach, top, b, parts)
            own, *joint = later_columns(plan, reach, top, share(rows, n_far), a, row_lse, half_x, step == ITERS - 1)
            if step < ITERS - 1:
                parts = swap_all(own, near, n_near)
        rows = own.shape[0]
        joint = [joint[0], swap(joint[0], near, n_near, 1)]
        mine, other = [value[rows:].reshape(n_x, n_z, part) for value in joint]
        pair = [value[:rows] for value in joint]
        parts = swap_far(own, pair, near, n_near)
        first, second = jnp.where(core == 0, mine, other), jnp.where(core == 0, other, mine)
        source_potential = jnp.stack([first, second], axis=2).swapaxes(0, 1).reshape(-1)
        source_potential, *parts = lax.optimization_barrier((source_potential, *parts))
        target_potential = half_y - UNIT * log_sum(parts)
        target_potential = target_potential.reshape(CORES, -1)
        target_potential = lax.dynamic_index_in_dim(target_potential, core, axis=0, keepdims=False)
        return source_potential, target_potential

    return local


def solution(mesh):
    n_src, n_tgt = mesh.shape["src"], mesh.shape["tgt"]
    n_z = 4
    n_x = n_tgt // (n_z * CORES)
    split = Mesh(mesh.devices.reshape(n_src, n_z, n_x, CORES), ("src", "z", "x", "core"))
    tgt = ("z", "x", "core")
    placed = (P(("src", *tgt), None), P((*tgt, "src"), None), P("src"), P(tgt))
    return jax.shard_map(
        make_local(n_src, n_z, n_x),
        mesh=split,
        in_specs=placed,
        out_specs=(P("src"), P(tgt)),
        check_vma=False,
    )
```

```python
import math

import jax
import jax.numpy as jnp
from jax import lax
from jax.experimental import pallas as pl
from jax.experimental.pallas import tpu as pltpu
from jax.sharding import Mesh, PartitionSpec as P

ITERS = 3
EPS = 0.05
SCALE = 1.0 / (EPS * math.log(2.0))
UNIT = EPS * math.log(2.0)
LANES = 128
CORES = 2
PIECES = 3
ROWS = 256
F32 = jnp.float32
VMEM = pl.BlockSpec(memory_space=pltpu.VMEM)
SMEM = pl.BlockSpec(memory_space=pltpu.SMEM)


def params(limit=24):
    return pltpu.CompilerParams(vmem_limit_bytes=limit * 1024 * 1024)


def pin(value):
    return pltpu.with_memory_space_constraint(value, pltpu.VMEM)


def rows_of(count):
    return jax.ShapeDtypeStruct((count // LANES, LANES), F32)


def diagonal():
    shape = (LANES, LANES)
    return lax.broadcasted_iota(jnp.int32, shape, 0) == lax.broadcasted_iota(jnp.int32, shape, 1)


def to_column(row, mask):
    return jnp.sum(jnp.where(mask, jnp.broadcast_to(row, mask.shape), 0.0), axis=1, keepdims=True)


def to_row(column, mask):
    return jnp.sum(jnp.where(mask, jnp.broadcast_to(column, mask.shape), 0.0), axis=0, keepdims=True)


def unfold(value):
    return jnp.concatenate([value[i : i + 1, :] for i in range(value.shape[0])], axis=1)


def fold_into(ref, value):
    for row in range(ref.shape[0]):
        ref[row : row + 1, :] = value[:, row * LANES : (row + 1) * LANES]


def tree(values, join):
    while len(values) > 1:
        values = [join(values[i], values[i + 1]) for i in range(0, len(values), 2)]
    return values[0]


def log_sum(values):
    peak = tree(values, jnp.maximum)
    return peak + jnp.log2(tree([jnp.exp2(value - peak) for value in values], jnp.add))


def product(rows, cols):
    return lax.dot_general(rows, cols, (((1,), (1,)), ((), ())), preferred_element_type=F32)


def ready(sources, targets, mass, source_mass):
    part, chunk = targets.shape[0], mass.shape[0]
    anywhere = pl.BlockSpec(memory_space=pl.ANY)

    def kernel(sources_ref, targets_ref, mass_ref, source_ref, sources_out, packed_ref, mass_out, source_out, *sems):
        copies = [
            pltpu.make_async_copy(mass_ref, mass_out, sems[0]),
            pltpu.make_async_copy(targets_ref, packed_ref.at[:part], sems[1]),
            pltpu.make_async_copy(sources_ref, sources_out, sems[2]),
        ]
        for copy in copies:
            copy.start()
        source_out[...] = jnp.log2(source_ref[...])
        copies[0].wait()
        value, pieces = mass_out[...], []
        for step in range(PIECES):
            pieces.append(value.astype(jnp.bfloat16).astype(F32))
            value = value - pieces[-1]
        pieces.append(jnp.zeros_like(value))
        packed_ref[part:, :] = jnp.concatenate(pieces, axis=0).astype(jnp.bfloat16)
        copies[1].wait()
        copies[2].wait()

    return pl.pallas_call(
        kernel,
        out_shape=(
            pltpu.VMEM(sources.shape, jnp.bfloat16),
            pltpu.VMEM((part + (PIECES + 1) * chunk, LANES), jnp.bfloat16),
            pltpu.VMEM(mass.shape, F32),
            pltpu.VMEM(source_mass.shape, F32),
        ),
        in_specs=[anywhere, anywhere, anywhere, VMEM],
        out_specs=(VMEM,) * 4,
        scratch_shapes=[pltpu.SemaphoreType.DMA] * 3,
        compiler_params=params(),
        cost_estimate=pl.CostEstimate(flops=1 << 20, bytes_accessed=1 << 20, transcendentals=0),
        name="ready",
    )(*[pltpu.with_memory_space_constraint(value, pltpu.HBM) for value in (sources, targets, mass)], source_mass)


def lay(place, block, step, count):
    part = block.shape[0]

    def kernel(place_ref, block_ref, out_ref):
        start = pl.multiple_of(jnp.bitwise_xor(place_ref[0], step) * part, part)
        out_ref[pl.ds(start, part), :] = block_ref[...]

    return pl.pallas_call(
        kernel,
        out_shape=pltpu.VMEM((count * part, LANES), jnp.bfloat16),
        in_specs=[SMEM, VMEM],
        out_specs=VMEM,
        compiler_params=params(),
        cost_estimate=pl.CostEstimate(flops=1 << 30, bytes_accessed=1 << 18, transcendentals=0),
        name="lay",
    )(place, block)


def pack(place, blocks, laid):
    part = blocks[0].shape[0]

    def kernel(place_ref, *refs):
        out_ref = refs[-1]
        for step in range(len(blocks)):
            start = pl.multiple_of(jnp.bitwise_xor(place_ref[0], step) * part, part)
            out_ref[pl.ds(start, part), :] = refs[step][...]

    return pl.pallas_call(
        kernel,
        out_shape=pltpu.VMEM(laid.shape, jnp.bfloat16),
        in_specs=[SMEM] + [VMEM] * (len(blocks) + 1),
        out_specs=VMEM,
        input_output_aliases={1 + len(blocks): 0},
        compiler_params=params(),
        cost_estimate=pl.CostEstimate(flops=1 << 20, bytes_accessed=1 << 18, transcendentals=0),
        name="pack",
    )(place, *blocks, laid)


def pieces_of(value):
    lane = lax.broadcasted_iota(jnp.int32, (value.shape[0], LANES), 1)
    tile = jnp.zeros((value.shape[0], LANES), F32)
    for step in range(PIECES):
        piece = value.astype(jnp.bfloat16).astype(F32)
        tile = jnp.where(lane == step, piece, tile)
        value = value - piece
    return tile.astype(jnp.bfloat16)


def ones_for(rows):
    lane = lax.broadcasted_iota(jnp.int32, (rows, LANES), 1)
    return jnp.where(lane < PIECES, 1.0, 0.0).astype(jnp.bfloat16)


class Rows:
    def __init__(self, count):
        self.peak = jnp.full((8, count), -1e30, F32)
        self.total = jnp.zeros((8, count), F32)

    def add(self, scores_ref):
        tops = self.peak
        for row in range(0, ROWS, 8):
            tops = jnp.maximum(tops, scores_ref[row : row + 8, :])
        self.total = self.total * jnp.exp2((self.peak - tops) * SCALE)
        self.peak = tops
        for row in range(0, ROWS, 8):
            self.total = self.total + jnp.exp2((scores_ref[row : row + 8, :] - tops) * SCALE)

    def lse(self):
        widest = jnp.max(self.peak, axis=0, keepdims=True)
        total = jnp.sum(self.total * jnp.exp2((self.peak - widest) * SCALE), axis=0, keepdims=True)
        return widest * SCALE + jnp.log2(total)


def first_rows(place, mass, packed, blocks, sources):
    count, chunk = sources.shape[0], mass.shape[0]
    n_src = len(blocks) // CORES + 1
    part = blocks[0].shape[0]
    width = CORES * n_src * part

    def kernel(place_ref, mass_ref, sources_ref, *refs):
        own_ref, other_ref, block_refs = refs[0], refs[1], refs[2 : 2 + len(blocks)]
        targets_ref, offset_ref, full_ref, out_ref, *score_refs = refs[2 + len(blocks) :]
        src, core = place_ref[0], place_ref[1]
        full_ref[pl.ds(pl.multiple_of(core * chunk, chunk), chunk), :] = jnp.log2(mass_ref[...])
        parts = [other_ref[part + i * chunk : part + (i + 1) * chunk, :].astype(F32) for i in range(PIECES)]
        start = pl.multiple_of(jnp.bitwise_xor(core, 1) * chunk, chunk)
        full_ref[pl.ds(start, chunk), :] = jnp.log2(parts[0] + (parts[1] + parts[2]))
        for dc in range(CORES):
            for ds in range(n_src):
                index = jnp.bitwise_xor(core, dc) * n_src + jnp.bitwise_xor(src, ds)
                start = pl.multiple_of(index * part, part)
                ref = refs[dc] if ds == 0 else block_refs[dc * (n_src - 1) + ds - 1]
                targets_ref[pl.ds(start, part), :] = ref[:part, :]
        mask = diagonal()
        log_mass = full_ref[...] * (1.0 / SCALE)
        cols = jnp.concatenate([sources_ref[...], ones_for(count)], axis=1)
        rows = Rows(count)
        for at in range(0, width, ROWS):
            scores_ref = score_refs[at // ROWS % len(score_refs)]
            for row in range(at, at + ROWS, LANES):
                values = targets_ref[row : row + LANES, :].astype(F32)
                half = 0.5 * jnp.sum(values * values, axis=1, keepdims=True)
                block = row // LANES
                offset_ref[row : row + LANES, :] = pieces_of(to_column(log_mass[block : block + 1, :], mask) - half)
            scores_ref[...] = product(jnp.concatenate([targets_ref[at : at + ROWS, :], offset_ref[at : at + ROWS, :]], axis=1), cols)
            rows.add(scores_ref)
        fold_into(out_ref, rows.lse())

    return pl.pallas_call(
        kernel,
        out_shape=(
            pltpu.VMEM((width, LANES), jnp.bfloat16),
            pltpu.VMEM((width, LANES), jnp.bfloat16),
            rows_of(width),
            rows_of(count),
        ),
        in_specs=[SMEM] + [VMEM] * (4 + len(blocks)),
        out_specs=(VMEM,) * 4,
        scratch_shapes=[pltpu.VMEM((ROWS, count), F32)] * 2,
        compiler_params=params(),
        cost_estimate=pl.CostEstimate(flops=1 << 29, bytes_accessed=1 << 20, transcendentals=1 << 20),
        name="first_rows",
    )(place, mass, pin(sources), *[pin(value) for value in packed], *[pin(value) for value in blocks])


def other_rows(place, targets, offsets, first, groups):
    mine, groups = groups[0], groups[1:]
    width, count, each = targets.shape[0], sum(group.shape[0] for group in groups), mine.shape[0] // LANES

    def kernel(place_ref, targets_ref, offset_ref, first_ref, mine_ref, *refs):
        group_refs, (out_ref, sources_ref, *score_refs) = refs[: len(groups)], refs[len(groups) :]
        cols = jnp.concatenate([ref[...] for ref in group_refs], axis=0)
        cols = jnp.concatenate([cols, ones_for(count)], axis=1)
        rows = Rows(count)
        for at in range(0, width, ROWS):
            scores_ref = score_refs[at // ROWS % len(score_refs)]
            scores_ref[...] = product(jnp.concatenate([targets_ref[at : at + ROWS, :], offset_ref[at : at + ROWS, :]], axis=1), cols)
            rows.add(scores_ref)
        lse = rows.lse()
        for step in range(len(groups) + 1):
            start = jnp.bitwise_xor(place_ref[2], step) * each
            ref = group_refs[step - 1] if step else mine_ref
            sources_ref[pl.ds(pl.multiple_of(start * LANES, each * LANES), each * LANES), :] = ref[...]
            for row in range(each):
                at = ((step - 1) * each + row) * LANES
                out_ref[pl.ds(start + row, 1), :] = first_ref[row : row + 1, :] if step == 0 else lse[:, at : at + LANES]

    return pl.pallas_call(
        kernel,
        out_shape=(rows_of(count + each * LANES), pltpu.VMEM((count + each * LANES, LANES), jnp.bfloat16)),
        in_specs=[SMEM] + [VMEM] * (3 + len(groups) + 1),
        out_specs=(VMEM,) * 2,
        scratch_shapes=[pltpu.VMEM((ROWS, count), F32)] * 2,
        compiler_params=params(),
        name="other_rows",
    )(place, pin(targets), pin(offsets), first, pin(mine), *groups)


def first_columns(sources, targets, parts, log_mass):
    count, width = sources.shape[0], targets.shape[0]

    def kernel(sources_ref, targets_ref, parts_ref, log_ref, plan_ref, reach_ref, top_ref, out_ref, lse_ref, *score_refs):
        lse = log_sum([parts_ref[i] for i in range(parts.shape[0])])
        lse_ref[...] = lse
        mask = diagonal()
        shift = (log_ref[...] - lse) * (1.0 / SCALE)
        shift = [pieces_of(to_column(shift[i : i + 1, :], mask)) for i in range(count // LANES)]
        cols = jnp.concatenate([sources_ref[...], jnp.concatenate(shift, axis=0)], axis=1)
        ones = ones_for(ROWS)
        for at in range(0, width, ROWS):
            scores_ref = score_refs[at // ROWS % len(score_refs)]
            scores_ref[...] = product(jnp.concatenate([targets_ref[at : at + ROWS, :], ones], axis=1), cols)
            for block in range(0, ROWS, LANES):
                peaks, totals = [], []
                for row in range(block, block + LANES, 8):
                    scores = scores_ref[row : row + 8, :]
                    pieces = [scores[:, lane : lane + LANES] for lane in range(0, count, LANES)]
                    peak = tree(pieces, jnp.maximum)
                    pieces = [jnp.exp2((piece - peak) * SCALE) for piece in pieces]
                    plan_ref[at + row : at + row + 8, :] = jnp.concatenate(pieces, axis=1)
                    peaks.append(peak * SCALE)
                    totals.append(tree(pieces, jnp.add))
                peak = jnp.concatenate(peaks, axis=0)
                top = jnp.max(peak, axis=1, keepdims=True)
                reach = jnp.exp2(peak - top)
                reach_ref[at + block : at + block + LANES, :] = reach
                total = jnp.sum((jnp.concatenate(totals, axis=0) * reach).T, axis=0, keepdims=True)
                index = (at + block) // LANES
                top_ref[index : index + 1, :] = to_row(top, mask)
                out_ref[index : index + 1, :] = top_ref[index : index + 1, :] + jnp.log2(total)

    return pl.pallas_call(
        kernel,
        out_shape=(
            pltpu.VMEM((width, count), F32),
            pltpu.VMEM((width, LANES), F32),
            rows_of(width),
            rows_of(width),
            rows_of(count),
        ),
        in_specs=[VMEM] * 4,
        out_specs=(VMEM,) * 5,
        scratch_shapes=[pltpu.VMEM((ROWS, count), F32)] * 2,
        compiler_params=params(),
        name="first_columns",
    )(pin(sources), pin(targets), parts, log_mass)


def later_rows(plan, reach, top, log_mass, parts):
    width, count = plan.shape
    rows = width // LANES

    def kernel(plan_ref, reach_ref, top_ref, log_ref, *refs):
        part_refs, out_ref = refs[:-1], refs[-1]
        weight = jnp.exp2(log_ref[...] + (top_ref[...] - log_sum([ref[...] for ref in part_refs])))
        mask = diagonal()
        total = jnp.zeros((8, count), F32)
        for block in range(rows):
            at = block * LANES
            factors = reach_ref[at : at + LANES, :] * to_column(weight[block : block + 1, :], mask)
            for row in range(0, LANES, 8):
                factor = jnp.concatenate([factors[row : row + 8, :]] * (count // LANES), axis=1)
                total = total + plan_ref[at + row : at + row + 8, :] * factor
        fold_into(out_ref, jnp.sum(total, axis=0, keepdims=True))

    return pl.pallas_call(
        kernel,
        out_shape=rows_of(count),
        in_specs=[VMEM] * (4 + len(parts)),
        out_specs=VMEM,
        compiler_params=params(),
        name="later_rows",
    )(pin(plan), pin(reach), top, log_mass, *parts)


def later_columns(plan, reach, top, parts, log_mass, lse, half, last):
    width, count = plan.shape

    def kernel(plan_ref, reach_ref, top_ref, parts_ref, log_ref, lse_ref, half_ref, out_ref, *potential_refs):
        factor = log_ref[...] - jnp.log2(tree([parts_ref[i] for i in range(parts.shape[0])], jnp.add))
        for ref in potential_refs:
            ref[...] = half_ref[...] + UNIT * (factor - lse_ref[...])
        factor = unfold(jnp.exp2(factor))
        factors = [factor[:, lane : lane + LANES] for lane in range(0, count, LANES)]
        for at in range(0, width, LANES):
            totals = []
            for row in range(at, at + LANES, 8):
                plan = plan_ref[row : row + 8, :]
                totals.append(tree([plan[:, i * LANES : (i + 1) * LANES] * factors[i] for i in range(count // LANES)], jnp.add))
            total = jnp.concatenate(totals, axis=0) * reach_ref[at : at + LANES, :]
            index = at // LANES
            total = jnp.log2(jnp.sum(total.T, axis=0, keepdims=True))
            out_ref[index : index + 1, :] = top_ref[index : index + 1, :] + total

    return pl.pallas_call(
        kernel,
        out_shape=(rows_of(width),) + (rows_of(count),) * last,
        in_specs=[VMEM] * 7,
        out_specs=(VMEM,) * (1 + last),
        compiler_params=params(),
        name="later_columns",
    )(pin(plan), pin(reach), top, parts, log_mass, lse, half)


def levels_of(size):
    bits = size.bit_length() - 1
    out = []
    while bits > 0:
        take = 2 if bits % 2 == 0 else 1
        bits -= take
        out.append([step << bits for step in range(1, 1 << take)])
    return out


def swap(value, axes, size, distance):
    return lax.ppermute(value, axes, [(i, i ^ distance) for i in range(size)])


def swap_all(value, axes, size):
    values = [value]
    for distances in levels_of(size):
        got = {d: [swap(value, axes, size, d) for value in values] for d in reversed(distances)}
        values = [part for i in range(len(values)) for part in [values[i]] + [got[d][i] for d in distances]]
    return values


def share(value, size):
    copies = jnp.broadcast_to(value[None], (size,) + value.shape)
    return lax.all_to_all(copies, ("z", "x"), 0, 0, tiled=True)


def half_norm(points):
    values = points.astype(F32)
    return 0.5 * jnp.sum(values * values, axis=1)


def make_local(n_src, n_z, n_x):
    near, n_near = ("src", "core"), n_src * CORES
    n_far = n_z * n_x

    def local(source_points, target_points, source_mass, target_mass):
        core, x = lax.axis_index("core"), lax.axis_index("x")
        place = jnp.stack([lax.axis_index("src"), core, x]).astype(jnp.int32)
        along = lax.axis_index("z").astype(jnp.int32).reshape(1)
        part = source_points.shape[0]
        a = source_mass.reshape(n_z, n_x, CORES, part)
        a = lax.dynamic_index_in_dim(a, core, axis=2, keepdims=False).swapaxes(0, 1).reshape(-1, LANES)
        direct = swap_all(target_points, near, n_near)
        blocks = direct[CORES::CORES] + direct[CORES + 1 :: CORES]
        three, two, one = [swap(source_points, "z", n_z, d) for d in (3, 2, 1)]
        mine, packed, b, a = ready(source_points, target_points, target_mass.reshape(-1, LANES), a)
        laid = lay(along, three, 3, n_z)
        packed = swap_all(packed, "core", CORES)
        groups = swap_all(pack(along, [mine, one, two], laid), "x", n_x)
        place, a = lax.optimization_barrier((place, a))
        targets, offsets, b, first = first_rows(place, b, packed, blocks, groups[0])
        own, sources = other_rows(place, targets, offsets, first, groups)
        plan, reach, top, own, row_lse = first_columns(sources, targets, share(own, n_far), a)
        early_x, early_y, own = lax.optimization_barrier((sources, targets, own))
        half_x, half_y = half_norm(early_x).reshape(-1, LANES), half_norm(early_y).reshape(-1, LANES)
        parts = swap_all(own, near, n_near)
        half_x, half_y, *parts = lax.optimization_barrier((half_x, half_y, *parts))
        for step in range(1, ITERS):
            rows = later_rows(plan, reach, top, b, parts)
            own, *potential = later_columns(plan, reach, top, share(rows, n_far), a, row_lse, half_x, step == ITERS - 1)
            parts = swap_all(own, near, n_near)
        mine, other = swap_all(potential[0].reshape(n_x, n_z, part), "core", CORES)
        first, second = jnp.where(core == 0, mine, other), jnp.where(core == 0, other, mine)
        source_potential = jnp.stack([first, second], axis=2).swapaxes(0, 1).reshape(-1)
        target_potential = half_y - UNIT * log_sum(parts)
        target_potential = target_potential.reshape(CORES, -1)
        target_potential = lax.dynamic_index_in_dim(target_potential, core, axis=0, keepdims=False)
        return source_potential, target_potential

    return local


def solution(mesh):
    n_src, n_tgt = mesh.shape["src"], mesh.shape["tgt"]
    n_z = 4
    n_x = n_tgt // (n_z * CORES)
    split = Mesh(mesh.devices.reshape(n_src, n_z, n_x, CORES), ("src", "z", "x", "core"))
    tgt = ("z", "x", "core")
    placed = (P(("src", *tgt), None), P((*tgt, "src"), None), P("src"), P(tgt))
    return jax.shard_map(
        make_local(n_src, n_z, n_x),
        mesh=split,
        in_specs=placed,
        out_specs=(P("src"), P(tgt)),
        check_vma=False,
    )
```
